32 devices in a mesh: seq: 4 (over y, x), ctx: 8 (over z, core).
Axes of the slice: x: 2, y: 2, z: 4, core: 2. Of those that a mesh axis runs over, the one named last changes fastest.
Arguments:
- tokens: bfloat16 [8, 2048, 768], P('seq', 'ctx'), may hold values from -6 to 6
- norm_gain: float32 [768], replicated, may hold values from 0.5 to 1.5
- gate_projection_matrix: bfloat16 [768, 1536], replicated, may hold values from -0.21875 to 0.21875
- mixer_projection_matrix: bfloat16 [768, 1792], replicated, may hold values from -0.21875 to 0.21875
- step_projection_matrix: bfloat16 [768, 24], replicated, may hold values from -0.21875 to 0.21875
- conv_weight: float32 [4, 1792], replicated, may hold values from -3 to 3
- conv_bias: float32 [1792], replicated, may hold values from -3 to 3
- step_bias: float32 [24], replicated, may hold values from -2 to 0
- log_rates: float32 [24], replicated, may hold values from -12 to -2, as said below
- skip_gain: float32 [24], replicated, may hold values from 0.5 to 2
- gate_gain: float32 [1536], replicated, may hold values from 0.5 to 1.5
- out_weight: bfloat16 [1536, 768], replicated, may hold values from -0.15625 to 0.15625
- cotangent: bfloat16 [8, 2048, 768], P('seq', 'ctx'), may hold values from -6 to 6
Outputs:
- result: bfloat16 [8, 2048, 768], P('seq', 'ctx')
- token_grad: bfloat16 [8, 2048, 768], P('seq', 'ctx')
- grad_norm_gain: float32 [768], replicated
- grad_gate_weight: float32 [768, 1536], replicated
- grad_mixer_weight: float32 [768, 1792], replicated
- grad_step_weight: float32 [768, 24], replicated
- grad_conv_weight: float32 [4, 1792], replicated
- grad_conv_bias: float32 [1792], replicated
- grad_step_bias: float32 [24], replicated
- grad_log_rates: float32 [24], replicated
- grad_skip_gain: float32 [24], replicated
- grad_gate_gain: float32 [1536], replicated
- grad_out_weight: float32 [1536, 768], replicated
The draws below stay inside these ranges and needn't reach their ends.
Inputs may be any that keep to these rules, and one draw needn't show every extreme that they name: `log_rates`: logarithms of the heads' decay rates.
All inputs are finite; a program needn't handle non-finite values.
Results may differ from the reference program's by a relative error of at most 0.0055.
The reference program's roundings to bfloat16 on the way count: a program that leaves them out, or rounds other values in their place, can miss the bound.
Values may be sent and summed in bfloat16 or wider, within the bound.
A program may use at most 256 MiB of HBM per device.

```python
import jax
import jax.numpy as jnp
from jax import lax

DM = 768
DI = 1536
H = 24
KW = 4
GROUP = 256
SEQS = 8
LEN = 2048
XBC = 1792


def draw_log_rates(key, part):
    key = jax.random.fold_in(key, 7)
    order_key, slow_key, fast_key = jax.random.split(key, 3)
    ranking = jax.random.permutation(order_key, H)
    keep_count = H // 2
    slow_rates = jnp.log(jax.random.uniform(slow_key, (H,), minval=0.5, maxval=2.0) / (0.4 * LEN))
    fast_rates = jnp.log(jax.random.uniform(fast_key, (H,), minval=0.04, maxval=0.1))
    return jnp.where(ranking < keep_count, slow_rates, fast_rates).astype(jnp.float32)


def steps_of(stream_key, shape, cuts, least, top_value):
    def one(position, parts):
        steps = jax.random.uniform(jax.random.fold_in(jax.random.fold_in(stream_key, 6), position), (parts,), jnp.float32, least / len(cuts), top_value / len(cuts))
        return jnp.repeat(jnp.exp(steps), shape[position] // parts).reshape((-1,) + (1,) * (len(shape) - position - 1))

    factor_of = one(*cuts[0])
    for cut in cuts[1:]:
        factor_of = factor_of * one(*cut)
    return factor_of


def noise(rng, dims, scale, most, cuts=(), held_as=jnp.bfloat16):
    array = scale * jax.random.normal(rng, dims, jnp.float32)
    if cuts:
        array = array * steps_of(rng, dims, cuts, -0.22, 0.18)
    return jnp.clip(array, -most, most).astype(held_as)


def setup_inputs(seed: int = 0) -> dict:
    arg_keys = jax.random.split(jax.random.key(seed), 14)
    tokens = noise(arg_keys[0], (SEQS, LEN, DM), 1.0, 6.0, ((0, 4), (1, 8)))
    norm_gain = jnp.clip(1.0 + 0.1 * jax.random.normal(arg_keys[1], (DM,), jnp.float32), 0.5, 1.5)
    gate_projection_matrix = noise(arg_keys[2], (DM, DI), DM ** -0.5, 0.21875)
    mixer_projection_matrix = noise(arg_keys[3], (DM, XBC), DM ** -0.5, 0.21875)
    step_projection_matrix = noise(arg_keys[4], (DM, H), DM ** -0.5, 0.21875)
    conv_weight = noise(arg_keys[5], (KW, XBC), KW ** -0.5, 3.0, (), jnp.float32)
    conv_bias = noise(arg_keys[6], (XBC,), 0.5, 3.0, (), jnp.float32)
    step_bias = jnp.clip(jax.random.uniform(arg_keys[7], (H,), jnp.float32, -2.0, 0.0), -2.0, 0.0)
    log_rates = draw_log_rates(jax.random.fold_in(arg_keys[13], 71), 0)
    skip_gain = jnp.clip(jax.random.uniform(arg_keys[9], (H,), jnp.float32, 0.5, 2.0), 0.5, 2.0)
    gate_gain = jnp.clip(1.0 + 0.1 * jax.random.normal(arg_keys[10], (DI,), jnp.float32), 0.5, 1.5)
    out_weight = noise(arg_keys[11], (DI, DM), DI ** -0.5, 0.15625)
    cotangent = noise(arg_keys[12], (SEQS, LEN, DM), 1.0, 6.0, ((0, 4), (1, 8)))
    return {"tokens": tokens, "norm_gain": norm_gain, "gate_projection_matrix": gate_projection_matrix, "mixer_projection_matrix": mixer_projection_matrix, "step_projection_matrix": step_projection_matrix, "conv_weight": conv_weight, "conv_bias": conv_bias, "step_bias": step_bias, "log_rates": log_rates, "skip_gain": skip_gain, "gate_gain": gate_gain, "out_weight": out_weight, "cotangent": cotangent}


EPSILON = 1e-05
HIGHEST = lax.Precision.HIGHEST

@jax.custom_vjp
def low(v):
    return lax.optimization_barrier(v.astype(jnp.bfloat16)).astype(jnp.float32)

@jax.custom_vjp
def low_back(v):
    return v

def low_keep(v):
    return (low(v), None)

def low_pass(kept, grad):
    return (grad,)

def back_keep(v):
    return (v, None)

def back_low(kept, grad):
    return (low(grad),)
low.defvjp(low_keep, low_pass)
low_back.defvjp(back_keep, back_low)

def swish(value):
    return value * jax.nn.sigmoid(value)

def matmul_high(left, right):
    return jnp.dot(left, right, precision=HIGHEST)

def group_step(carry, pieces):
    carried, rates = carry
    signal, driven, inflow, outflow, step_size = pieces
    length, inner_width = signal.shape
    head_count = step_size.shape[1]
    head_size = inner_width // head_count
    cumulative = jnp.cumsum(step_size * rates, axis=0)
    end_total = cumulative[-1]
    tail = jnp.exp(end_total[None, :] - cumulative)
    scaled = low(signal * jnp.repeat(step_size, head_size, axis=1) * jnp.repeat(tail, head_size, axis=1))
    summary = matmul_high(scaled.T, inflow)
    scores = low_back(matmul_high(outflow, inflow.T))
    positions = jnp.arange(length)
    causal = positions[:, None] >= positions[None, :]
    gaps = cumulative.T[:, :, None] - cumulative.T[:, None, :]
    factor = jnp.where(causal, jnp.exp(jnp.where(causal, gaps, 0.0)), 0.0)
    mixing = low(scores[None] * factor)
    inner_part = jnp.einsum('htu,uhp->thp', mixing, driven.reshape(length, head_count, head_size), precision=HIGHEST).reshape(length, inner_width)
    outer_part = matmul_high(outflow, carried.T) * jnp.repeat(jnp.exp(cumulative), head_size, axis=1)
    updated = jnp.repeat(jnp.exp(end_total), head_size)[:, None] * carried + summary
    return ((updated, rates), inner_part + outer_part)

def layer_forward(params, hidden):
    norm_gain, gate_projection_matrix, mixer_projection_matrix, step_projection_matrix, conv_weight, conv_bias, step_bias, log_rates, skip_gain, gate_gain, out_weight = params
    length = hidden.shape[0]
    inner_width = gate_projection_matrix.shape[1]
    head_count = step_projection_matrix.shape[1]
    head_size = inner_width // head_count
    state_width = (mixer_projection_matrix.shape[1] - inner_width) // 2
    window = conv_weight.shape[0] - 1
    inverse = lax.rsqrt(lax.optimization_barrier(jnp.mean(hidden * hidden, axis=-1, keepdims=True)) + EPSILON)
    normalized_input = low(hidden * inverse * norm_gain)
    gate_preactivation = low_back(matmul_high(normalized_input, gate_projection_matrix))
    mixed = low(low_back(matmul_high(normalized_input, mixer_projection_matrix)))
    step_preactivation = low_back(matmul_high(normalized_input, step_projection_matrix))
    padded = jnp.pad(mixed, ((window, 0), (0, 0)))
    filtered = conv_bias
    for offset in range(window + 1):
        filtered = filtered + conv_weight[offset] * padded[offset:offset + length]
    activated = swish(filtered)
    signal = activated[:, :inner_width]
    inflow = low(activated[:, inner_width:inner_width + state_width])
    outflow = low(activated[:, inner_width + state_width:])
    step_size = jax.nn.softplus(step_preactivation + step_bias)
    rates = -jnp.exp(log_rates)
    driven = low(signal * jnp.repeat(step_size, head_size, axis=1))
    blocks = length // GROUP
    pieces = (signal.reshape(blocks, GROUP, inner_width), driven.reshape(blocks, GROUP, inner_width), inflow.reshape(blocks, GROUP, state_width), outflow.reshape(blocks, GROUP, state_width), step_size.reshape(blocks, GROUP, head_count))
    start = (jnp.zeros((inner_width, state_width), jnp.float32), rates)
    unused_carry, mixed_out = lax.scan(jax.checkpoint(group_step), start, pieces)
    output_y = low_back(mixed_out.reshape(length, inner_width) + jnp.repeat(skip_gain, head_size) * signal)
    gated = output_y * swish(gate_preactivation)
    inverse_out = lax.rsqrt(lax.optimization_barrier(jnp.mean(gated * gated, axis=-1, keepdims=True)) + EPSILON)
    normout = low(gated * inverse_out * gate_gain)
    return hidden + matmul_high(normout, out_weight)

def reference(tokens, norm_gain, gate_projection_matrix, mixer_projection_matrix, step_projection_matrix, conv_weight, conv_bias, step_bias, log_rates, skip_gain, gate_gain, out_weight, cotangent):
    params = tuple((item.astype(jnp.float32) for item in (norm_gain, gate_projection_matrix, mixer_projection_matrix, step_projection_matrix, conv_weight, conv_bias, step_bias, log_rates, skip_gain, gate_gain, out_weight)))

    def per_sequence(running, sequence):
        hidden, upstream = sequence
        output, pullback = jax.vjp(layer_forward, params, hidden.astype(jnp.float32))
        param_grads, hidden_grad = pullback(upstream.astype(jnp.float32))
        running = tuple((total + part for total, part in zip(running, param_grads)))
        return (running, (output.astype(jnp.bfloat16), hidden_grad.astype(jnp.bfloat16)))
    zeros = tuple((jnp.zeros_like(item) for item in params))
    grad_totals, (result, token_grad) = lax.scan(per_sequence, zeros, (tokens, cotangent))
    return (result, token_grad) + grad_totals
```

```python
import functools

import jax
import jax.numpy as jnp
from jax import lax
from jax.experimental import pallas as pl
from jax.experimental.pallas import tpu as pltpu
from jax.sharding import PartitionSpec as P

MESH = pl.DeviceIdType.MESH
BF = jnp.bfloat16
F32 = jnp.float32
EPSILON = 1e-05
BW = 256
LN = 128


def dot(a, b):
    return jnp.dot(a, b, preferred_element_type=F32)


def dot_nt(a, b):
    return lax.dot_general(a, b, (((1,), (1,)), ((), ())), preferred_element_type=F32)


def split2(v):
    hi = v.astype(BF)
    return hi, (v - hi.astype(F32)).astype(BF)


def split3(v):
    hi = v.astype(BF)
    rest = v - hi.astype(F32)
    mid = rest.astype(BF)
    return hi, mid, (rest - mid.astype(F32)).astype(BF)


def dot3(a, v):
    hi, mid, lo = split3(v)
    return dot(a, hi) + dot(a, mid) + dot(a, lo)


def pieces3(v):
    lane = lax.broadcasted_iota(jnp.int32, v.shape, 1)
    hi, mid, lo = split3(v)
    z = jnp.zeros_like(v)
    return jnp.where(
        lane < 32,
        hi.astype(F32),
        jnp.where(lane < 64, mid.astype(F32), jnp.where(lane < 96, lo.astype(F32), z)),
    ).astype(BF)


def sigmoid(v):
    return 1.0 / (1.0 + jnp.exp(-v))


def ds(start, size):
    return pl.ds(pl.multiple_of(start, size), size)


def layer_kernel(
    nctx,
    tok_h, ng_r, wg_h, wm_h, ws_r, cw_r, cb_r, sb_r, lr_r, sk_r, gg_r, wo_h, cot_h,
    res_r, tg_r, go_h, gw_h, gm_h, small_r, stepg_r,
    tok, cot, wg, wm, wo, halo, ne, nt, ext, fil, drv, scl, y, z, big, gy, ggz, nrm, nrt,
    acc_a, acc_b, gn, sum_s, out_f, in_f, out_b, in_b, sraw, st, cum, cum_t, pst, ptl, pdc,
    dlast, infl, outf, inf_t, outf_t, sco, sco_t, gsc, xx, tri, ginf, gout, hs_d, hs_g, bdh,
    skw, gstage,
    in_sem, out_sem, st_sem, halo_s, halo_r, fs_s, fs_r, bs_s, bs_r, gh_s, gh_r,
):
    seqs, length, dm = tok.shape
    di = wg.shape[1]
    xbc = wm.shape[1]
    heads = ws_r.shape[1]
    hp = di // heads
    nst = (xbc - di) // 2
    window = cw_r.shape[0] - 1
    nblk = di // BW
    nchunk = di // LN
    hw = 16
    seq = lax.axis_index("seq")
    ctx = lax.axis_index("ctx")
    has_prev = ctx > 0
    has_next = ctx < nctx - 1
    prv = (seq, ctx - 1)
    nxt = (seq, ctx + 1)

    barrier = pltpu.get_barrier_semaphore()

    @pl.when(has_prev)
    def _():
        pl.semaphore_signal(barrier, inc=1, device_id=prv, device_id_type=MESH)

    @pl.when(has_next)
    def _():
        pl.semaphore_signal(barrier, inc=1, device_id=nxt, device_id_type=MESH)

    loads = [
        pltpu.make_async_copy(a, b, in_sem.at[i])
        for i, (a, b) in enumerate(
            ((tok_h, tok), (wm_h, wm), (cot_h, cot), (wo_h, wo), (wg_h, wg))
        )
    ]
    for copy in loads:
        copy.start()

    pl.semaphore_wait(barrier, has_prev.astype(jnp.int32) + has_next.astype(jnp.int32))
    loads[0].wait()

    halo_copy = pltpu.make_async_remote_copy(
        src_ref=tok.at[:, pl.ds(length - hw, hw), :], dst_ref=halo, send_sem=halo_s,
        recv_sem=halo_r, device_id=nxt, device_id_type=MESH,
    )

    @pl.when(has_next)
    def _():
        halo_copy.start()

    @pl.when(jnp.logical_not(has_prev))
    def _():
        halo[...] = jnp.zeros_like(halo)
        in_f[...] = jnp.zeros_like(in_f)

    @pl.when(jnp.logical_not(has_next))
    def _():
        in_b[...] = jnp.zeros_like(in_b)

    lane128 = lax.broadcasted_iota(jnp.int32, (1, LN), 1)
    r_i = lax.broadcasted_iota(jnp.int32, (LN, di), 0)
    c_i = lax.broadcasted_iota(jnp.int32, (LN, di), 1)
    xx[...] = jnp.where((r_i % 32 == c_i // hp) & (r_i < 96), 1.0, 0.0).astype(BF)
    t_r = lax.broadcasted_iota(jnp.int32, (length, length), 0)
    t_c = lax.broadcasted_iota(jnp.int32, (length, length), 1)
    tri[0] = jnp.where(t_r >= t_c, 1.0, 0.0).astype(BF)
    tri[1] = jnp.where(t_r <= t_c, 1.0, 0.0).astype(BF)
    k_i = lax.broadcasted_iota(jnp.int32, (heads, LN), 0)
    l_i = lax.broadcasted_iota(jnp.int32, (heads, LN), 1)
    rep = jnp.where((l_i % 32 == k_i) & (l_i < 96), 1.0, 0.0)

    def replicated(row_ref):
        row = jnp.broadcast_to(row_ref[...].reshape(1, heads), (8, heads))
        hi, mid, lo = split3(row)
        r = rep.astype(BF)
        return (dot(hi, r) + dot(mid, r) + dot(lo, r))[0:1]

    ws3 = dot(ws_r[...], rep.astype(BF)).astype(BF)
    bias3 = replicated(sb_r)
    rates3 = -jnp.exp(replicated(lr_r))
    sk8 = jnp.broadcast_to(replicated(sk_r), (8, LN))
    skw[...] = dot(pieces3(sk8), xx[...])

    gain = ng_r[...].reshape(1, dm)

    def norm_rows(rows):
        v = rows.astype(F32)
        inv = lax.rsqrt(jnp.mean(v * v, axis=-1, keepdims=True) + EPSILON)
        return ((v * inv) * gain).astype(BF)

    for s in range(seqs):

        def norm_body(i, _, s=s):
            ne[s, ds(hw + i * 16, 16), :] = norm_rows(tok[s, ds(i * 16, 16), :])
            return 0

        lax.fori_loop(0, length // 16, norm_body, 0, unroll=2)

    for s in range(seqs):
        raw = dot(ne[s, pl.ds(hw, length), :], ws3)
        sraw[s] = raw
        step = jax.nn.softplus(raw + bias3)
        st[s] = step
        cu = dot3(tri[0], step * rates3)
        cum[s] = cu
        cum_t[s] = cu.T
        last = cu[length - 1 : length]
        pst[s] = pieces3(step)
        ptl[s] = pieces3(jnp.exp(last - cu))
        dec = jnp.exp(cu)
        pdc[s] = pieces3(dec)
        dlast[s] = dot(pieces3(dec[length - 8 :]), xx[...])

    for s in range(seqs):
        for b in range(dm // BW):
            nt[b * BW : (b + 1) * BW, s * length : (s + 1) * length] = ne[
                s, hw : hw + length, b * BW : (b + 1) * BW
            ].T

    @pl.when(has_prev)
    def _():
        halo_copy.wait_recv()

    for s in range(seqs):
        ne[s, 0:hw, :] = norm_rows(halo[s])

    loads[1].wait()

    def filter_block(b, s):
        cols = ds(b * BW, BW)
        m = dot(ne[s], wm[:, cols]).astype(BF)
        ext[s, :, cols] = m
        m = m.astype(F32)
        f = cb_r[cols].reshape(1, BW)
        for k in range(window + 1):
            shift = window - k
            moved = pltpu.roll(m, shift, 0) if shift else m
            f = f + cw_r[k : k + 1, cols] * moved[hw:]
        fil[s, :, cols] = f
        return f

    for s in range(seqs):
        f = filter_block(nblk, s)
        act = f * sigmoid(f)
        i_bf = act[:, :nst].astype(BF)
        o_bf = act[:, nst:].astype(BF)
        infl[s] = i_bf
        outf[s] = o_bf
        inf_t[s] = i_bf.T
        outf_t[s] = o_bf.T
        sco[s] = dot_nt(o_bf, i_bf)
        sco_t[s] = dot_nt(i_bf, o_bf)

    def signal_body(b, _):
        cols = ds(b * BW, BW)
        for s in range(seqs):
            f = filter_block(b, s)
            sig = f * sigmoid(f)
            x = xx[:, cols]
            dr = sig * dot(pst[s], x)
            drv[s, :, cols] = dr.astype(BF)
            sc = (dr * dot(ptl[s], x)).astype(BF)
            scl[s, :, cols] = sc
            y[s, :, cols] = skw[0:1, cols] * sig
            summ = dot(inf_t[s], sc)
            sum_s[2 * b, s] = summ[:, :LN]
            sum_s[2 * b + 1, s] = summ[:, LN:]
        return 0

    lax.fori_loop(0, nblk, signal_body, 0)

    def relay(c, in_buf, out_buf, sems, has_in, has_out, to):
        copy = pltpu.make_async_remote_copy(
            src_ref=out_buf.at[c], dst_ref=in_buf.at[c], send_sem=sems[0].at[c],
            recv_sem=sems[1].at[c], device_id=to, device_id_type=MESH,
        )

        @pl.when(has_in)
        def _():
            copy.wait_recv()

        @pl.when(has_out)
        def _():
            for s in range(seqs):
                row = dlast[s, 7:8, ds(c * LN, LN)]
                out_buf[c, s] = (row * in_buf[c, s].astype(F32) + sum_s[c, s]).astype(out_buf.dtype)
            copy.start()

    def relay_slot(slot, skew, *rest):
        c = slot - skew

        @pl.when((c >= 0) & (c < nchunk))
        def _():
            relay(c, *rest)

    half = length // 2
    d_r = lax.broadcasted_iota(jnp.int32, (half, half), 0)
    d_c = lax.broadcasted_iota(jnp.int32, (half, half), 1)
    NEG = -1e30

    def columns_of(s, j):
        moved = pltpu.roll(cum[s], lax.rem(LN - 2 * j, LN), 1)
        return moved[:, 0:1], moved[:, 1:2]

    def pair_forward(j, s):
        cols = ds(j * LN, LN)
        d = drv[s, :, cols]
        lane_low = lane128 < hp
        top, bottom = [], []
        for hh, col in enumerate(columns_of(s, j)):
            row = cum_t[s, pl.ds(2 * j + hh, 1), :]
            fa = jnp.exp(jnp.where(d_r >= d_c, col[:half] - row[:, :half], NEG))
            fb = jnp.exp(col[half:] - row[:, :half])
            fc = jnp.exp(jnp.where(d_r >= d_c, col[half:] - row[:, half:], NEG))
            top.append((sco[s, :half, :half] * fa).astype(BF))
            bottom.append(
                jnp.concatenate(
                    [
                        (sco[s, half:, :half] * fb).astype(BF),
                        (sco[s, half:, half:] * fc).astype(BF),
                    ],
                    axis=1,
                )
            )
        lo = dot(jnp.concatenate(top, axis=0), d[:half])
        hi = dot(jnp.concatenate(bottom, axis=0), d)
        y[s, :half, cols] += jnp.where(lane_low, lo[:half], lo[half:])
        y[s, half:, cols] += jnp.where(lane_low, hi[:half], hi[half:])

    loads[2].wait()
    loads[3].wait()
    loads[4].wait()

    fskew = (3 * ctx) // 2
    bskew = (3 * (nctx - 1 - ctx)) // 2
    slots = nchunk + (3 * (nctx - 1)) // 2

    f_args = (in_f, out_f, (fs_s, fs_r), has_prev, has_next, nxt)
    b_args = (in_b, out_b, (bs_s, bs_r), has_next, has_prev, prv)

    def forward_body(b, _):
        cols = ds(b * BW, BW)
        relay_slot(2 * b, fskew, *f_args)
        for s in range(seqs):
            big[s, 0:length, cols] = dot_nt(cot[s], wo[cols, :])
            pair_forward(2 * b, s)
        relay_slot(2 * b + 1, fskew, *f_args)
        for s in range(seqs):
            z[s, :, cols] = dot(ne[s, hw : hw + length, :], wg[:, cols])
            pair_forward(2 * b + 1, s)
        return 0

    lax.fori_loop(0, nblk, forward_body, 0)

    def forward_rest(slot, _):
        relay_slot(slot, fskew, *f_args)
        return 0

    lax.fori_loop(nchunk, slots, forward_rest, 0)

    acc_a[...] = jnp.zeros_like(acc_a)
    acc_b[...] = jnp.zeros_like(acc_b)

    def gate_body(b, _):
        cols = ds(b * BW, BW)
        for s in range(seqs):
            pr = jnp.concatenate([in_f[2 * b, s], in_f[2 * b + 1, s]], axis=1)
            phi, plo = split2(pr)
            out = (dot(outf[s], phi) + dot(outf[s], plo)) * dot(pdc[s], xx[:, cols])
            yy = y[s, :, cols] + out
            y[s, :, cols] = yy
            zz = z[s, :, cols]
            gated = yy * (zz * sigmoid(zz))
            q = big[s, 0:length, cols] * gg_r[cols].reshape(1, BW)
            a = gated * gated
            c = q * gated
            acc_a[s] += a[:, :LN] + a[:, LN:]
            acc_b[s] += c[:, :LN] + c[:, LN:]
        return 0

    lax.fori_loop(0, nblk, gate_body, 0)

    inv_out, mean_out = [], []
    for s in range(seqs):
        iv = lax.rsqrt(jnp.sum(acc_a[s], axis=-1, keepdims=True) / di + EPSILON)
        inv_out.append(iv)
        mean_out.append(iv * jnp.sum(acc_b[s], axis=-1, keepdims=True) / di)
    gout[...] = jnp.zeros_like(gout)

    def grad_body(b, _):
        cols = ds(b * BW, BW)
        gg_sum = jnp.zeros((1, BW), F32)
        for s in range(seqs):
            yy = y[s, :, cols]
            zz = z[s, :, cols]
            sg = sigmoid(zz)
            act = zz * sg
            unit = (yy * act) * inv_out[s]
            gain_row = gg_r[cols].reshape(1, BW)
            g = big[s, 0:length, cols]
            no = (unit * gain_row).astype(BF)
            nrm[s, :, cols] = no
            nrt[cols, s * length : (s + 1) * length] = no.T
            gg_sum = gg_sum + jnp.sum(g * unit, axis=0, keepdims=True)
            gr = inv_out[s] * (g * gain_row - unit * mean_out[s])
            gyb = (gr * act).astype(BF)
            gy[s, :, cols] = gyb
            ggz[s, :, cols] = (gr * yy * (sg * (1.0 + zz * (1.0 - sg)))).astype(BF)
            w = gyb.astype(F32) * dot(pdc[s], xx[:, cols])
            whi, wlo = split2(w)
            pr = jnp.concatenate([in_f[2 * b, s], in_f[2 * b + 1, s]], axis=1)
            gp = dot(outf_t[s], whi) + dot(outf_t[s], wlo)
            sum_s[2 * b, s] = gp[:, :LN]
            sum_s[2 * b + 1, s] = gp[:, LN:]
            phi, plo = split2(pr)
            gout[s] += dot_nt(whi, phi) + (dot_nt(wlo, phi) + dot_nt(whi, plo))
        small_r[0:1, cols] = gg_sum
        return 0

    lax.fori_loop(0, nblk, grad_body, 0)

    gsc[...] = jnp.zeros_like(gsc)

    def pair_backward(j, s):
        cols = ds(j * LN, LN)
        d = drv[s, :, cols]
        g = gy[s, :, cols]
        lane_low = lane128 < hp
        zero = jnp.zeros_like(d)
        top, bottom = [], []
        t1 = t2 = t3 = None
        for hh, col in enumerate(columns_of(s, j)):
            row = cum_t[s, pl.ds(2 * j + hh, 1), :]
            dh = jnp.where(lane_low if hh == 0 else jnp.logical_not(lane_low), d, zero)
            m1 = dot_nt(dh[:half], g)
            m2 = dot_nt(dh[half:], g[half:])
            fa = jnp.exp(jnp.where(d_r <= d_c, row[:, :half] - col[:half], NEG))
            fb = jnp.exp(row[:, half:] - col[:half])
            fc = jnp.exp(jnp.where(d_r <= d_c, row[:, half:] - col[half:], NEG))
            top.append(
                jnp.concatenate(
                    [
                        (sco_t[s, :half, :half] * fa).astype(BF),
                        (sco_t[s, :half, half:] * fb).astype(BF),
                    ],
                    axis=1,
                )
            )
            bottom.append((sco_t[s, half:, half:] * fc).astype(BF))
            p1, p2, p3 = m1[:, :half] * fa, m1[:, half:] * fb, m2 * fc
            t1, t2, t3 = (p1, p2, p3) if hh == 0 else (t1 + p1, t2 + p2, t3 + p3)
        gsc[s, :half, :half] += t1
        gsc[s, :half, half:] += t2
        gsc[s, half:, half:] += t3
        lo = dot(jnp.concatenate(top, axis=0), g)
        hi = dot(jnp.concatenate(bottom, axis=0), g[half:])
        z[s, :half, cols] = jnp.where(lane_low, lo[:half], lo[half:])
        z[s, half:, cols] = jnp.where(lane_low, hi[:half], hi[half:])

    def stage_out(slot, value, dst):
        gstage[slot] = value
        copy = pltpu.make_async_copy(gstage.at[slot], dst, st_sem.at[slot])
        copy.start()
        copy.wait()

    def backward_body(b, _):
        cols = ds(b * BW, BW)
        relay_slot(2 * b, bskew, *b_args)
        both = jnp.concatenate([ggz[s, :, cols] for s in range(seqs)], axis=0)
        stage_out(0, dot(nt[...], both), gw_h.at[:, cols])
        rows = jnp.concatenate([cot[s] for s in range(seqs)], axis=0)
        t = dot(nrt[cols, :], rows)
        for i in range(dm // BW):
            gstage[1, i * BW : (i + 1) * BW] = t[:, i * BW : (i + 1) * BW]
        for i in range(dm // BW):
            copy = pltpu.make_async_copy(
                gstage.at[1, pl.ds(i * BW, BW)], go_h.at[cols, pl.ds(i * BW, BW)],
                st_sem.at[1],
            )
            copy.start()
            copy.wait()
        for s in range(seqs):
            pair_backward(2 * b, s)
        relay_slot(2 * b + 1, bskew, *b_args)
        for s in range(seqs):
            pair_backward(2 * b + 1, s)
        return 0

    lax.fori_loop(0, nblk, backward_body, 0)

    for s in range(seqs):
        for i in range(dm // BW):
            cols = slice(i * BW, (i + 1) * BW)
            pj = dot(nrm[s], wo[:, cols])
            res_r[s, :, cols] = (tok[s, :, cols].astype(F32) + pj).astype(BF)
            gn[s, :, cols] = dot_nt(ggz[s], wg[cols, :])

    def backward_rest(slot, _):
        relay_slot(slot, bskew, *b_args)
        return 0

    lax.fori_loop(nchunk, slots, backward_rest, 0)

    ginf[...] = jnp.zeros_like(ginf)
    hs_d[...] = jnp.zeros_like(hs_d)
    hs_g[...] = jnp.zeros_like(hs_g)
    bdh[...] = jnp.zeros_like(bdh)

    def head_sum(v, x):
        hi, lo = split2(v)
        return dot_nt(hi, x) + dot_nt(lo, x)

    def head_sum3(v, x):
        hi, mid, lo = split3(v)
        return dot_nt(hi, x) + dot_nt(mid, x) + dot_nt(lo, x)

    def gh_copy(b):
        cols = ds(b * BW, BW)
        return pltpu.make_async_remote_copy(
            src_ref=big.at[:, pl.ds(0, 8), cols], dst_ref=big.at[:, pl.ds(length, 8), cols],
            send_sem=gh_s.at[b], recv_sem=gh_r.at[b], device_id=prv, device_id_type=MESH,
        )

    @pl.when(jnp.logical_not(has_next))
    def _():
        big[:, length : length + 8, :] = jnp.zeros((seqs, 8, xbc), F32)

    def finish_block(b, s, ga):
        cols = ds(b * BW, BW)
        f = fil[s, :, cols]
        sg = sigmoid(f)
        gf = ga * (sg * (1.0 + f * (1.0 - sg)))
        big[s, 0:length, cols] = gf
        return jnp.sum(gf, axis=0, keepdims=True)

    def last_body(b, _):
        cols = ds(b * BW, BW)
        cb_sum = jnp.zeros((1, BW), F32)
        sk_sum = jnp.zeros((1, BW), F32)
        x = xx[:, cols]
        for s in range(seqs):
            lt = jnp.concatenate([in_b[2 * b, s], in_b[2 * b + 1, s]], axis=1)
            pr = jnp.concatenate([in_f[2 * b, s], in_f[2 * b + 1, s]], axis=1)
            f = fil[s, :, cols]
            sg = sigmoid(f)
            sig = f * sg
            stw = dot(pst[s], x)
            gst = dot(infl[s], lt) * dot(ptl[s], x)
            gd = z[s, :, cols]
            gyf = gy[s, :, cols].astype(F32)
            sk_row = skw[0:1, cols]
            gg = gst + gd
            ga = sk_row * gyf + stw * gg
            t1 = stw * sig * gst
            dd = gyf * (y[s, :, cols] - sk_row * sig) - drv[s, :, cols].astype(F32) * gd - t1
            hs_d[s] += head_sum(dd, x)
            hs_g[s] += head_sum(sig * gg, x)
            bd = jnp.sum(t1, axis=0, keepdims=True) + dlast[s, 7:8, cols] * jnp.sum(
                lt.astype(F32) * pr, axis=0, keepdims=True
            )
            bdh[s] += head_sum3(jnp.broadcast_to(bd, (8, BW)), x)
            sk_sum = sk_sum + jnp.sum(gyf * sig, axis=0, keepdims=True)
            ginf[s] += dot_nt(scl[s, :, cols], lt)
            gf = ga * (sg * (1.0 + f * (1.0 - sg)))
            big[s, 0:length, cols] = gf
            cb_sum = cb_sum + jnp.sum(gf, axis=0, keepdims=True)
        small_r[1:2, cols] = cb_sum
        small_r[2:3, cols] = sk_sum

        @pl.when(has_prev)
        def _():
            gh_copy(b).start()

        return 0

    lax.fori_loop(0, nblk, last_body, 0)

    cb_sum = jnp.zeros((1, BW), F32)
    for s in range(seqs):
        gst_bf = gsc[s].astype(BF)
        gi = ginf[s] + dot(gst_bf, outf[s])
        go = gout[s] + dot(gst_bf.T, infl[s])
        cb_sum = cb_sum + finish_block(nblk, s, jnp.concatenate([gi, go], axis=1))
    small_r[1:2, di:] = cb_sum

    @pl.when(has_prev)
    def _():
        gh_copy(nblk).start()

    row_i = lax.broadcasted_iota(jnp.int32, (length, LN), 0)
    glr = jnp.zeros((1, LN), F32)
    gsb = jnp.zeros((1, LN), F32)
    grl = []
    for s in range(seqs):
        gc = hs_d[s] + jnp.where(row_i == length - 1, bdh[s, 0:1], 0.0)
        terms = dot3(tri[1], gc)
        gst = hs_g[s] + terms * rates3
        glr = glr + jnp.sum(terms * st[s], axis=0, keepdims=True)
        graw = gst * sigmoid(sraw[s] + bias3)
        gsb = gsb + jnp.sum(graw, axis=0, keepdims=True)
        grl.append(jnp.where(lane128 < heads, graw, 0.0).astype(BF))
    small_r[3:4, 0:LN] = gsb
    small_r[4:5, 0:LN] = rates3 * glr
    sk_h = head_sum3(jnp.broadcast_to(small_r[2:3, :di], (8, di)), xx[...])
    small_r[5:6, 0:LN] = sk_h[0:1]
    stepg_r[...] = dot(nt[...], jnp.concatenate(grl, axis=0))

    def mixed_body(b, _):
        cols = ds(b * BW, BW)

        @pl.when(has_next)
        def _():
            gh_copy(b).wait_recv()

        parts = []
        sums = [jnp.zeros((1, BW), F32) for _ in range(window + 1)]
        for s in range(seqs):
            gf = big[s, :, cols]
            rows = gf.shape[0]
            m = ext[s, :, cols].astype(F32)
            gm = jnp.zeros((length, BW), F32)
            for k in range(window + 1):
                shift = window - k
                moved = pltpu.roll(gf, rows - shift, 0) if shift else gf
                gm = gm + cw_r[k : k + 1, cols] * moved[:length]
                em = pltpu.roll(m, shift, 0) if shift else m
                sums[k] = sums[k] + jnp.sum(gf[:length] * em[hw:], axis=0, keepdims=True)
            gmb = gm.astype(BF)
            parts.append(gmb)
            gn[s] += dot_nt(gmb, wm[:, cols])
        for k in range(window + 1):
            small_r[8 + k : 9 + k, cols] = sums[k]
        stage_out(0, dot(nt[...], jnp.concatenate(parts, axis=0)), gm_h.at[:, cols])
        return 0

    lax.fori_loop(0, xbc // BW, mixed_body, 0)
    for s in range(seqs):
        gn[s] += dot_nt(grl[s], ws3)

    def token_body(i, sums):
        for s in range(seqs):
            rows = ds(i * 16, 16)
            v = tok[s, rows, :].astype(F32)
            inv = lax.rsqrt(jnp.mean(v * v, axis=-1, keepdims=True) + EPSILON)
            unit = v * inv
            gr = gn[s, rows, :]
            sums = sums + jnp.sum(gr * unit, axis=0, keepdims=True)
            q = gr * gain
            back = inv * (q - unit * jnp.mean(q * unit, axis=-1, keepdims=True))
            tg_r[s, rows, :] = (cot[s, rows, :].astype(F32) + back).astype(BF)
        return sums

    small_r[6:7, 0:dm] = lax.fori_loop(
        0, length // 16, token_body, jnp.zeros((1, dm), F32)
    )

    @pl.when(has_next)
    def _():
        halo_copy.wait_send()

    def drain(c, _):
        @pl.when(has_next)
        def _():
            pltpu.make_async_remote_copy(
                src_ref=out_f.at[c], dst_ref=in_f.at[c], send_sem=fs_s.at[c],
                recv_sem=fs_r.at[c], device_id=nxt, device_id_type=MESH,
            ).wait_send()

        @pl.when(has_prev)
        def _():
            pltpu.make_async_remote_copy(
                src_ref=out_b.at[c], dst_ref=in_b.at[c], send_sem=bs_s.at[c],
                recv_sem=bs_r.at[c], device_id=prv, device_id_type=MESH,
            ).wait_send()

        return 0

    lax.fori_loop(0, nchunk, drain, 0)

    def drain_halo(b, _):
        @pl.when(has_prev)
        def _():
            gh_copy(b).wait_send()

        return 0

    lax.fori_loop(0, xbc // BW, drain_halo, 0)


def on_device(nctx, *args):
    tokens, norm_gain, wg, wm, ws, conv_w, conv_b, sb, lr, sk, gg, wo, cot = args
    seqs, length, dm = tokens.shape
    di = wg.shape[1]
    xbc = wm.shape[1]
    heads = ws.shape[1]
    nst = (xbc - di) // 2
    nchunk = di // LN
    hw = 16
    vm = pltpu.VMEM
    any_spec = pl.BlockSpec(memory_space=pl.ANY)
    vm_spec = pl.BlockSpec(memory_space=vm)
    dma = pltpu.SemaphoreType.DMA
    out = pl.pallas_call(
        functools.partial(layer_kernel, nctx),
        out_shape=(
            jax.ShapeDtypeStruct(tokens.shape, BF),
            jax.ShapeDtypeStruct(tokens.shape, BF),
            jax.ShapeDtypeStruct((di, dm), F32),
            jax.ShapeDtypeStruct((dm, di), F32),
            jax.ShapeDtypeStruct((dm, xbc), F32),
            jax.ShapeDtypeStruct((16, xbc), F32),
            jax.ShapeDtypeStruct((dm, LN), F32),
        ),
        in_specs=[any_spec, vm_spec, any_spec, any_spec] + [vm_spec] * 7 + [any_spec] * 2,
        out_specs=(vm_spec, vm_spec, any_spec, any_spec, any_spec, vm_spec, vm_spec),
        scratch_shapes=[
            vm((seqs, length, dm), BF),
            vm((seqs, length, dm), BF),
            vm((dm, di), BF),
            vm((dm, xbc), BF),
            vm((di, dm), BF),
            vm((seqs, hw, dm), BF),
            vm((seqs, hw + length, dm), BF),
            vm((dm, seqs * length), BF),
            vm((seqs, hw + length, xbc), BF),
            vm((seqs, length, xbc), F32),
            vm((seqs, length, di), BF),
            vm((seqs, length, di), BF),
            vm((seqs, length, di), F32),
            vm((seqs, length, di), F32),
            vm((seqs, length + 8, xbc), F32),
            vm((seqs, length, di), BF),
            vm((seqs, length, di), BF),
            vm((seqs, length, di), BF),
            vm((di, seqs * length), BF),
            vm((seqs, length, LN), F32),
            vm((seqs, length, LN), F32),
            vm((seqs, length, dm), F32),
            vm((nchunk, seqs, nst, LN), F32),
            vm((nchunk, seqs, nst, LN), F32),
            vm((nchunk, seqs, nst, LN), F32),
            vm((nchunk, seqs, nst, LN), BF),
            vm((nchunk, seqs, nst, LN), BF),
            vm((seqs, length, LN), F32),
            vm((seqs, length, LN), F32),
            vm((seqs, length, LN), F32),
            vm((seqs, LN, length), F32),
            vm((seqs, length, LN), BF),
            vm((seqs, length, LN), BF),
            vm((seqs, length, LN), BF),
            vm((seqs, 8, di), F32),
            vm((seqs, length, nst), BF),
            vm((seqs, length, nst), BF),
            vm((seqs, nst, length), BF),
            vm((seqs, nst, length), BF),
            vm((seqs, length, length), F32),
            vm((seqs, length, length), F32),
            vm((seqs, length, length), F32),
            vm((LN, di), BF),
            vm((2, length, length), BF),
            vm((seqs, length, nst), F32),
            vm((seqs, length, nst), F32),
            vm((seqs, length, LN), F32),
            vm((seqs, length, LN), F32),
            vm((seqs, 8, LN), F32),
            vm((8, di), F32),
            vm((2, dm, BW), F32),
            dma((5,)), dma, dma((2,)), dma, dma,
            dma((nchunk,)), dma((nchunk,)), dma((nchunk,)), dma((nchunk,)),
            dma((xbc // BW,)), dma((xbc // BW,)),
        ],
        compiler_params=pltpu.CompilerParams(
            collective_id=0, has_side_effects=True, vmem_limit_bytes=62 * 1024 * 1024
        ),
    )(*args)
    res, tg, g_out, g_gate, g_mixer, small, stepg = out
    both = ("seq", "ctx")
    g_out, g_gate, g_mixer, small, stepg = lax.psum(
        (g_out, g_gate, g_mixer, small, stepg), both
    )
    return (
        res, tg, small[6, :dm], g_gate, g_mixer, stepg[:, :heads], small[8:12], small[1],
        small[3, :heads], small[4, :heads], small[5, :heads], small[0, :di], g_out,
    )


def solution(mesh):
    tok = P("seq", "ctx", None)
    return jax.shard_map(
        functools.partial(on_device, mesh.shape["ctx"]),
        mesh=mesh,
        in_specs=(tok,) + (P(),) * 11 + (tok,),
        out_specs=(tok, tok) + (P(),) * 11,
        check_vma=False,
    )
```

```python
import functools

import jax
import jax.numpy as jnp
from jax import lax
from jax.experimental import pallas as pl
from jax.experimental.pallas import tpu as pltpu
from jax.sharding import PartitionSpec as P

MESH = pl.DeviceIdType.MESH
BF = jnp.bfloat16
F32 = jnp.float32
EPSILON = 1e-05
BW = 256
LN = 128


def dot(a, b):
    return jnp.dot(a, b, preferred_element_type=F32)


def dot_nt(a, b):
    return lax.dot_general(a, b, (((1,), (1,)), ((), ())), preferred_element_type=F32)


def split2(v):
    hi = v.astype(BF)
    return hi, (v - hi.astype(F32)).astype(BF)


def split3(v):
    hi = v.astype(BF)
    rest = v - hi.astype(F32)
    mid = rest.astype(BF)
    return hi, mid, (rest - mid.astype(F32)).astype(BF)


def dot3(a, v):
    hi, mid, lo = split3(v)
    return dot(a, hi) + dot(a, mid) + dot(a, lo)


def pieces3(v):
    lane = lax.broadcasted_iota(jnp.int32, v.shape, 1)
    hi, mid, lo = split3(v)
    z = jnp.zeros_like(v)
    return jnp.where(
        lane < 32,
        hi.astype(F32),
        jnp.where(lane < 64, mid.astype(F32), jnp.where(lane < 96, lo.astype(F32), z)),
    ).astype(BF)


def sigmoid(v):
    return 1.0 / (1.0 + jnp.exp(-v))


def ds(start, size):
    return pl.ds(pl.multiple_of(start, size), size)


def layer_kernel(
    nctx,
    tok_h, ng_r, wg_h, wm_h, ws_r, cw_r, cb_r, sb_r, lr_r, sk_r, gg_r, wo_h, cot_h,
    res_h, tg_h, go_h, gw_h, gm_h, sm_h,
    tok, cot, wg, wm, wo, halo, ne, nt, ext, fil, drv, scl, y, z, big, gy, ggz, nrm, nrt,
    acc_a, acc_b, gn, sum_s, in_f, out_b, in_b, sraw, st, cum, cum_t, pst, ptl, pdc,
    dlast, infl, outf, inf_t, outf_t, sco, sco_t, xx, tri, hs_d, hs_g, bdh,
    res_r, tok_sem, skw, sm, sk_row_r, bufs, ar_s, ar_r, loc_sem, ex_s, ex_r,
    in_sem, halo_s, halo_r, fs_s, fs_r, bs_s, bs_r, gh_s, gh_r,
):
    seqs, length, dm = tok.shape
    di = wg.shape[1]
    xbc = wm.shape[1]
    heads = ws_r.shape[1]
    hp = di // heads
    nst = (xbc - di) // 2
    window = cw_r.shape[0] - 1
    nblk = di // BW
    gsc, gout, ginf = sco, acc_a, acc_b
    nchunk = di // LN
    hw = 16
    seq = lax.axis_index("seq")
    ctx = lax.axis_index("ctx")
    has_prev = ctx > 0
    has_next = ctx < nctx - 1
    prv = (seq, ctx - 1)
    nxt = (seq, ctx + 1)

    barrier = pltpu.get_barrier_semaphore()

    @pl.when(has_prev)
    def _():
        pl.semaphore_signal(barrier, inc=1, device_id=prv, device_id_type=MESH)

    @pl.when(has_next)
    def _():
        pl.semaphore_signal(barrier, inc=1, device_id=nxt, device_id_type=MESH)

    loads = [
        pltpu.make_async_copy(a, b, in_sem.at[i])
        for i, (a, b) in enumerate(
            ((tok_h, tok), (wm_h, wm), (cot_h, cot), (wo_h, wo), (wg_h, wg))
        )
    ]
    for copy in loads:
        copy.start()

    core = lax.rem(ctx, 2)

    def flipped(index, mask):
        bit = lax.rem(index // mask, 2)
        return bit, index + mask - 2 * mask * bit

    core_peer = (seq, flipped(ctx, 1)[1])
    stages = []
    for mask in (1 + core, 2 - core):
        bit, other = flipped(seq, mask)
        stages.append((bit, (other, ctx)))
    mask = 2
    while mask < nctx:
        bit, other = flipped(ctx, mask)
        stages.append((bit, (seq, other)))
        mask *= 2
    for _, peer in stages:
        pl.semaphore_signal(barrier, inc=1, device_id=peer, device_id_type=MESH)
    pl.semaphore_wait(
        barrier, has_prev.astype(jnp.int32) + has_next.astype(jnp.int32) + len(stages)
    )
    stages, extras = stages[:4], stages[4:]
    loads[0].wait()

    halo_copy = pltpu.make_async_remote_copy(
        src_ref=tok.at[:, pl.ds(length - hw, hw), :], dst_ref=halo, send_sem=halo_s,
        recv_sem=halo_r, device_id=nxt, device_id_type=MESH,
    )

    @pl.when(has_next)
    def _():
        halo_copy.start()

    @pl.when(jnp.logical_not(has_prev))
    def _():
        halo[...] = jnp.zeros_like(halo)
        in_f[...] = jnp.zeros_like(in_f)

    @pl.when(jnp.logical_not(has_next))
    def _():
        in_b[...] = jnp.zeros_like(in_b)

    lane128 = lax.broadcasted_iota(jnp.int32, (1, LN), 1)
    r_i = lax.broadcasted_iota(jnp.int32, (LN, di), 0)
    c_i = lax.broadcasted_iota(jnp.int32, (LN, di), 1)
    xx[...] = jnp.where((r_i % 32 == c_i // hp) & (r_i < 96), 1.0, 0.0).astype(BF)
    t_r = lax.broadcasted_iota(jnp.int32, (length, length), 0)
    t_c = lax.broadcasted_iota(jnp.int32, (length, length), 1)
    tri[0] = jnp.where(t_r >= t_c, 1.0, 0.0).astype(BF)
    tri[1] = jnp.where(t_r <= t_c, 1.0, 0.0).astype(BF)
    k_i = lax.broadcasted_iota(jnp.int32, (heads, LN), 0)
    l_i = lax.broadcasted_iota(jnp.int32, (heads, LN), 1)
    rep = jnp.where((l_i % 32 == k_i) & (l_i < 96), 1.0, 0.0)

    def replicated(row_ref):
        row = jnp.broadcast_to(row_ref[...].reshape(1, heads), (8, heads))
        hi, mid, lo = split3(row)
        r = rep.astype(BF)
        return (dot(hi, r) + dot(mid, r) + dot(lo, r))[0:1]

    ws3 = dot(ws_r[...], rep.astype(BF)).astype(BF)
    bias3 = replicated(sb_r)
    rates3 = -jnp.exp(replicated(lr_r))
    sk8 = jnp.broadcast_to(replicated(sk_r), (8, LN))
    skw[...] = dot(pieces3(sk8), xx[...])

    gain = ng_r[...].reshape(1, dm)

    def norm_rows(rows):
        v = rows.astype(F32)
        inv = lax.rsqrt(jnp.mean(v * v, axis=-1, keepdims=True) + EPSILON)
        return ((v * inv) * gain).astype(BF)

    for s in range(seqs):

        def norm_body(i, _, s=s):
            ne[s, ds(hw + i * 16, 16), :] = norm_rows(tok[s, ds(i * 16, 16), :])
            return 0

        lax.fori_loop(0, length // 16, norm_body, 0, unroll=2)

    for s in range(seqs):
        raw = dot(ne[s, pl.ds(hw, length), :], ws3)
        sraw[s] = raw
        step = jax.nn.softplus(raw + bias3)
        st[s] = step
        cu = dot3(tri[0], step * rates3)
        cum[s] = cu
        cum_t[s] = cu.T
        last = cu[length - 1 : length]
        pst[s] = pieces3(step)
        ptl[s] = pieces3(jnp.exp(last - cu))
        dec = jnp.exp(cu)
        pdc[s] = pieces3(dec)
        dlast[s] = dot(pieces3(dec[length - 8 :]), xx[...])

    for s in range(seqs):
        for b in range(dm // BW):
            nt[b * BW : (b + 1) * BW, s * length : (s + 1) * length] = ne[
                s, hw : hw + length, b * BW : (b + 1) * BW
            ].T

    @pl.when(has_prev)
    def _():
        halo_copy.wait_recv()

    for s in range(seqs):
        ne[s, 0:hw, :] = norm_rows(halo[s])

    loads[1].wait()

    def filter_block(b, s):
        cols = ds(b * BW, BW)
        m = dot(ne[s], wm[:, cols]).astype(BF)
        ext[s, :, cols] = m
        m = m.astype(F32)
        f = cb_r[cols].reshape(1, BW)
        for k in range(window + 1):
            shift = window - k
            moved = pltpu.roll(m, shift, 0) if shift else m
            f = f + cw_r[k : k + 1, cols] * moved[hw:]
        fil[s, :, cols] = f
        return f

    for s in range(seqs):
        f = filter_block(nblk, s)
        act = f * sigmoid(f)
        i_bf = act[:, :nst].astype(BF)
        o_bf = act[:, nst:].astype(BF)
        infl[s] = i_bf
        outf[s] = o_bf
        inf_t[s] = i_bf.T
        outf_t[s] = o_bf.T
        sco[s] = dot_nt(o_bf, i_bf)
        sco_t[s] = dot_nt(i_bf, o_bf)

    def signal_body(b, _):
        cols = ds(b * BW, BW)
        for s in range(seqs):
            f = filter_block(b, s)
            sig = f * sigmoid(f)
            x = xx[:, cols]
            dr = sig * dot(pst[s], x)
            drv[s, :, cols] = dr.astype(BF)
            sc = (dr * dot(ptl[s], x)).astype(BF)
            scl[s, :, cols] = sc
            y[s, :, cols] = skw[0:1, cols] * sig
            summ = dot(inf_t[s], sc)
            sum_s[2 * b, s] = summ[:, :LN]
            sum_s[2 * b + 1, s] = summ[:, LN:]
        return 0

    lax.fori_loop(0, nblk, signal_body, 0)

    def relay(c, in_buf, out_buf, sems, has_in, has_out, to):
        copy = pltpu.make_async_remote_copy(
            src_ref=out_buf.at[c], dst_ref=in_buf.at[c], send_sem=sems[0].at[c],
            recv_sem=sems[1].at[c], device_id=to, device_id_type=MESH,
        )

        @pl.when(has_in)
        def _():
            copy.wait_recv()

        @pl.when(has_out)
        def _():
            for s in range(seqs):
                row = dlast[s, 7:8, ds(c * LN, LN)]
                out_buf[c, s] = (row * in_buf[c, s].astype(F32) + sum_s[c, s]).astype(
                    out_buf.dtype
                )
            copy.start()

    def relay_slot(slot, skew, *rest):
        c = slot - skew

        @pl.when((c >= 0) & (c < nchunk))
        def _():
            relay(c, *rest)

    SM_CONVB = 0
    SM_GATE = SM_CONVB + xbc // LN
    SM_NORM = SM_GATE + di // LN
    SM_CONVW = SM_NORM + dm // LN
    SM_HEADS = SM_CONVW + (window + 1) * (xbc // LN)
    SM_STEP = -(-(SM_HEADS + 3) // 8) * 8
    sm[...] = jnp.zeros_like(sm)

    def small_one(row, value):
        sm[row // 128, pl.ds(row % 128, 1), :] = value

    def small_put(base, b, value):
        small_one(base + 2 * b, value[:, :LN])
        small_one(base + 2 * b + 1, value[:, LN:])

    half = length // 2
    d_r = lax.broadcasted_iota(jnp.int32, (half, half), 0)
    d_c = lax.broadcasted_iota(jnp.int32, (half, half), 1)
    NEG = -1e30

    def columns_of(s, j):
        moved = pltpu.roll(cum[s], lax.rem(LN - 2 * j, LN), 1)
        return moved[:, 0:1], moved[:, 1:2]

    def pair_forward(j, s):
        cols = ds(j * LN, LN)
        d = drv[s, :, cols]
        lane_low = lane128 < hp
        top, bottom = [], []
        for hh, col in enumerate(columns_of(s, j)):
            row = cum_t[s, pl.ds(2 * j + hh, 1), :]
            fa = jnp.exp(jnp.where(d_r >= d_c, col[:half] - row[:, :half], NEG))
            fb = jnp.exp(col[half:] - row[:, :half])
            fc = jnp.exp(jnp.where(d_r >= d_c, col[half:] - row[:, half:], NEG))
            top.append((sco[s, :half, :half] * fa).astype(BF))
            bottom.append(
                jnp.concatenate(
                    [
                        (sco[s, half:, :half] * fb).astype(BF),
                        (sco[s, half:, half:] * fc).astype(BF),
                    ],
                    axis=1,
                )
            )
        lo = dot(jnp.concatenate(top, axis=0), d[:half])
        hi = dot(jnp.concatenate(bottom, axis=0), d)
        y[s, :half, cols] += jnp.where(lane_low, lo[:half], lo[half:])
        y[s, half:, cols] += jnp.where(lane_low, hi[:half], hi[half:])

    loads[2].wait()
    loads[3].wait()
    loads[4].wait()

    fskew = (3 * ctx) // 2
    bskew = (3 * (nctx - 1 - ctx)) // 2
    slots = nchunk + (3 * (nctx - 1)) // 2

    f_args = (in_f, sum_s, (fs_s, fs_r), has_prev, has_next, nxt)
    b_args = (in_b, out_b, (bs_s, bs_r), has_next, has_prev, prv)

    def forward_body(b, _):
        cols = ds(b * BW, BW)
        relay_slot(2 * b, fskew, *f_args)
        for s in range(seqs):
            big[s, 0:length, cols] = dot_nt(cot[s], wo[cols, :])
            pair_forward(2 * b, s)
        relay_slot(2 * b + 1, fskew, *f_args)
        for s in range(seqs):
            z[s, :, cols] = dot(ne[s, hw : hw + length, :], wg[:, cols])
            pair_forward(2 * b + 1, s)
        return 0

    lax.fori_loop(0, nblk, forward_body, 0)

    def forward_rest(slot, _):
        relay_slot(slot, fskew, *f_args)
        return 0

    lax.fori_loop(nchunk, slots, forward_rest, 0)

    def sent_forward(c, _):
        @pl.when(has_next)
        def _():
            pltpu.make_async_remote_copy(
                src_ref=sum_s.at[c], dst_ref=in_f.at[c], send_sem=fs_s.at[c],
                recv_sem=fs_r.at[c], device_id=nxt, device_id_type=MESH,
            ).wait_send()

        return 0

    acc_a[...] = jnp.zeros_like(acc_a)
    acc_b[...] = jnp.zeros_like(acc_b)

    def gate_body(b, _):
        cols = ds(b * BW, BW)
        for s in range(seqs):
            pr = jnp.concatenate([in_f[2 * b, s], in_f[2 * b + 1, s]], axis=1)
            phi, plo = split2(pr)
            out = (dot(outf[s], phi) + dot(outf[s], plo)) * dot(pdc[s], xx[:, cols])
            yy = y[s, :, cols] + out
            y[s, :, cols] = yy
            zz = z[s, :, cols]
            gated = yy * (zz * sigmoid(zz))
            q = big[s, 0:length, cols] * gg_r[cols].reshape(1, BW)
            a = gated * gated
            c = q * gated
            acc_a[s] += a[:, :LN] + a[:, LN:]
            acc_b[s] += c[:, :LN] + c[:, LN:]
        return 0

    lax.fori_loop(0, nblk, gate_body, 0)

    inv_out, mean_out = [], []
    for s in range(seqs):
        iv = lax.rsqrt(jnp.sum(acc_a[s], axis=-1, keepdims=True) / di + EPSILON)
        inv_out.append(iv)
        mean_out.append(iv * jnp.sum(acc_b[s], axis=-1, keepdims=True) / di)
    gout[...] = jnp.zeros_like(gout)
    lax.fori_loop(0, nchunk, sent_forward, 0)

    def grad_body(b, _):
        cols = ds(b * BW, BW)
        gg_sum = jnp.zeros((1, BW), F32)
        for s in range(seqs):
            yy = y[s, :, cols]
            zz = z[s, :, cols]
            sg = sigmoid(zz)
            act = zz * sg
            unit = (yy * act) * inv_out[s]
            gain_row = gg_r[cols].reshape(1, BW)
            g = big[s, 0:length, cols]
            no = (unit * gain_row).astype(BF)
            nrm[s, :, cols] = no
            nrt[cols, s * length : (s + 1) * length] = no.T
            gg_sum = gg_sum + jnp.sum(g * unit, axis=0, keepdims=True)
            gr = inv_out[s] * (g * gain_row - unit * mean_out[s])
            gyb = (gr * act).astype(BF)
            gy[s, :, cols] = gyb
            ggz[s, :, cols] = (gr * yy * (sg * (1.0 + zz * (1.0 - sg)))).astype(BF)
            w = gyb.astype(F32) * dot(pdc[s], xx[:, cols])
            whi, wlo = split2(w)
            pr = jnp.concatenate([in_f[2 * b, s], in_f[2 * b + 1, s]], axis=1)
            gp = dot(outf_t[s], whi) + dot(outf_t[s], wlo)
            sum_s[2 * b, s] = gp[:, :LN]
            sum_s[2 * b + 1, s] = gp[:, LN:]
            phi, plo = split2(pr)
            gout[s] += dot_nt(whi, phi) + (dot_nt(wlo, phi) + dot_nt(whi, plo))
        small_put(SM_GATE, b, gg_sum)
        return 0

    lax.fori_loop(0, nblk, grad_body, 0)

    gsc[...] = jnp.zeros_like(gsc)

    def pair_backward(j, s):
        cols = ds(j * LN, LN)
        d = drv[s, :, cols]
        g = gy[s, :, cols]
        lane_low = lane128 < hp
        zero = jnp.zeros_like(d)
        top, bottom = [], []
        t1 = t2 = t3 = None
        for hh, col in enumerate(columns_of(s, j)):
            row = cum_t[s, pl.ds(2 * j + hh, 1), :]
            dh = jnp.where(lane_low if hh == 0 else jnp.logical_not(lane_low), d, zero)
            m1 = dot_nt(dh[:half], g)
            m2 = dot_nt(dh[half:], g[half:])
            fa = jnp.exp(jnp.where(d_r <= d_c, row[:, :half] - col[:half], NEG))
            fb = jnp.exp(row[:, half:] - col[:half])
            fc = jnp.exp(jnp.where(d_r <= d_c, row[:, half:] - col[half:], NEG))
            top.append(
                jnp.concatenate(
                    [
                        (sco_t[s, :half, :half] * fa).astype(BF),
                        (sco_t[s, :half, half:] * fb).astype(BF),
                    ],
                    axis=1,
                )
            )
            bottom.append((sco_t[s, half:, half:] * fc).astype(BF))
            p1, p2, p3 = m1[:, :half] * fa, m1[:, half:] * fb, m2 * fc
            t1, t2, t3 = (p1, p2, p3) if hh == 0 else (t1 + p1, t2 + p2, t3 + p3)
        gsc[s, :half, :half] += t1
        gsc[s, :half, half:] += t2
        gsc[s, half:, half:] += t3
        lo = dot(jnp.concatenate(top, axis=0), g)
        hi = dot(jnp.concatenate(bottom, axis=0), g[half:])
        z[s, :half, cols] = jnp.where(lane_low, lo[:half], lo[half:])
        z[s, half:, cols] = jnp.where(lane_low, hi[:half], hi[half:])

    sent = []
    running = []

    def wide(a_ref, b_ref, rows, cols):
        t = dot(a_ref[rows, 0:length], b_ref[0, :, cols])
        for s in range(1, seqs):
            t = t + dot(a_ref[rows, s * length : (s + 1) * length], b_ref[s, :, cols])
        return t

    def from_out(i):
        return lambda part, r0, n: wide(
            nrt, cot, pl.ds(pl.multiple_of(i * dm + r0, 16), n),
            pl.ds(pl.multiple_of(part * (dm // 2), LN), dm // 2),
        )

    def from_columns(ref, base, w):
        return lambda part, r0, n: wide(
            nt, ref, pl.ds(pl.multiple_of(r0, 16), n),
            pl.ds(pl.multiple_of(base + part * w, LN), w),
        )

    def group_steps(g, produce, out_ref, row0, col0, part_cols):
        sb, rb, rr, acc, rx = bufs[5 * g : 5 * g + 5]
        total, w = sb.shape
        kind = sb.dtype
        tile = min(192, total // 2)

        def place(off, n, part):
            if part_cols:
                return out_ref.at[
                    pl.ds(pl.multiple_of(row0 + off, 8), n),
                    pl.ds(pl.multiple_of(col0 + part * w, LN), w),
                ]
            return out_ref.at[pl.ds(pl.multiple_of(part * total + off, 8), n), :]

        def copy_of(i, src, dst, peer):
            copy = pltpu.make_async_remote_copy(
                src_ref=src, dst_ref=dst, send_sem=ar_s.at[g, i], recv_sem=ar_r.at[g, i],
                device_id=peer, device_id_type=MESH,
            )
            copy.start()
            return copy

        def rows_at(start, n):
            return pl.ds(pl.multiple_of(start, 8), n)

        def tiles(count, body):
            if count == 1:
                body(0)
            else:
                lax.fori_loop(0, count, lambda i, _: (body(i), 0)[1], 0)

        def give(i):
            sb[rows_at(i * tile, tile), :] = produce(1 - core, i * tile, tile).astype(kind)

        tiles(total // tile, give)
        copy = copy_of(0, sb, rb, core_peer)
        yield
        copy.wait()
        bit, peer = stages[0]
        n = total // 2

        def own(i, start):
            r0 = start + i * tile
            return produce(core, r0, tile) + rb[rows_at(r0, tile), :].astype(F32)

        def give_half(i):
            sb[rows_at(i * tile, tile), :] = own(i, (1 - bit) * n).astype(kind)

        def keep_half(i):
            acc[rows_at(i * tile, tile), :] = own(i, bit * n)

        tiles(n // tile, give_half)
        copy = copy_of(1, sb.at[pl.ds(0, n)], rr.at[pl.ds(0, n)], peer)
        tiles(n // tile, keep_half)
        first = copy
        if not extras:
            sent.append(first)
        yield
        base, at, off = 0, 0, bit * n
        offs = [off]
        for k in range(1, len(stages)):
            copy.wait_recv()
            bit, peer = stages[k]
            n //= 2
            nbase = base + 2 * n
            r_give = (1 - bit) * n
            r_keep = bit * n
            sb[nbase : nbase + n, :] = (
                acc[rows_at(at + r_give, n), :]
                + rr[rows_at(base + r_give, n), :].astype(F32)
            ).astype(kind)
            copy = copy_of(k + 1, sb.at[pl.ds(nbase, n)], rr.at[pl.ds(nbase, n)], peer)
            sent.append(copy)
            acc[rows_at(at + r_keep, n), :] += rr[rows_at(base + r_keep, n), :].astype(F32)
            base, at, off = nbase, at + r_keep, off + r_keep
            offs.append(off)
            yield
        copy.wait_recv()
        value = acc[rows_at(at, n), :] + rr[base : base + n, :].astype(F32)
        if extras:
            first.wait_send()
        for e, (_, peer) in enumerate(extras):
            mine = value.astype(kind)
            sb[e * n : (e + 1) * n, :] = mine
            copy = pltpu.make_async_remote_copy(
                src_ref=sb.at[pl.ds(e * n, n)], dst_ref=rx.at[e], send_sem=ex_s.at[g, e],
                recv_sem=ex_r.at[g, e], device_id=peer, device_id_type=MESH,
            )
            copy.start()
            copy.wait()
            value = mine.astype(F32) + rx[e].astype(F32)
        done = total - n
        sb[done:, :] = value.astype(kind)
        k = len(stages) - 1
        here = place(offs[k], n, core)
        local = pltpu.make_async_copy(sb.at[pl.ds(done, n)], here, loc_sem.at[g])
        local.start()
        copy = copy_of(5, sb.at[pl.ds(done, n)], here, stages[k][1])
        sent.append(copy)
        yield
        local.wait()
        for k in range(len(stages) - 2, -1, -1):
            copy.wait_recv()
            n *= 2
            here = place(offs[k], n, core)
            copy = copy_of(8 - k, here, here, stages[k][1])
            sent.append(copy)
            yield
        copy.wait_recv()
        here = place(0, total, core)
        copy = copy_of(9, here, here, core_peer)
        sent.append(copy)
        yield
        copy.wait_recv()

    wide_w = dm // 2
    groups = [
        (0, from_out(0), go_h, 0, 0, True),
        (1, from_out(1), go_h, dm, 0, True),
        (2, from_columns(ggz, 0, wide_w), gw_h, 0, 0, True),
        (3, from_columns(ggz, dm, wide_w), gw_h, 0, dm, True),
        (4, from_columns(nrm, 0, wide_w), gm_h, 0, 0, True),
        (5, from_columns(nrm, dm, wide_w), gm_h, 0, dm, True),
        (6, from_columns(ggz, 0, LN), gm_h, 0, di, True),
        (7, lambda part, r0, n: sm[part, pl.ds(pl.multiple_of(r0, 8), n), :], sm_h, 0, 0, False),
    ]

    def service(new=()):
        for steps in list(running):
            if next(steps, running) is running:
                running.remove(steps)
        for g in new:
            steps = group_steps(*groups[g])
            next(steps)
            running.append(steps)

    def backward_body(j, _):
        relay_slot(j, bskew, *b_args)
        for s in range(seqs):
            pair_backward(j, s)
        return 0

    new = [[0], [1], [2], [3], [], []]
    for i in range(nblk):
        service(new[i])
        lax.fori_loop(2 * i, 2 * i + 2, backward_body, 0)

    for s in range(seqs):
        for i in range(dm // BW):
            cols = slice(i * BW, (i + 1) * BW)
            pj = dot(nrm[s], wo[:, cols])
            res_r[s, :, cols] = (tok[s, :, cols].astype(F32) + pj).astype(BF)
            gn[s, :, cols] = dot_nt(ggz[s], wg[cols, :])
    res_copy = pltpu.make_async_copy(res_r, res_h, tok_sem.at[0])
    res_copy.start()
    service()

    def backward_rest(slot, _):
        relay_slot(slot, bskew, *b_args)
        return 0

    lax.fori_loop(nchunk, slots, backward_rest, 0)
    service()

    ginf[...] = jnp.zeros_like(ginf)
    hs_d[...] = jnp.zeros_like(hs_d)
    hs_g[...] = jnp.zeros_like(hs_g)
    bdh[...] = jnp.zeros_like(bdh)

    def head_sum(v, x):
        hi, lo = split2(v)
        return dot_nt(hi, x) + dot_nt(lo, x)

    def head_sum3(v, x):
        hi, mid, lo = split3(v)
        return dot_nt(hi, x) + dot_nt(mid, x) + dot_nt(lo, x)

    def gh_copy(b):
        cols = ds(b * BW, BW)
        return pltpu.make_async_remote_copy(
            src_ref=big.at[:, pl.ds(0, 8), cols], dst_ref=big.at[:, pl.ds(length, 8), cols],
            send_sem=gh_s.at[b], recv_sem=gh_r.at[b], device_id=prv, device_id_type=MESH,
        )

    @pl.when(jnp.logical_not(has_next))
    def _():
        big[:, length : length + 8, :] = jnp.zeros((seqs, 8, xbc), F32)

    def finish_block(b, s, ga):
        cols = ds(b * BW, BW)
        f = fil[s, :, cols]
        sg = sigmoid(f)
        gf = ga * (sg * (1.0 + f * (1.0 - sg)))
        big[s, 0:length, cols] = gf
        return jnp.sum(gf, axis=0, keepdims=True)

    def last_body(b, _):
        cols = ds(b * BW, BW)
        cb_sum = jnp.zeros((1, BW), F32)
        sk_sum = jnp.zeros((1, BW), F32)
        x = xx[:, cols]
        for s in range(seqs):
            lt = jnp.concatenate([in_b[2 * b, s], in_b[2 * b + 1, s]], axis=1)
            pr = jnp.concatenate([in_f[2 * b, s], in_f[2 * b + 1, s]], axis=1)
            f = fil[s, :, cols]
            sg = sigmoid(f)
            sig = f * sg
            stw = dot(pst[s], x)
            gst = dot(infl[s], lt) * dot(ptl[s], x)
            gd = z[s, :, cols]
            gyf = gy[s, :, cols].astype(F32)
            sk_row = skw[0:1, cols]
            gg = gst + gd
            ga = sk_row * gyf + stw * gg
            t1 = stw * sig * gst
            dd = gyf * (y[s, :, cols] - sk_row * sig) - drv[s, :, cols].astype(F32) * gd - t1
            hs_d[s] += head_sum(dd, x)
            hs_g[s] += head_sum(sig * gg, x)
            bd = jnp.sum(t1, axis=0, keepdims=True) + dlast[s, 7:8, cols] * jnp.sum(
                lt.astype(F32) * pr, axis=0, keepdims=True
            )
            bdh[s] += head_sum3(jnp.broadcast_to(bd, (8, BW)), x)
            sk_sum = sk_sum + jnp.sum(gyf * sig, axis=0, keepdims=True)
            ginf[s] += dot_nt(scl[s, :, cols], lt)
            gf = ga * (sg * (1.0 + f * (1.0 - sg)))
            big[s, 0:length, cols] = gf
            cb_sum = cb_sum + jnp.sum(gf, axis=0, keepdims=True)
        small_put(SM_CONVB, b, cb_sum)
        sk_row_r[0:1, cols] = sk_sum

        @pl.when(has_prev)
        def _():
            gh_copy(b).start()

        return 0

    for i in range(0, nblk, 2):
        lax.fori_loop(i, i + 2, last_body, 0)
        service()

    cb_sum = jnp.zeros((1, BW), F32)
    for s in range(seqs):
        gst_bf = gsc[s].astype(BF)
        gi = ginf[s] + dot(gst_bf, outf[s])
        go = gout[s] + dot(gst_bf.T, infl[s])
        cb_sum = cb_sum + finish_block(nblk, s, jnp.concatenate([gi, go], axis=1))
    small_put(SM_CONVB, nblk, cb_sum)

    @pl.when(has_prev)
    def _():
        gh_copy(nblk).start()

    row_i = lax.broadcasted_iota(jnp.int32, (length, LN), 0)
    glr = jnp.zeros((1, LN), F32)
    gsb = jnp.zeros((1, LN), F32)
    grl = []
    for s in range(seqs):
        gc = hs_d[s] + jnp.where(row_i == length - 1, bdh[s, 0:1], 0.0)
        terms = dot3(tri[1], gc)
        gst = hs_g[s] + terms * rates3
        glr = glr + jnp.sum(terms * st[s], axis=0, keepdims=True)
        graw = gst * sigmoid(sraw[s] + bias3)
        gsb = gsb + jnp.sum(graw, axis=0, keepdims=True)
        grl.append(jnp.where(lane128 < heads, graw, 0.0).astype(BF))
    sk_h = head_sum3(jnp.broadcast_to(sk_row_r[0:1, :], (8, di)), xx[...])
    small_one(SM_HEADS, gsb)
    small_one(SM_HEADS + 1, rates3 * glr)
    small_one(SM_HEADS + 2, sk_h[0:1])
    stepg = dot(grl[0].T, ne[0, hw:, :])
    for s in range(1, seqs):
        stepg = stepg + dot(grl[s].T, ne[s, hw:, :])
    for i in range(dm // LN):
        row = SM_STEP + 24 * i
        for lo, hi in ((row, min(row + 24, 128)), (max(row, 128), row + 24)):
            if lo < hi:
                sm[lo // 128, lo % 128 : lo % 128 + hi - lo, :] = stepg[
                    lo - row : hi - row, i * LN : (i + 1) * LN
                ]

    def mixed_body(b):
        cols = ds(b * BW, BW)

        @pl.when(has_next)
        def _():
            gh_copy(b).wait_recv()

        parts = []
        sums = [jnp.zeros((1, BW), F32) for _ in range(window + 1)]
        for s in range(seqs):
            gf = big[s, :, cols]
            rows = gf.shape[0]
            m = ext[s, :, cols].astype(F32)
            gm = jnp.zeros((length, BW), F32)
            for k in range(window + 1):
                shift = window - k
                moved = pltpu.roll(gf, rows - shift, 0) if shift else gf
                gm = gm + cw_r[k : k + 1, cols] * moved[:length]
                em = pltpu.roll(m, shift, 0) if shift else m
                sums[k] = sums[k] + jnp.sum(gf[:length] * em[hw:], axis=0, keepdims=True)
            gmb = gm.astype(BF)
            parts.append(gmb)
            gn[s] += dot_nt(gmb, wm[:, cols])
        for k in range(window + 1):
            small_put(SM_CONVW + k * (xbc // LN), b, sums[k])
        return parts

    def mixed_loop(b, _):
        cols = ds(b * BW, BW)
        for s, part in enumerate(mixed_body(b)):
            nrm[s, :, cols] = part
        return 0

    lax.fori_loop(0, 3, mixed_loop, 0)
    service([4])
    lax.fori_loop(3, 6, mixed_loop, 0)
    service([5])
    for s, part in enumerate(mixed_body(6)):
        ggz[s, :, 0:BW] = part
    service([6])
    for s in range(seqs):
        gn[s] += dot_nt(grl[s], ws3)
    service()

    @pl.when(has_next)
    def _():
        halo_copy.wait_send()

    def token_body(i, sums):
        for s in range(seqs):
            rows = ds(i * 16, 16)
            v = tok[s, rows, :].astype(F32)
            inv = lax.rsqrt(jnp.mean(v * v, axis=-1, keepdims=True) + EPSILON)
            unit = v * inv
            gr = gn[s, rows, :]
            sums = sums + jnp.sum(gr * unit, axis=0, keepdims=True)
            q = gr * gain
            back = inv * (q - unit * jnp.mean(q * unit, axis=-1, keepdims=True))
            tok[s, rows, :] = (cot[s, rows, :].astype(F32) + back).astype(BF)
        return sums

    n_sum = lax.fori_loop(0, length // 16, token_body, jnp.zeros((1, dm), F32))
    for i in range(dm // LN):
        small_one(SM_NORM + i, n_sum[:, i * LN : (i + 1) * LN])
    tg_copy = pltpu.make_async_copy(tok, tg_h, tok_sem.at[1])
    tg_copy.start()
    service([7])
    while running:
        service()
    res_copy.wait()
    tg_copy.wait()
    for copy in sent:
        copy.wait_send()

    def drain(c, _):
        @pl.when(has_prev)
        def _():
            pltpu.make_async_remote_copy(
                src_ref=out_b.at[c], dst_ref=in_b.at[c], send_sem=bs_s.at[c],
                recv_sem=bs_r.at[c], device_id=prv, device_id_type=MESH,
            ).wait_send()

        return 0

    lax.fori_loop(0, nchunk, drain, 0)

    def drain_halo(b, _):
        @pl.when(has_prev)
        def _():
            gh_copy(b).wait_send()

        return 0

    lax.fori_loop(0, xbc // BW, drain_halo, 0)


def on_device(nctx, *args):
    tokens, norm_gain, wg, wm, ws, conv_w, conv_b, sb, lr, sk, gg, wo, cot = args
    seqs, length, dm = tokens.shape
    di = wg.shape[1]
    xbc = wm.shape[1]
    heads = ws.shape[1]
    nst = (xbc - di) // 2
    nchunk = di // LN
    hw = 16
    vm = pltpu.VMEM
    any_spec = pl.BlockSpec(memory_space=pl.ANY)
    vm_spec = pl.BlockSpec(memory_space=vm)
    dma = pltpu.SemaphoreType.DMA
    extras = max(1, (nctx // 16).bit_length())
    bufs = []
    for rows, w, kind in [(dm, dm // 2, BF)] * 6 + [(dm, LN, BF), (128, LN, F32)]:
        bufs += [vm((rows, w), kind)] * 3 + [vm((rows // 2, w), F32)]
        bufs += [vm((extras, rows // 16, w), kind) if nctx > 8 else vm((1, 16, LN), kind)]
    out = pl.pallas_call(
        functools.partial(layer_kernel, nctx),
        out_shape=(
            jax.ShapeDtypeStruct(tokens.shape, BF),
            jax.ShapeDtypeStruct(tokens.shape, BF),
            jax.ShapeDtypeStruct((di, dm), BF),
            jax.ShapeDtypeStruct((dm, di), BF),
            jax.ShapeDtypeStruct((dm, xbc), BF),
            jax.ShapeDtypeStruct((256, LN), F32),
        ),
        in_specs=[any_spec, vm_spec, any_spec, any_spec] + [vm_spec] * 7 + [any_spec] * 2,
        out_specs=(any_spec,) * 6,
        scratch_shapes=[
            vm((seqs, length, dm), BF),
            vm((seqs, length, dm), BF),
            vm((dm, di), BF),
            vm((dm, xbc), BF),
            vm((di, dm), BF),
            vm((seqs, hw, dm), BF),
            vm((seqs, hw + length, dm), BF),
            vm((dm, seqs * length), BF),
            vm((seqs, hw + length, xbc), BF),
            vm((seqs, length, xbc), F32),
            vm((seqs, length, di), BF),
            vm((seqs, length, di), BF),
            vm((seqs, length, di), F32),
            vm((seqs, length, di), F32),
            vm((seqs, length + 8, xbc), F32),
            vm((seqs, length, di), BF),
            vm((seqs, length, di), BF),
            vm((seqs, length, di), BF),
            vm((di, seqs * length), BF),
            vm((seqs, length, LN), F32),
            vm((seqs, length, LN), F32),
            vm((seqs, length, dm), F32),
            vm((nchunk, seqs, nst, LN), F32),
            vm((nchunk, seqs, nst, LN), F32),
            vm((nchunk, seqs, nst, LN), BF),
            vm((nchunk, seqs, nst, LN), BF),
            vm((seqs, length, LN), F32),
            vm((seqs, length, LN), F32),
            vm((seqs, length, LN), F32),
            vm((seqs, LN, length), F32),
            vm((seqs, length, LN), BF),
            vm((seqs, length, LN), BF),
            vm((seqs, length, LN), BF),
            vm((seqs, 8, di), F32),
            vm((seqs, length, nst), BF),
            vm((seqs, length, nst), BF),
            vm((seqs, nst, length), BF),
            vm((seqs, nst, length), BF),
            vm((seqs, length, length), F32),
            vm((seqs, length, length), F32),
            vm((LN, di), BF),
            vm((2, length, length), BF),
            vm((seqs, length, LN), F32),
            vm((seqs, length, LN), F32),
            vm((seqs, 8, LN), F32),
            vm((seqs, length, dm), BF),
            dma((2,)),
            vm((8, di), F32),
            vm((2, 128, LN), F32),
            vm((8, di), F32),
            bufs,
            dma((8, 10)), dma((8, 10)), dma((8,)), dma((8, extras)), dma((8, extras)),
            dma((5,)), dma, dma,
            dma((nchunk,)), dma((nchunk,)), dma((nchunk,)), dma((nchunk,)),
            dma((xbc // BW,)), dma((xbc // BW,)),
        ],
        compiler_params=pltpu.CompilerParams(
            collective_id=0, has_side_effects=True, vmem_limit_bytes=65200 * 1024
        ),
    )(*args)
    res, tg, g_out, g_gate, g_mixer, small = out
    gate0 = xbc // LN
    norm0 = gate0 + di // LN
    convw0 = norm0 + dm // LN
    taps = conv_w.shape[0]
    heads0 = convw0 + taps * (xbc // LN)
    step0 = -(-(heads0 + 3) // 8) * 8
    step = small[step0 : step0 + heads * (dm // LN)].reshape(dm // LN, heads, LN)
    return (
        res, tg, small[norm0:convw0].reshape(dm), g_gate.astype(F32), g_mixer.astype(F32),
        step.transpose(0, 2, 1).reshape(dm, heads),
        small[convw0:heads0].reshape(taps, xbc), small[:gate0].reshape(xbc),
        small[heads0, :heads], small[heads0 + 1, :heads], small[heads0 + 2, :heads],
        small[gate0:norm0].reshape(di), g_out.astype(F32),
    )


def solution(mesh):
    tok = P("seq", "ctx", None)
    return jax.shard_map(
        functools.partial(on_device, mesh.shape["ctx"]),
        mesh=mesh,
        in_specs=(tok,) + (P(),) * 11 + (tok,),
        out_specs=(tok, tok) + (P(),) * 11,
        check_vma=False,
    )
```

```python
import functools

import jax
import jax.numpy as jnp
from jax import lax
from jax.experimental import pallas as pl
from jax.experimental.pallas import tpu as pltpu
from jax.sharding import PartitionSpec as P

MESH = pl.DeviceIdType.MESH
BF = jnp.bfloat16
F32 = jnp.float32
EPSILON = 1e-05
BW = 256
LN = 128
SKEW = 3
PLAN = (
    (0, 1, 2, 0, 1, 2, 3),
    (0,),
    (3, 1),
    (),
    (),
    (2, 0),
    (3,),
    (1, 0, 2),
    (3,),
    (1,),
    (0,),
    (),
    (2, 0, 4, 3),
    (4, 0, 1, 5),
    (0, 2, 6, 5, 3, 4, 1, 6, 2),
    (),
    (5, 3, 7, 4, 7, 1, 6, 1, 4, 2, 5, 2, 3, 4, 7, 6, 3, 5, 4, 7, 6, 5, 4, 7, 6, 4, 5, 7, 6,
    5, 7, 6, 5, 6, 7, 7),
)


def dot(a, b):
    return jnp.dot(a, b, preferred_element_type=F32)


def dot_nt(a, b):
    return lax.dot_general(a, b, (((1,), (1,)), ((), ())), preferred_element_type=F32)


def split2(v):
    hi = v.astype(BF)
    return hi, (v - hi.astype(F32)).astype(BF)


def split3(v):
    hi = v.astype(BF)
    rest = v - hi.astype(F32)
    mid = rest.astype(BF)
    return hi, mid, (rest - mid.astype(F32)).astype(BF)


def dot3(a, v):
    hi, mid, lo = split3(v)
    return dot(a, hi) + dot(a, mid) + dot(a, lo)


def pieces3(v):
    lane = lax.broadcasted_iota(jnp.int32, v.shape, 1)
    hi, mid, lo = split3(v)
    z = jnp.zeros_like(v)
    return jnp.where(
        lane < 32,
        hi.astype(F32),
        jnp.where(lane < 64, mid.astype(F32), jnp.where(lane < 96, lo.astype(F32), z)),
    ).astype(BF)


def sigmoid(v):
    return 1.0 / (1.0 + jnp.exp(-v))


def ds(start, size):
    return pl.ds(pl.multiple_of(start, size), size)


def layer_kernel(
    nctx,
    tok_h, ng_r, wg_h, wm_h, ws_r, cw_r, cb_r, sb_r, lr_r, sk_r, gg_r, wo_h, cot_h,
    res_h, tg_h, go_h, gw_h, gm_h, sm_h,
    tok, cot, wg, wm, wo, halo, ne, nt, ext, fil, drv, scl, y, z, big, gy, ggz, nrm, nrt,
    acc_a, acc_b, gn, sum_s, in_f, out_b, in_b, sraw, st, cum, cum_t, pst, ptl, pdc,
    dlast, infl, outf, inf_t, outf_t, sco, sco_t, xx, tri, hs_d, hs_g, bdh,
    res_r, tok_sem, skw, sm, sk_row_r, bufs, ar_s, ar_r, loc_sem, ex_s, ex_r,
    in_sem, halo_s, halo_r, fs_s, fs_r, bs_s, bs_r, gh_s, gh_r,
):
    seqs, length, dm = tok.shape
    di = wg.shape[1]
    xbc = wm.shape[1]
    heads = ws_r.shape[1]
    hp = di // heads
    nst = (xbc - di) // 2
    window = cw_r.shape[0] - 1
    nblk = di // BW
    gsc, gout, ginf = sco, acc_a, acc_b
    nchunk = di // LN
    hw = 16
    seq = lax.axis_index("seq")
    ctx = lax.axis_index("ctx")
    has_prev = ctx > 0
    has_next = ctx < nctx - 1
    prv = (seq, ctx - 1)
    nxt = (seq, ctx + 1)

    barrier = pltpu.get_barrier_semaphore()

    @pl.when(has_prev)
    def _():
        pl.semaphore_signal(barrier, inc=1, device_id=prv, device_id_type=MESH)

    @pl.when(has_next)
    def _():
        pl.semaphore_signal(barrier, inc=1, device_id=nxt, device_id_type=MESH)

    loads = [
        pltpu.make_async_copy(a, b, in_sem.at[i])
        for i, (a, b) in enumerate(
            ((tok_h, tok), (wm_h, wm), (cot_h, cot), (wo_h, wo), (wg_h, wg))
        )
    ]
    for copy in loads:
        copy.start()

    core = lax.rem(ctx, 2)

    def flipped(index, mask):
        bit = lax.rem(index // mask, 2)
        return bit, index + mask - 2 * mask * bit

    core_peer = (seq, flipped(ctx, 1)[1])
    stages = []
    for mask in (1 + core, 2 - core):
        bit, other = flipped(seq, mask)
        stages.append((bit, (other, ctx)))
    in_row = lax.rem(ctx // 2, 4)
    row_peers = [(seq, ctx + 2 * (lax.rem(in_row + d, 4) - in_row)) for d in (1, 2, 3)]
    extras = []
    mask = 8
    while mask < nctx:
        extras.append((seq, flipped(ctx, mask)[1]))
        mask *= 2
    peers = [peer for _, peer in stages] + row_peers + extras
    for peer in peers:
        pl.semaphore_signal(barrier, inc=1, device_id=peer, device_id_type=MESH)
    pl.semaphore_wait(
        barrier, has_prev.astype(jnp.int32) + has_next.astype(jnp.int32) + len(peers)
    )
    loads[0].wait()

    halo_copy = pltpu.make_async_remote_copy(
        src_ref=tok.at[:, pl.ds(length - hw, hw), :], dst_ref=halo, send_sem=halo_s,
        recv_sem=halo_r, device_id=nxt, device_id_type=MESH,
    )

    @pl.when(has_next)
    def _():
        halo_copy.start()

    @pl.when(jnp.logical_not(has_prev))
    def _():
        halo[...] = jnp.zeros_like(halo)
        in_f[...] = jnp.zeros_like(in_f)

    @pl.when(jnp.logical_not(has_next))
    def _():
        in_b[...] = jnp.zeros_like(in_b)

    lane128 = lax.broadcasted_iota(jnp.int32, (1, LN), 1)
    r_i = lax.broadcasted_iota(jnp.int32, (LN, di), 0)
    c_i = lax.broadcasted_iota(jnp.int32, (LN, di), 1)
    xx[...] = jnp.where((r_i % 32 == c_i // hp) & (r_i < 96), 1.0, 0.0).astype(BF)
    t_r = lax.broadcasted_iota(jnp.int32, (length, length), 0)
    t_c = lax.broadcasted_iota(jnp.int32, (length, length), 1)
    tri[0] = jnp.where(t_r >= t_c, 1.0, 0.0).astype(BF)
    tri[1] = jnp.where(t_r <= t_c, 1.0, 0.0).astype(BF)
    k_i = lax.broadcasted_iota(jnp.int32, (heads, LN), 0)
    l_i = lax.broadcasted_iota(jnp.int32, (heads, LN), 1)
    rep = jnp.where((l_i % 32 == k_i) & (l_i < 96), 1.0, 0.0)

    def replicated(row_ref):
        row = jnp.broadcast_to(row_ref[...].reshape(1, heads), (8, heads))
        hi, mid, lo = split3(row)
        r = rep.astype(BF)
        return (dot(hi, r) + dot(mid, r) + dot(lo, r))[0:1]

    ws3 = dot(ws_r[...], rep.astype(BF)).astype(BF)
    bias3 = replicated(sb_r)
    rates3 = -jnp.exp(replicated(lr_r))
    sk8 = jnp.broadcast_to(replicated(sk_r), (8, LN))
    skw[...] = dot(pieces3(sk8), xx[...])

    gain = ng_r[...].reshape(1, dm)

    def norm_rows(rows):
        v = rows.astype(F32)
        inv = lax.rsqrt(jnp.mean(v * v, axis=-1, keepdims=True) + EPSILON)
        return ((v * inv) * gain).astype(BF)

    for s in range(seqs):

        def norm_body(i, _, s=s):
            ne[s, ds(hw + i * 16, 16), :] = norm_rows(tok[s, ds(i * 16, 16), :])
            return 0

        lax.fori_loop(0, length // 16, norm_body, 0, unroll=2)

    for s in range(seqs):
        raw = dot(ne[s, pl.ds(hw, length), :], ws3)
        sraw[s] = raw
        step = jax.nn.softplus(raw + bias3)
        st[s] = step
        cu = dot3(tri[0], step * rates3)
        cum[s] = cu
        cum_t[s] = cu.T
        last = cu[length - 1 : length]
        pst[s] = pieces3(step)
        ptl[s] = pieces3(jnp.exp(last - cu))
        dec = jnp.exp(cu)
        pdc[s] = pieces3(dec)
        dlast[s] = dot(pieces3(dec[length - 8 :]), xx[...])

    for s in range(seqs):
        for b in range(dm // BW):
            nt[b * BW : (b + 1) * BW, s * length : (s + 1) * length] = ne[
                s, hw : hw + length, b * BW : (b + 1) * BW
            ].T

    @pl.when(has_prev)
    def _():
        halo_copy.wait_recv()

    for s in range(seqs):
        ne[s, 0:hw, :] = norm_rows(halo[s])

    loads[1].wait()

    def filter_block(b, s):
        cols = ds(b * BW, BW)
        m = dot(ne[s], wm[:, cols]).astype(BF)
        ext[s, :, cols] = m
        m = m.astype(F32)
        f = cb_r[cols].reshape(1, BW)
        for k in range(window + 1):
            shift = window - k
            moved = pltpu.roll(m, shift, 0) if shift else m
            f = f + cw_r[k : k + 1, cols] * moved[hw:]
        fil[s, :, cols] = f
        return f

    for s in range(seqs):
        f = filter_block(nblk, s)
        act = f * sigmoid(f)
        i_bf = act[:, :nst].astype(BF)
        o_bf = act[:, nst:].astype(BF)
        infl[s] = i_bf
        outf[s] = o_bf
        inf_t[s] = i_bf.T
        outf_t[s] = o_bf.T
        sco[s] = dot_nt(o_bf, i_bf)
        sco_t[s] = dot_nt(i_bf, o_bf)

    def forward_copy(q):
        return pltpu.make_async_remote_copy(
            src_ref=sum_s.at[q], dst_ref=in_f.at[q], send_sem=fs_s.at[q],
            recv_sem=fs_r.at[q], device_id=nxt, device_id_type=MESH,
        )

    def backward_copy(q):
        return pltpu.make_async_remote_copy(
            src_ref=out_b.at[q], dst_ref=in_b.at[q], send_sem=bs_s.at[q],
            recv_sem=bs_r.at[q], device_id=prv, device_id_type=MESH,
        )

    f_skew = SKEW * ctx
    b_skew = SKEW * (nctx - 1 - ctx)
    f_slots = seqs * nchunk + SKEW * (nctx - 1)
    b_slots = seqs * nblk + SKEW * (nctx - 1)

    def forward_slot(slot):
        q = slot - f_skew

        @pl.when((q >= 0) & (q < seqs * nchunk))
        def _():
            @pl.when(has_prev)
            def _():
                forward_copy(q).wait_recv()

            @pl.when(has_next)
            def _():
                row = dlast[q // nchunk, 7:8, ds(lax.rem(q, nchunk) * LN, LN)]
                sum_s[q] = row * in_f[q] + sum_s[q]
                forward_copy(q).start()

    def backward_slot(slot):
        q = slot - b_skew

        @pl.when((q >= 0) & (q < seqs * nblk))
        def _():
            @pl.when(has_next)
            def _():
                backward_copy(q).wait_recv()

            @pl.when(has_prev)
            def _():
                row = dlast[q // nblk, 7:8, ds(lax.rem(q, nblk) * BW, BW)]
                add = jnp.concatenate([sum_s[2 * q], sum_s[2 * q + 1]], axis=1)
                out_b[q] = (row * in_b[q].astype(F32) + add).astype(BF)
                backward_copy(q).start()

    def slots_alone(one, first, last):
        lax.fori_loop(first, last, lambda t, _: (one(t), 0)[1], 0)

    for s in range(seqs):

        def signal_body(b, _, s=s):
            cols = ds(b * BW, BW)
            f = filter_block(b, s)
            sig = f * sigmoid(f)
            x = xx[:, cols]
            dr = sig * dot(pst[s], x)
            drv[s, :, cols] = dr.astype(BF)
            sc = (dr * dot(ptl[s], x)).astype(BF)
            scl[s, :, cols] = sc
            y[s, :, cols] = skw[0:1, cols] * sig
            summ = dot(inf_t[s], sc)
            sum_s[s * nchunk + 2 * b] = summ[:, :LN]
            sum_s[s * nchunk + 2 * b + 1] = summ[:, LN:]
            forward_slot(s * nblk + b)
            return 0

        lax.fori_loop(0, nblk, signal_body, 0)

    SM_CONVB = 0
    SM_GATE = SM_CONVB + xbc // LN
    SM_NORM = SM_GATE + di // LN
    SM_CONVW = SM_NORM + dm // LN
    SM_HEADS = SM_CONVW + (window + 1) * (xbc // LN)
    SM_STEP = -(-(SM_HEADS + 3) // 8) * 8
    sm[...] = jnp.zeros_like(sm)

    def small_one(row, value):
        sm[row // 128, pl.ds(row % 128, 1), :] = value

    def small_put(base, b, value):
        small_one(base + 2 * b, value[:, :LN])
        small_one(base + 2 * b + 1, value[:, LN:])

    half = length // 2
    d_r = lax.broadcasted_iota(jnp.int32, (half, half), 0)
    d_c = lax.broadcasted_iota(jnp.int32, (half, half), 1)
    NEG = -1e30

    def columns_of(s, j):
        moved = pltpu.roll(cum[s], lax.rem(LN - 2 * j, LN), 1)
        return moved[:, 0:1], moved[:, 1:2]

    def pair_forward(j, s):
        cols = ds(j * LN, LN)
        d = drv[s, :, cols]
        lane_low = lane128 < hp
        top, bottom = [], []
        for hh, col in enumerate(columns_of(s, j)):
            row = cum_t[s, pl.ds(2 * j + hh, 1), :]
            fa = jnp.exp(jnp.where(d_r >= d_c, col[:half] - row[:, :half], NEG))
            fb = jnp.exp(col[half:] - row[:, :half])
            fc = jnp.exp(jnp.where(d_r >= d_c, col[half:] - row[:, half:], NEG))
            top.append((sco[s, :half, :half] * fa).astype(BF))
            bottom.append(
                jnp.concatenate(
                    [
                        (sco[s, half:, :half] * fb).astype(BF),
                        (sco[s, half:, half:] * fc).astype(BF),
                    ],
                    axis=1,
                )
            )
        lo = dot(jnp.concatenate(top, axis=0), d[:half])
        hi = dot(jnp.concatenate(bottom, axis=0), d)
        y[s, :half, cols] += jnp.where(lane_low, lo[:half], lo[half:])
        y[s, half:, cols] += jnp.where(lane_low, hi[:half], hi[half:])

    loads[2].wait()
    loads[3].wait()
    loads[4].wait()

    for s in range(seqs):

        def forward_body(b, _, s=s):
            cols = ds(b * BW, BW)
            big[s, 0:length, cols] = dot_nt(cot[s], wo[cols, :])
            pair_forward(2 * b, s)
            z[s, :, cols] = dot(ne[s, hw : hw + length, :], wg[:, cols])
            pair_forward(2 * b + 1, s)
            forward_slot((seqs + s) * nblk + b)
            return 0

        lax.fori_loop(0, nblk, forward_body, 0)

    acc_a[...] = jnp.zeros_like(acc_a)
    acc_b[...] = jnp.zeros_like(acc_b)

    def prior_of(s, b):
        return jnp.concatenate(
            [in_f[s * nchunk + 2 * b], in_f[s * nchunk + 2 * b + 1]], axis=1
        )

    def gate_block(b, s):
        cols = ds(b * BW, BW)
        phi, plo = split2(prior_of(s, b))
        out = (dot(outf[s], phi) + dot(outf[s], plo)) * dot(pdc[s], xx[:, cols])
        yy = y[s, :, cols] + out
        y[s, :, cols] = yy
        zz = z[s, :, cols]
        gated = yy * (zz * sigmoid(zz))
        q = big[s, 0:length, cols] * gg_r[cols].reshape(1, BW)
        a = gated * gated
        c = q * gated
        acc_a[s] += a[:, :LN] + a[:, LN:]
        acc_b[s] += c[:, :LN] + c[:, LN:]

    def grad_block(b, s, iv, mean):
        cols = ds(b * BW, BW)
        yy = y[s, :, cols]
        zz = z[s, :, cols]
        sg = sigmoid(zz)
        act = zz * sg
        unit = (yy * act) * iv
        gain_row = gg_r[cols].reshape(1, BW)
        g = big[s, 0:length, cols]
        no = (unit * gain_row).astype(BF)
        nrm[s, :, cols] = no
        nrt[cols, s * length : (s + 1) * length] = no.T
        sk_row_r[1 + s : 2 + s, cols] = jnp.sum(g * unit, axis=0, keepdims=True)
        gr = iv * (g * gain_row - unit * mean)
        gyb = (gr * act).astype(BF)
        gy[s, :, cols] = gyb
        ggz[s, :, cols] = (gr * yy * (sg * (1.0 + zz * (1.0 - sg)))).astype(BF)
        w = gyb.astype(F32) * dot(pdc[s], xx[:, cols])
        whi, wlo = split2(w)
        gp = dot(outf_t[s], whi) + dot(outf_t[s], wlo)
        sum_s[s * nchunk + 2 * b] = gp[:, :LN]
        sum_s[s * nchunk + 2 * b + 1] = gp[:, LN:]
        phi, plo = split2(prior_of(s, b))
        gout[s] += dot_nt(whi, phi) + (dot_nt(wlo, phi) + dot_nt(whi, plo))

    first_done = f_slots - nchunk * (seqs - 1)
    slots_alone(forward_slot, seqs * nchunk, first_done)
    for s in range(seqs):
        slot0 = first_done + s * nchunk

        def passing(i, s=s, slot0=slot0):
            if s < seqs - 1:
                forward_slot(slot0 + i)
            else:
                backward_slot(i)

        def gate_body(b, _, s=s, passing=passing):
            gate_block(b, s)
            passing(b)
            return 0

        lax.fori_loop(0, nblk, gate_body, 0)
        iv = lax.rsqrt(jnp.sum(acc_a[s], axis=-1, keepdims=True) / di + EPSILON)
        mean = iv * jnp.sum(acc_b[s], axis=-1, keepdims=True) / di
        gout[s] = jnp.zeros_like(gout[s])

        def sent_forward(c, _, s=s):
            @pl.when(has_next)
            def _():
                forward_copy(s * nchunk + c).wait_send()

            return 0

        lax.fori_loop(0, nchunk, sent_forward, 0)

        def grad_body(b, _, s=s, iv=iv, mean=mean, passing=passing):
            grad_block(b, s, iv, mean)
            passing(nblk + b)
            return 0

        lax.fori_loop(0, nblk, grad_body, 0)

    def gate_gain_body(b, _):
        cols = ds(b * BW, BW)
        total = sk_row_r[1:2, cols]
        for s in range(1, seqs):
            total = total + sk_row_r[1 + s : 2 + s, cols]
        small_put(SM_GATE, b, total)
        return 0

    lax.fori_loop(0, nblk, gate_gain_body, 0)

    gsc[...] = jnp.zeros_like(gsc)

    def pair_backward(j, s):
        cols = ds(j * LN, LN)
        d = drv[s, :, cols]
        g = gy[s, :, cols]
        lane_low = lane128 < hp
        zero = jnp.zeros_like(d)
        top, bottom = [], []
        t1 = t2 = t3 = None
        for hh, col in enumerate(columns_of(s, j)):
            row = cum_t[s, pl.ds(2 * j + hh, 1), :]
            dh = jnp.where(lane_low if hh == 0 else jnp.logical_not(lane_low), d, zero)
            m1 = dot_nt(dh[:half], g)
            m2 = dot_nt(dh[half:], g[half:])
            fa = jnp.exp(jnp.where(d_r <= d_c, row[:, :half] - col[:half], NEG))
            fb = jnp.exp(row[:, half:] - col[:half])
            fc = jnp.exp(jnp.where(d_r <= d_c, row[:, half:] - col[half:], NEG))
            top.append(
                jnp.concatenate(
                    [
                        (sco_t[s, :half, :half] * fa).astype(BF),
                        (sco_t[s, :half, half:] * fb).astype(BF),
                    ],
                    axis=1,
                )
            )
            bottom.append((sco_t[s, half:, half:] * fc).astype(BF))
            p1, p2, p3 = m1[:, :half] * fa, m1[:, half:] * fb, m2 * fc
            t1, t2, t3 = (p1, p2, p3) if hh == 0 else (t1 + p1, t2 + p2, t3 + p3)
        gsc[s, :half, :half] += t1
        gsc[s, :half, half:] += t2
        gsc[s, half:, half:] += t3
        lo = dot(jnp.concatenate(top, axis=0), g)
        hi = dot(jnp.concatenate(bottom, axis=0), g[half:])
        z[s, :half, cols] = jnp.where(lane_low, lo[:half], lo[half:])
        z[s, half:, cols] = jnp.where(lane_low, hi[:half], hi[half:])

    sent = []

    def wide(a_ref, b_ref, rows, cols):
        t = dot(a_ref[rows, 0:length], b_ref[0, :, cols])
        for s in range(1, seqs):
            t = t + dot(a_ref[rows, s * length : (s + 1) * length], b_ref[s, :, cols])
        return t

    def from_out(i):
        return lambda part, r0, n: wide(
            nrt, cot, pl.ds(pl.multiple_of(i * dm + r0, 16), n),
            pl.ds(pl.multiple_of(part * (dm // 2), LN), dm // 2),
        )

    def from_columns(ref, base, w):
        return lambda part, r0, n: wide(
            nt, ref, pl.ds(pl.multiple_of(r0, 16), n),
            pl.ds(pl.multiple_of(base + part * w, LN), w),
        )

    def group_steps(g, produce, out_ref, row0, col0, part_cols):
        sb, rb, rr, acc, rx = bufs[5 * g : 5 * g + 5]
        total, w = sb.shape
        kind = sb.dtype
        tile = min(192, total // 2)

        def place(off, n, part):
            if part_cols:
                return out_ref.at[
                    pl.ds(pl.multiple_of(row0 + off, 8), n),
                    pl.ds(pl.multiple_of(col0 + part * w, LN), w),
                ]
            return out_ref.at[pl.ds(pl.multiple_of(part * total + off, 8), n), :]

        def copy_of(i, src, dst, peer):
            copy = pltpu.make_async_remote_copy(
                src_ref=src, dst_ref=dst, send_sem=ar_s.at[g, i], recv_sem=ar_r.at[g, i],
                device_id=peer, device_id_type=MESH,
            )
            copy.start()
            sent.append(copy)
            return copy

        def rows_at(start, n):
            return pl.ds(pl.multiple_of(start, 8), n)

        def tiles(count, body):
            if count == 1:
                body(0)
            else:
                lax.fori_loop(0, count, lambda i, _: (body(i), 0)[1], 0)

        def give(i):
            sb[rows_at(i * tile, tile), :] = produce(1 - core, i * tile, tile).astype(kind)

        tiles(total // tile, give)
        copy = copy_of(0, sb, rb, core_peer)
        sent.pop()
        yield
        copy.wait()
        bit, peer = stages[0]
        n = total // 2

        def own(i, start):
            r0 = start + i * tile
            return produce(core, r0, tile) + rb[rows_at(r0, tile), :].astype(F32)

        def give_half(i):
            sb[rows_at(i * tile, tile), :] = own(i, (1 - bit) * n).astype(kind)

        def keep_half(i):
            acc[rows_at(i * tile, tile), :] = own(i, bit * n)

        tiles(n // tile, give_half)
        copy = copy_of(1, sb.at[pl.ds(0, n)], rr.at[pl.ds(0, n)], peer)
        tiles(n // tile, keep_half)
        first_copy = copy
        if extras:
            sent.pop()
        yield
        copy.wait_recv()
        off1 = bit * n
        bit, peer = stages[1]
        base, n = n, n // 2
        gone, kept = (1 - bit) * n, bit * n
        sb[base : base + n, :] = (
            acc[rows_at(gone, n), :] + rr[rows_at(gone, n), :].astype(F32)
        ).astype(kind)
        copy = copy_of(2, sb.at[pl.ds(base, n)], rr.at[pl.ds(base, n)], peer)
        acc[rows_at(kept, n), :] += rr[rows_at(kept, n), :].astype(F32)
        yield
        copy.wait_recv()
        off2 = off1 + kept
        first, base, n = base, base + n, n // 4
        copies = []
        for d in (2, 1, 3):
            at = lax.rem(in_row + d, 4) * n
            here = base + (d - 1) * n
            sb[here : here + n, :] = (
                acc[rows_at(kept + at, n), :] + rr[rows_at(first + at, n), :].astype(F32)
            ).astype(kind)
            copies.append(
                copy_of(
                    2 + d, sb.at[pl.ds(here, n)], rr.at[pl.ds(here, n)], row_peers[d - 1]
                )
            )
        yield
        at = in_row * n
        value = acc[rows_at(kept + at, n), :] + rr[rows_at(first + at, n), :].astype(F32)
        for copy in copies:
            copy.wait_recv()
        for d in range(3):
            value = value + rr[base + d * n : base + (d + 1) * n, :].astype(F32)
        if extras:
            first_copy.wait_send()
        for e, peer in enumerate(extras):
            mine = value.astype(kind)
            sb[e * n : (e + 1) * n, :] = mine
            copy = pltpu.make_async_remote_copy(
                src_ref=sb.at[pl.ds(e * n, n)], dst_ref=rx.at[e], send_sem=ex_s.at[g, e],
                recv_sem=ex_r.at[g, e], device_id=peer, device_id_type=MESH,
            )
            copy.start()
            copy.wait()
            value = mine.astype(F32) + rx[e].astype(F32)
        done = total - n
        sb[done:, :] = value.astype(kind)
        here = place(off2 + at, n, core)
        copies = [
            copy_of(5 + d, sb.at[pl.ds(done, n)], here, row_peers[d - 1]) for d in (2, 1, 3)
        ]
        local = pltpu.make_async_copy(sb.at[pl.ds(done, n)], here, loc_sem.at[g])
        local.start()
        yield
        for copy in copies:
            copy.wait_recv()
        local.wait()
        for i, off, n, peer in (
            (9, off2, total // 4, stages[1][1]),
            (10, off1, total // 2, stages[0][1]),
            (11, 0, total, core_peer),
        ):
            here = place(off, n, core)
            copy = copy_of(i, here, here, peer)
            yield
            copy.wait_recv()

    wide_w = dm // 2
    groups = [
        (0, from_out(0), go_h, 0, 0, True),
        (1, from_out(1), go_h, dm, 0, True),
        (2, from_columns(ggz, 0, wide_w), gw_h, 0, 0, True),
        (3, from_columns(ggz, dm, wide_w), gw_h, 0, dm, True),
        (4, from_columns(nrm, 0, wide_w), gm_h, 0, 0, True),
        (5, from_columns(nrm, dm, wide_w), gm_h, 0, dm, True),
        (6, from_columns(ggz, 0, LN), gm_h, 0, di, True),
        (7, lambda part, r0, n: sm[part, pl.ds(pl.multiple_of(r0, 8), n), :], sm_h, 0, 0, False),
    ]

    plan = list(PLAN)
    live = {}

    def service(last=False):
        todo = [g for part in plan for g in part] if last else plan.pop(0)
        for g in todo:
            if g not in live:
                live[g] = group_steps(*groups[g])
            next(live[g], None)

    for i in range(seqs * nblk // 2):
        s, b0 = (2 * i) // nblk, (2 * i) % nblk

        def backward_body(b, _, s=s):
            pair_backward(2 * b, s)
            pair_backward(2 * b + 1, s)
            backward_slot((seqs + s) * nblk + b)
            return 0

        service()
        lax.fori_loop(b0, b0 + 2, backward_body, 0)

    slot = 2 * seqs * nblk
    for s in range(seqs):
        for i in range(dm // BW):
            cols = slice(i * BW, (i + 1) * BW)
            pj = dot(nrm[s], wo[:, cols])
            res_r[s, :, cols] = (tok[s, :, cols].astype(F32) + pj).astype(BF)
            gn[s, :, cols] = dot_nt(ggz[s], wg[cols, :])
            backward_slot(slot)
            slot += 1
        service()
    res_copy = pltpu.make_async_copy(res_r, res_h, tok_sem.at[0])
    res_copy.start()
    slots_alone(backward_slot, slot, b_slots)

    ginf[...] = jnp.zeros_like(ginf)
    hs_d[...] = jnp.zeros_like(hs_d)
    hs_g[...] = jnp.zeros_like(hs_g)
    bdh[...] = jnp.zeros_like(bdh)

    def head_sum(v, x):
        hi, lo = split2(v)
        return dot_nt(hi, x) + dot_nt(lo, x)

    def head_sum3(v, x):
        hi, mid, lo = split3(v)
        return dot_nt(hi, x) + dot_nt(mid, x) + dot_nt(lo, x)

    def gh_copy(b):
        cols = ds(b * BW, BW)
        return pltpu.make_async_remote_copy(
            src_ref=big.at[:, pl.ds(0, 8), cols], dst_ref=big.at[:, pl.ds(length, 8), cols],
            send_sem=gh_s.at[b], recv_sem=gh_r.at[b], device_id=prv, device_id_type=MESH,
        )

    @pl.when(jnp.logical_not(has_next))
    def _():
        big[:, length : length + 8, :] = jnp.zeros((seqs, 8, xbc), F32)

    def finish_block(b, s, ga):
        cols = ds(b * BW, BW)
        f = fil[s, :, cols]
        sg = sigmoid(f)
        gf = ga * (sg * (1.0 + f * (1.0 - sg)))
        big[s, 0:length, cols] = gf
        return jnp.sum(gf, axis=0, keepdims=True)

    def last_body(b, _):
        cols = ds(b * BW, BW)
        cb_sum = jnp.zeros((1, BW), F32)
        sk_sum = jnp.zeros((1, BW), F32)
        x = xx[:, cols]
        for s in range(seqs):
            lt = in_b[s * nblk + b]
            pr = prior_of(s, b)
            f = fil[s, :, cols]
            sg = sigmoid(f)
            sig = f * sg
            stw = dot(pst[s], x)
            gst = dot(infl[s], lt) * dot(ptl[s], x)
            gd = z[s, :, cols]
            gyf = gy[s, :, cols].astype(F32)
            sk_row = skw[0:1, cols]
            gg = gst + gd
            ga = sk_row * gyf + stw * gg
            t1 = stw * sig * gst
            dd = gyf * (y[s, :, cols] - sk_row * sig) - drv[s, :, cols].astype(F32) * gd - t1
            hs_d[s] += head_sum(dd, x)
            hs_g[s] += head_sum(sig * gg, x)
            bd = jnp.sum(t1, axis=0, keepdims=True) + dlast[s, 7:8, cols] * jnp.sum(
                lt.astype(F32) * pr, axis=0, keepdims=True
            )
            bdh[s] += head_sum3(jnp.broadcast_to(bd, (8, BW)), x)
            sk_sum = sk_sum + jnp.sum(gyf * sig, axis=0, keepdims=True)
            ginf[s] += dot_nt(scl[s, :, cols], lt)
            gf = ga * (sg * (1.0 + f * (1.0 - sg)))
            big[s, 0:length, cols] = gf
            cb_sum = cb_sum + jnp.sum(gf, axis=0, keepdims=True)
        small_put(SM_CONVB, b, cb_sum)
        sk_row_r[0:1, cols] = sk_sum

        @pl.when(has_prev)
        def _():
            gh_copy(b).start()

        return 0

    for i in range(0, nblk, 2):
        lax.fori_loop(i, i + 2, last_body, 0)
        service()

    cb_sum = jnp.zeros((1, BW), F32)
    for s in range(seqs):
        gst_bf = gsc[s].astype(BF)
        gi = ginf[s] + dot(gst_bf, outf[s])
        go = gout[s] + dot(gst_bf.T, infl[s])
        cb_sum = cb_sum + finish_block(nblk, s, jnp.concatenate([gi, go], axis=1))
    small_put(SM_CONVB, nblk, cb_sum)

    @pl.when(has_prev)
    def _():
        gh_copy(nblk).start()

    row_i = lax.broadcasted_iota(jnp.int32, (length, LN), 0)
    glr = jnp.zeros((1, LN), F32)
    gsb = jnp.zeros((1, LN), F32)
    grl = []
    for s in range(seqs):
        gc = hs_d[s] + jnp.where(row_i == length - 1, bdh[s, 0:1], 0.0)
        terms = dot3(tri[1], gc)
        gst = hs_g[s] + terms * rates3
        glr = glr + jnp.sum(terms * st[s], axis=0, keepdims=True)
        graw = gst * sigmoid(sraw[s] + bias3)
        gsb = gsb + jnp.sum(graw, axis=0, keepdims=True)
        grl.append(jnp.where(lane128 < heads, graw, 0.0).astype(BF))
    sk_h = head_sum3(jnp.broadcast_to(sk_row_r[0:1, :], (8, di)), xx[...])
    small_one(SM_HEADS, gsb)
    small_one(SM_HEADS + 1, rates3 * glr)
    small_one(SM_HEADS + 2, sk_h[0:1])
    stepg = dot(grl[0].T, ne[0, hw:, :])
    for s in range(1, seqs):
        stepg = stepg + dot(grl[s].T, ne[s, hw:, :])
    for i in range(dm // LN):
        row = SM_STEP + 24 * i
        for lo, hi in ((row, min(row + 24, 128)), (max(row, 128), row + 24)):
            if lo < hi:
                sm[lo // 128, lo % 128 : lo % 128 + hi - lo, :] = stepg[
                    lo - row : hi - row, i * LN : (i + 1) * LN
                ]

    def mixed_body(b):
        cols = ds(b * BW, BW)

        @pl.when(has_next)
        def _():
            gh_copy(b).wait_recv()

        parts = []
        sums = [jnp.zeros((1, BW), F32) for _ in range(window + 1)]
        for s in range(seqs):
            gf = big[s, :, cols]
            rows = gf.shape[0]
            m = ext[s, :, cols].astype(F32)
            gm = jnp.zeros((length, BW), F32)
            for k in range(window + 1):
                shift = window - k
                moved = pltpu.roll(gf, rows - shift, 0) if shift else gf
                gm = gm + cw_r[k : k + 1, cols] * moved[:length]
                em = pltpu.roll(m, shift, 0) if shift else m
                sums[k] = sums[k] + jnp.sum(gf[:length] * em[hw:], axis=0, keepdims=True)
            gmb = gm.astype(BF)
            parts.append(gmb)
            gn[s] += dot_nt(gmb, wm[:, cols])
        for k in range(window + 1):
            small_put(SM_CONVW + k * (xbc // LN), b, sums[k])
        return parts

    def mixed_loop(b, _):
        cols = ds(b * BW, BW)
        for s, part in enumerate(mixed_body(b)):
            nrm[s, :, cols] = part
        return 0

    service()
    lax.fori_loop(0, 3, mixed_loop, 0)
    service()
    lax.fori_loop(3, 6, mixed_loop, 0)
    service()
    for s, part in enumerate(mixed_body(6)):
        ggz[s, :, 0:BW] = part
    service()
    for s in range(seqs):
        gn[s] += dot_nt(grl[s], ws3)
    service()

    @pl.when(has_next)
    def _():
        halo_copy.wait_send()

    def token_body(i, sums):
        for s in range(seqs):
            rows = ds(i * 16, 16)
            v = tok[s, rows, :].astype(F32)
            inv = lax.rsqrt(jnp.mean(v * v, axis=-1, keepdims=True) + EPSILON)
            unit = v * inv
            gr = gn[s, rows, :]
            sums = sums + jnp.sum(gr * unit, axis=0, keepdims=True)
            q = gr * gain
            back = inv * (q - unit * jnp.mean(q * unit, axis=-1, keepdims=True))
            tok[s, rows, :] = (cot[s, rows, :].astype(F32) + back).astype(BF)
        return sums

    n_sum = lax.fori_loop(0, length // 16, token_body, jnp.zeros((1, dm), F32))
    for i in range(dm // LN):
        small_one(SM_NORM + i, n_sum[:, i * LN : (i + 1) * LN])
    tg_copy = pltpu.make_async_copy(tok, tg_h, tok_sem.at[1])
    tg_copy.start()
    service(last=True)
    res_copy.wait()
    tg_copy.wait()
    for copy in sent:
        copy.wait_send()

    def drain(q, _):
        @pl.when(has_prev)
        def _():
            backward_copy(q).wait_send()

        return 0

    lax.fori_loop(0, seqs * nblk, drain, 0)

    def drain_halo(b, _):
        @pl.when(has_prev)
        def _():
            gh_copy(b).wait_send()

        return 0

    lax.fori_loop(0, xbc // BW, drain_halo, 0)


def on_device(nctx, *args):
    tokens, norm_gain, wg, wm, ws, conv_w, conv_b, sb, lr, sk, gg, wo, cot = args
    seqs, length, dm = tokens.shape
    di = wg.shape[1]
    xbc = wm.shape[1]
    heads = ws.shape[1]
    nst = (xbc - di) // 2
    nchunk = di // LN
    nblk = di // BW
    hw = 16
    vm = pltpu.VMEM
    any_spec = pl.BlockSpec(memory_space=pl.ANY)
    vm_spec = pl.BlockSpec(memory_space=vm)
    dma = pltpu.SemaphoreType.DMA
    extras = max(1, (nctx // 16).bit_length())
    bufs = []
    for rows, w, kind in [(dm, dm // 2, BF)] * 6 + [(dm, LN, BF), (128, LN, F32)]:
        bufs += [vm((rows, w), kind)] * 3 + [vm((rows // 2, w), F32)]
        bufs += [vm((extras, rows // 16, w), kind) if nctx > 8 else vm((1, 16, LN), kind)]
    out = pl.pallas_call(
        functools.partial(layer_kernel, nctx),
        out_shape=(
            jax.ShapeDtypeStruct(tokens.shape, BF),
            jax.ShapeDtypeStruct(tokens.shape, BF),
            jax.ShapeDtypeStruct((di, dm), BF),
            jax.ShapeDtypeStruct((dm, di), BF),
            jax.ShapeDtypeStruct((dm, xbc), BF),
            jax.ShapeDtypeStruct((256, LN), F32),
        ),
        in_specs=[any_spec, vm_spec, any_spec, any_spec] + [vm_spec] * 7 + [any_spec] * 2,
        out_specs=(any_spec,) * 6,
        scratch_shapes=[
            vm((seqs, length, dm), BF),
            vm((seqs, length, dm), BF),
            vm((dm, di), BF),
            vm((dm, xbc), BF),
            vm((di, dm), BF),
            vm((seqs, hw, dm), BF),
            vm((seqs, hw + length, dm), BF),
            vm((dm, seqs * length), BF),
            vm((seqs, hw + length, xbc), BF),
            vm((seqs, length, xbc), F32),
            vm((seqs, length, di), BF),
            vm((seqs, length, di), BF),
            vm((seqs, length, di), F32),
            vm((seqs, length, di), F32),
            vm((seqs, length + 8, xbc), F32),
            vm((seqs, length, di), BF),
            vm((seqs, length, di), BF),
            vm((seqs, length, di), BF),
            vm((di, seqs * length), BF),
            vm((seqs, length, LN), F32),
            vm((seqs, length, LN), F32),
            vm((seqs, length, dm), F32),
            vm((seqs * nchunk, nst, LN), F32),
            vm((seqs * nchunk, nst, LN), F32),
            vm((seqs * nblk, nst, BW), BF),
            vm((seqs * nblk, nst, BW), BF),
            vm((seqs, length, LN), F32),
            vm((seqs, length, LN), F32),
            vm((seqs, length, LN), F32),
            vm((seqs, LN, length), F32),
            vm((seqs, length, LN), BF),
            vm((seqs, length, LN), BF),
            vm((seqs, length, LN), BF),
            vm((seqs, 8, di), F32),
            vm((seqs, length, nst), BF),
            vm((seqs, length, nst), BF),
            vm((seqs, nst, length), BF),
            vm((seqs, nst, length), BF),
            vm((seqs, length, length), F32),
            vm((seqs, length, length), F32),
            vm((LN, di), BF),
            vm((2, length, length), BF),
            vm((seqs, length, LN), F32),
            vm((seqs, length, LN), F32),
            vm((seqs, 8, LN), F32),
            vm((seqs, length, dm), BF),
            dma((2,)),
            vm((8, di), F32),
            vm((2, 128, LN), F32),
            vm((8, di), F32),
            bufs,
            dma((8, 12)), dma((8, 12)), dma((8,)), dma((8, extras)), dma((8, extras)),
            dma((5,)), dma, dma,
            dma((seqs * nchunk,)), dma((seqs * nchunk,)), dma((seqs * nblk,)), dma((seqs * nblk,)),
            dma((xbc // BW,)), dma((xbc // BW,)),
        ],
        compiler_params=pltpu.CompilerParams(
            collective_id=0, has_side_effects=True, vmem_limit_bytes=65200 * 1024
        ),
    )(*args)
    res, tg, g_out, g_gate, g_mixer, small = out
    gate0 = xbc // LN
    norm0 = gate0 + di // LN
    convw0 = norm0 + dm // LN
    taps = conv_w.shape[0]
    heads0 = convw0 + taps * (xbc // LN)
    step0 = -(-(heads0 + 3) // 8) * 8
    step = small[step0 : step0 + heads * (dm // LN)].reshape(dm // LN, heads, LN)
    return (
        res, tg, small[norm0:convw0].reshape(dm), g_gate.astype(F32), g_mixer.astype(F32),
        step.transpose(0, 2, 1).reshape(dm, heads),
        small[convw0:heads0].reshape(taps, xbc), small[:gate0].reshape(xbc),
        small[heads0, :heads], small[heads0 + 1, :heads], small[heads0 + 2, :heads],
        small[gate0:norm0].reshape(di), g_out.astype(F32),
    )


def solution(mesh):
    tok = P("seq", "ctx", None)
    return jax.shard_map(
        functools.partial(on_device, mesh.shape["ctx"]),
        mesh=mesh,
        in_specs=(tok,) + (P(),) * 11 + (tok,),
        out_specs=(tok, tok) + (P(),) * 11,
        check_vma=False,
    )
```

```python
import functools

import jax
import jax.numpy as jnp
from jax import lax
from jax.experimental import pallas as pl
from jax.experimental.pallas import tpu as pltpu
from jax.sharding import PartitionSpec as P

MESH = pl.DeviceIdType.MESH
BF = jnp.bfloat16
F32 = jnp.float32
EPSILON = 1e-05
BW = 256
LN = 128
SKEW = 2
PLAN = (
    (1, 0, 2, 1, 0, 2, 3),
    (),
    (1, 3),
    (0,),
    (),
    (),
    (2, 1),
    (3, 0),
    (4, 1, 3, 2, 4, 0),
    (1,),
    (4, 5, 1, 3),
    (6, 5, 4, 2, 6, 0),
    (1,),
    (),
    (3, 1),
    (5, 6),
    (4, 0),
    (2, 7, 6, 7, 5, 4, 7, 2, 0, 3, 7, 0, 6, 5, 4, 6, 7, 3, 7, 5, 4, 4, 7, 6, 5, 2, 2, 6, 6,
    7, 7, 3, 5, 5),
)


def dot(a, b):
    return jnp.dot(a, b, preferred_element_type=F32)


def dot_nt(a, b):
    return lax.dot_general(a, b, (((1,), (1,)), ((), ())), preferred_element_type=F32)


def split2(v):
    hi = v.astype(BF)
    return hi, (v - hi.astype(F32)).astype(BF)


def split3(v):
    hi = v.astype(BF)
    rest = v - hi.astype(F32)
    mid = rest.astype(BF)
    return hi, mid, (rest - mid.astype(F32)).astype(BF)


def dot3(a, v):
    hi, mid, lo = split3(v)
    return dot(a, hi) + dot(a, mid) + dot(a, lo)


def pieces3(v):
    lane = lax.broadcasted_iota(jnp.int32, v.shape, 1)
    hi, mid, lo = split3(v)
    z = jnp.zeros_like(v)
    return jnp.where(
        lane < 32,
        hi.astype(F32),
        jnp.where(lane < 64, mid.astype(F32), jnp.where(lane < 96, lo.astype(F32), z)),
    ).astype(BF)


def sigmoid(v):
    return 1.0 / (1.0 + jnp.exp(-v))


def ds(start, size):
    return pl.ds(pl.multiple_of(start, size), size)


def layer_kernel(
    nctx,
    tok_h, ng_r, wg_h, wm_h, ws_r, cw_r, cb_r, sb_r, lr_r, sk_r, gg_r, wo_h, cot_h,
    res_h, tg_h, go_h, gw_h, gm_h, sm_h,
    tok, cot, wg, wm, wo, halo, ne, nt, ext, fil, drv, scl, y, z, big, gy, ggz, nrm, nrt,
    acc_a, acc_b, gn, sum_s, in_f, out_b, in_b, sraw, st, cum, cum_t, pst, ptl, pdc,
    dlast, infl, outf, inf_t, outf_t, sco, sco_t, xx, tri, hs_d, hs_g, bdh,
    res_r, tok_sem, skw, sm, sk_row_r, bufs, ar_s, ar_r, loc_sem, ex_s, ex_r,
    in_sem, halo_s, halo_r, fs_s, fs_r, bs_s, bs_r, gh_s, gh_r,
):
    seqs, length, dm = tok.shape
    di = wg.shape[1]
    xbc = wm.shape[1]
    heads = ws_r.shape[0]
    hp = di // heads
    nst = (xbc - di) // 2
    window = cw_r.shape[0] - 1
    nblk = di // BW
    gsc, gout, ginf = sco, acc_a, acc_b
    nchunk = di // LN
    hw = 16
    seq = lax.axis_index("seq")
    ctx = lax.axis_index("ctx")
    has_prev = ctx > 0
    has_next = ctx < nctx - 1
    prv = (seq, ctx - 1)
    nxt = (seq, ctx + 1)

    barrier = pltpu.get_barrier_semaphore()

    @pl.when(has_prev)
    def _():
        pl.semaphore_signal(barrier, inc=1, device_id=prv, device_id_type=MESH)

    @pl.when(has_next)
    def _():
        pl.semaphore_signal(barrier, inc=1, device_id=nxt, device_id_type=MESH)

    loads = [
        pltpu.make_async_copy(a, b, in_sem.at[i])
        for i, (a, b) in enumerate(
            ((tok_h, tok), (wm_h, wm), (cot_h, cot), (wo_h, wo), (wg_h, wg))
        )
    ]
    for copy in loads[:2]:
        copy.start()

    core = lax.rem(ctx, 2)

    def flipped(index, mask):
        bit = lax.rem(index // mask, 2)
        return bit, index + mask - 2 * mask * bit

    core_peer = (seq, flipped(ctx, 1)[1])
    stages = []
    for mask in (1 + core, 2 - core):
        bit, other = flipped(seq, mask)
        stages.append((bit, (other, ctx)))
    in_row = lax.rem(ctx // 2, 4)
    row_peers = [(seq, ctx + 2 * (lax.rem(in_row + d, 4) - in_row)) for d in (1, 2, 3)]
    extras = []
    mask = 8
    while mask < nctx:
        extras.append((seq, flipped(ctx, mask)[1]))
        mask *= 2
    peers = [peer for _, peer in stages] + row_peers + extras
    for peer in peers:
        pl.semaphore_signal(barrier, inc=1, device_id=peer, device_id_type=MESH)
    lane128 = lax.broadcasted_iota(jnp.int32, (1, LN), 1)
    r_i = lax.broadcasted_iota(jnp.int32, (LN, di), 0)
    c_i = lax.broadcasted_iota(jnp.int32, (LN, di), 1)
    first = jnp.bitwise_and(r_i, 31) * hp
    xx[...] = jnp.where((c_i >= first) & (c_i < first + hp) & (r_i < 96), 1.0, 0.0).astype(BF)
    t_r = lax.broadcasted_iota(jnp.int32, (length, length), 0)
    t_c = lax.broadcasted_iota(jnp.int32, (length, length), 1)
    tri[0] = jnp.where(t_r >= t_c, 1.0, 0.0).astype(BF)
    tri[1] = jnp.where(t_r <= t_c, 1.0, 0.0).astype(BF)
    k_i = lax.broadcasted_iota(jnp.int32, (heads, LN), 0)
    l_i = lax.broadcasted_iota(jnp.int32, (heads, LN), 1)
    rep = jnp.where((l_i % 32 == k_i) & (l_i < 96), 1.0, 0.0)

    def replicated(row_ref):
        row = jnp.broadcast_to(row_ref[...].reshape(1, heads), (8, heads))
        hi, mid, lo = split3(row)
        r = rep.astype(BF)
        return (dot(hi, r) + dot(mid, r) + dot(lo, r))[0:1]

    ws3 = dot(ws_r[...].T, rep.astype(BF)).astype(BF)
    bias3 = replicated(sb_r)
    rates3 = -jnp.exp(replicated(lr_r))
    sk8 = jnp.broadcast_to(replicated(sk_r), (8, LN))
    skw[...] = dot(pieces3(sk8), xx[...])

    pl.semaphore_wait(
        barrier, has_prev.astype(jnp.int32) + has_next.astype(jnp.int32) + len(peers)
    )
    loads[0].wait()
    for copy in loads[2:]:
        copy.start()

    halo_copy = pltpu.make_async_remote_copy(
        src_ref=tok.at[:, pl.ds(length - hw, hw), :], dst_ref=halo, send_sem=halo_s,
        recv_sem=halo_r, device_id=nxt, device_id_type=MESH,
    )

    @pl.when(has_next)
    def _():
        halo_copy.start()

    @pl.when(jnp.logical_not(has_prev))
    def _():
        halo[...] = jnp.zeros_like(halo)
        in_f[...] = jnp.zeros_like(in_f)

    @pl.when(jnp.logical_not(has_next))
    def _():
        in_b[...] = jnp.zeros_like(in_b)

    gain = ng_r[...].reshape(1, dm)

    def norm_rows(rows):
        v = rows.astype(F32)
        inv = lax.rsqrt(jnp.mean(v * v, axis=-1, keepdims=True) + EPSILON)
        return ((v * inv) * gain).astype(BF)

    for s in range(seqs):

        def norm_body(i, _, s=s):
            ne[s, ds(hw + i * 16, 16), :] = norm_rows(tok[s, ds(i * 16, 16), :])
            return 0

        lax.fori_loop(0, length // 16, norm_body, 0, unroll=2)

    for s in range(seqs):
        raw = dot(ne[s, pl.ds(hw, length), :], ws3)
        sraw[s] = raw
        step = jax.nn.softplus(raw + bias3)
        st[s] = step
        cu = dot3(tri[0], step * rates3)
        cum[s] = cu
        cum_t[s] = cu.T
        last = cu[length - 1 : length]
        pst[s] = pieces3(step)
        ptl[s] = pieces3(jnp.exp(last - cu))
        dec = jnp.exp(cu)
        pdc[s] = pieces3(dec)
        dlast[s] = dot(pieces3(dec[length - 8 :]), xx[...])

    for s in range(seqs):
        for b in range(dm // BW):
            nt[b * BW : (b + 1) * BW, s * length : (s + 1) * length] = ne[
                s, hw : hw + length, b * BW : (b + 1) * BW
            ].T

    @pl.when(has_prev)
    def _():
        halo_copy.wait_recv()

    for s in range(seqs):
        ne[s, 0:hw, :] = norm_rows(halo[s])

    loads[1].wait()

    def filter_block(b, s):
        cols = ds(b * BW, BW)
        m_bf = dot(ne[s], wm[:, cols]).astype(BF)
        m = m_bf.astype(F32)
        f = cb_r[cols].reshape(1, BW)
        for k in range(window + 1):
            shift = window - k
            moved = pltpu.roll(m, shift, 0) if shift else m
            f = f + cw_r[k : k + 1, cols] * moved[hw:]
        return cols, m_bf, f

    for s in range(seqs):
        cols, m_bf, f = filter_block(nblk, s)
        ext[s, :, cols] = m_bf
        fil[s, :, cols] = f
        act = f * sigmoid(f)
        i_bf = act[:, :nst].astype(BF)
        o_bf = act[:, nst:].astype(BF)
        infl[s] = i_bf
        outf[s] = o_bf
        inf_t[s] = i_bf.T
        outf_t[s] = o_bf.T
        sco[s] = dot_nt(o_bf, i_bf)
        sco_t[s] = dot_nt(i_bf, o_bf)

    def forward_copy(q):
        return pltpu.make_async_remote_copy(
            src_ref=sum_s.at[q], dst_ref=in_f.at[q], send_sem=fs_s.at[q],
            recv_sem=fs_r.at[q], device_id=nxt, device_id_type=MESH,
        )

    def backward_copy(q):
        return pltpu.make_async_remote_copy(
            src_ref=out_b.at[q], dst_ref=in_b.at[q], send_sem=bs_s.at[q],
            recv_sem=bs_r.at[q], device_id=prv, device_id_type=MESH,
        )

    f_skew = SKEW * ctx
    b_skew = SKEW * (nctx - 1 - ctx)
    f_slots = seqs * nchunk + SKEW * (nctx - 1)
    b_slots = seqs * nblk + SKEW * (nctx - 1)

    def forward_slot(slot):
        q = slot - f_skew

        @pl.when((q >= 0) & (q < seqs * nchunk))
        def _():
            @pl.when(has_prev)
            def _():
                forward_copy(q).wait_recv()

            @pl.when(has_next)
            def _():
                row = dlast[q // nchunk, 7:8, ds(lax.rem(q, nchunk) * LN, LN)]
                sum_s[q] = row * in_f[q] + sum_s[q]
                forward_copy(q).start()

    def backward_slot(slot):
        q = slot - b_skew

        @pl.when((q >= 0) & (q < seqs * nblk))
        def _():
            @pl.when(has_next)
            def _():
                backward_copy(q).wait_recv()

            @pl.when(has_prev)
            def _():
                row = dlast[q // nblk, 7:8, ds(lax.rem(q, nblk) * BW, BW)]
                add = jnp.concatenate([sum_s[2 * q], sum_s[2 * q + 1]], axis=1)
                out_b[q] = (row * in_b[q].astype(F32) + add).astype(BF)
                backward_copy(q).start()

    def slots_alone(one, first, last):
        lax.fori_loop(first, last, lambda t, _: (one(t), 0)[1], 0)

    for s in range(seqs):

        def signal_body(i, _, s=s):
            made = []
            for b in (2 * i, 2 * i + 1):
                cols, m_bf, f = filter_block(b, s)
                sig = f * sigmoid(f)
                x = xx[:, cols]
                dr = sig * dot(pst[s], x)
                sc = (dr * dot(ptl[s], x)).astype(BF)
                made.append(
                    (b, cols, m_bf, f, skw[0:1, cols] * sig, dr.astype(BF), sc, dot(inf_t[s], sc))
                )
            for b, cols, m_bf, f, sk_sig, dr, sc, summ in made:
                ext[s, :, cols] = m_bf
                fil[s, :, cols] = f
                y[s, :, cols] = sk_sig
                drv[s, :, cols] = dr
                scl[s, :, cols] = sc
                sum_s[s * nchunk + 2 * b] = summ[:, :LN]
                sum_s[s * nchunk + 2 * b + 1] = summ[:, LN:]
            for slot in (2 * i, 2 * i + 1):
                forward_slot(s * nblk + slot)
            return 0

        lax.fori_loop(0, nblk // 2, signal_body, 0)

    SM_CONVB = 0
    SM_GATE = SM_CONVB + xbc // LN
    SM_NORM = SM_GATE + di // LN
    SM_CONVW = SM_NORM + dm // LN
    SM_HEADS = SM_CONVW + (window + 1) * (xbc // LN)
    SM_STEP = -(-(SM_HEADS + 3) // 8) * 8
    sm[...] = jnp.zeros_like(sm)

    def small_one(row, value):
        sm[row // 128, pl.ds(row % 128, 1), :] = value

    def small_put(base, b, value):
        small_one(base + 2 * b, value[:, :LN])
        small_one(base + 2 * b + 1, value[:, LN:])

    half = length // 2
    d_r = lax.broadcasted_iota(jnp.int32, (half, half), 0)
    d_c = lax.broadcasted_iota(jnp.int32, (half, half), 1)
    NEG = -1e30

    def columns_of(s, j):
        moved = pltpu.roll(cum[s], lax.rem(LN - 2 * j, LN), 1)
        return moved[:, 0:1], moved[:, 1:2]

    def pair_forward(j, s):
        cols = ds(j * LN, LN)
        d = drv[s, :, cols]
        lane_low = lane128 < hp
        top, bottom = [], []
        for hh, col in enumerate(columns_of(s, j)):
            row = cum_t[s, pl.ds(2 * j + hh, 1), :]
            fa = jnp.exp(jnp.where(d_r >= d_c, col[:half] - row[:, :half], NEG))
            fb = jnp.exp(col[half:] - row[:, :half])
            fc = jnp.exp(jnp.where(d_r >= d_c, col[half:] - row[:, half:], NEG))
            top.append((sco[s, :half, :half] * fa).astype(BF))
            bottom.append(
                jnp.concatenate(
                    [
                        (sco[s, half:, :half] * fb).astype(BF),
                        (sco[s, half:, half:] * fc).astype(BF),
                    ],
                    axis=1,
                )
            )
        lo = dot(jnp.concatenate(top, axis=0), d[:half])
        hi = dot(jnp.concatenate(bottom, axis=0), d)
        return (
            y[s, :half, cols] + jnp.where(lane_low, lo[:half], lo[half:]),
            y[s, half:, cols] + jnp.where(lane_low, hi[:half], hi[half:]),
        )

    loads[2].wait()
    loads[3].wait()
    loads[4].wait()

    for s in range(seqs):

        def forward_body(i, _, s=s):
            made = []
            for b in (2 * i, 2 * i + 1):
                cols = ds(b * BW, BW)
                made.append(
                    (
                        b, cols, dot_nt(cot[s], wo[cols, :]),
                        dot(ne[s, hw : hw + length, :], wg[:, cols]),
                        [pair_forward(2 * b + h, s) for h in range(2)],
                    )
                )
            for b, cols, g, zz, pairs in made:
                big[s, 0:length, cols] = g
                z[s, :, cols] = zz
                for h, (lo, hi) in enumerate(pairs):
                    lanes = ds((2 * b + h) * LN, LN)
                    y[s, :half, lanes] = lo
                    y[s, half:, lanes] = hi
            for slot in (2 * i, 2 * i + 1):
                forward_slot((seqs + s) * nblk + slot)
            return 0

        lax.fori_loop(0, nblk // 2, forward_body, 0)

    acc_a[...] = jnp.zeros_like(acc_a)
    acc_b[...] = jnp.zeros_like(acc_b)

    def prior_of(s, b):
        return jnp.concatenate(
            [in_f[s * nchunk + 2 * b], in_f[s * nchunk + 2 * b + 1]], axis=1
        )

    def gate_blocks(blocks, s):
        made = []
        a_sum = c_sum = None
        for b in blocks:
            cols = ds(b * BW, BW)
            phi, plo = split2(prior_of(s, b))
            out = (dot(outf[s], phi) + dot(outf[s], plo)) * dot(pdc[s], xx[:, cols])
            yy = y[s, :, cols] + out
            zz = z[s, :, cols]
            gated = yy * (zz * sigmoid(zz))
            q = big[s, 0:length, cols] * gg_r[cols].reshape(1, BW)
            a = gated * gated
            c = q * gated
            a, c = a[:, :LN] + a[:, LN:], c[:, :LN] + c[:, LN:]
            a_sum, c_sum = (a, c) if a_sum is None else (a_sum + a, c_sum + c)
            made.append((cols, yy))
        for cols, yy in made:
            y[s, :, cols] = yy
        acc_a[s] += a_sum
        acc_b[s] += c_sum

    def grad_blocks(blocks, s, iv, mean):
        made = []
        g_out = None
        for b in blocks:
            cols = ds(b * BW, BW)
            yy = y[s, :, cols]
            zz = z[s, :, cols]
            sg = sigmoid(zz)
            act = zz * sg
            unit = (yy * act) * iv
            gain_row = gg_r[cols].reshape(1, BW)
            g = big[s, 0:length, cols]
            no = (unit * gain_row).astype(BF)
            gain_sum = jnp.sum(g * unit, axis=0, keepdims=True)
            gr = iv * (g * gain_row - unit * mean)
            gyb = (gr * act).astype(BF)
            gzb = (gr * yy * (sg * (1.0 + zz * (1.0 - sg)))).astype(BF)
            w = gyb.astype(F32) * dot(pdc[s], xx[:, cols])
            whi, wlo = split2(w)
            gp = dot(outf_t[s], whi) + dot(outf_t[s], wlo)
            phi, plo = split2(prior_of(s, b))
            go = dot_nt(whi, phi) + (dot_nt(wlo, phi) + dot_nt(whi, plo))
            g_out = go if g_out is None else g_out + go
            made.append((b, cols, no, no.T, gain_sum, gyb, gzb, gp))
        for b, cols, no, no_t, gain_sum, gyb, gzb, gp in made:
            nrm[s, :, cols] = no
            nrt[cols, s * length : (s + 1) * length] = no_t
            sk_row_r[1 + s : 2 + s, cols] = gain_sum
            gy[s, :, cols] = gyb
            ggz[s, :, cols] = gzb
            sum_s[s * nchunk + 2 * b] = gp[:, :LN]
            sum_s[s * nchunk + 2 * b + 1] = gp[:, LN:]
        gout[s] += g_out

    first_done = f_slots - nchunk * (seqs - 1)
    slots_alone(forward_slot, seqs * nchunk, first_done)
    for s in range(seqs):
        slot0 = first_done + s * nchunk

        def passing(i, s=s, slot0=slot0):
            if s < seqs - 1:
                forward_slot(slot0 + i)
            else:
                backward_slot(i)

        def gate_body(i, _, s=s, passing=passing):
            gate_blocks((2 * i, 2 * i + 1), s)
            passing(2 * i)
            passing(2 * i + 1)
            return 0

        lax.fori_loop(0, nblk // 2, gate_body, 0)
        iv = lax.rsqrt(jnp.sum(acc_a[s], axis=-1, keepdims=True) / di + EPSILON)
        mean = iv * jnp.sum(acc_b[s], axis=-1, keepdims=True) / di
        gout[s] = jnp.zeros_like(gout[s])

        def sent_forward(c, _, s=s):
            @pl.when(has_next)
            def _():
                forward_copy(s * nchunk + c).wait_send()

            return 0

        lax.fori_loop(0, nchunk, sent_forward, 0)

        def grad_body(i, _, s=s, iv=iv, mean=mean, passing=passing):
            grad_blocks((2 * i, 2 * i + 1), s, iv, mean)
            passing(nblk + 2 * i)
            passing(nblk + 2 * i + 1)
            return 0

        lax.fori_loop(0, nblk // 2, grad_body, 0)

    def gate_gain_body(b, _):
        cols = ds(b * BW, BW)
        total = sk_row_r[1:2, cols]
        for s in range(1, seqs):
            total = total + sk_row_r[1 + s : 2 + s, cols]
        small_put(SM_GATE, b, total)
        return 0

    lax.fori_loop(0, nblk, gate_gain_body, 0)

    gsc[...] = jnp.zeros_like(gsc)

    def pair_backward(j, s):
        cols = ds(j * LN, LN)
        d = drv[s, :, cols]
        g = gy[s, :, cols]
        lane_low = lane128 < hp
        zero = jnp.zeros_like(d)
        top, bottom = [], []
        t1 = t2 = t3 = None
        for hh, col in enumerate(columns_of(s, j)):
            row = cum_t[s, pl.ds(2 * j + hh, 1), :]
            dh = jnp.where(lane_low if hh == 0 else jnp.logical_not(lane_low), d, zero)
            m1 = dot_nt(dh[:half], g)
            m2 = dot_nt(dh[half:], g[half:])
            fa = jnp.exp(jnp.where(d_r <= d_c, row[:, :half] - col[:half], NEG))
            fb = jnp.exp(row[:, half:] - col[:half])
            fc = jnp.exp(jnp.where(d_r <= d_c, row[:, half:] - col[half:], NEG))
            top.append(
                jnp.concatenate(
                    [
                        (sco_t[s, :half, :half] * fa).astype(BF),
                        (sco_t[s, :half, half:] * fb).astype(BF),
                    ],
                    axis=1,
                )
            )
            bottom.append((sco_t[s, half:, half:] * fc).astype(BF))
            p1, p2, p3 = m1[:, :half] * fa, m1[:, half:] * fb, m2 * fc
            t1, t2, t3 = (p1, p2, p3) if hh == 0 else (t1 + p1, t2 + p2, t3 + p3)
        lo = dot(jnp.concatenate(top, axis=0), g)
        hi = dot(jnp.concatenate(bottom, axis=0), g[half:])
        return (
            cols, (t1, t2, t3), jnp.where(lane_low, lo[:half], lo[half:]),
            jnp.where(lane_low, hi[:half], hi[half:]),
        )

    sent = []

    def wide(a_ref, b_ref, rows, cols):
        t = dot(a_ref[rows, 0:length], b_ref[0, :, cols])
        for s in range(1, seqs):
            t = t + dot(a_ref[rows, s * length : (s + 1) * length], b_ref[s, :, cols])
        return t

    def from_out(i):
        return lambda part, r0, n: wide(
            nrt, cot, pl.ds(pl.multiple_of(i * dm + r0, 16), n),
            pl.ds(pl.multiple_of(part * (dm // 2), LN), dm // 2),
        )

    def from_columns(ref, base, w):
        return lambda part, r0, n: wide(
            nt, ref, pl.ds(pl.multiple_of(r0, 16), n),
            pl.ds(pl.multiple_of(base + part * w, LN), w),
        )

    def group_steps(g, produce, out_ref, row0, col0, part_cols):
        sb, rb, rr, acc, rx = bufs[5 * g : 5 * g + 5]
        total, w = sb.shape
        kind = sb.dtype
        tile = min(384, total // 2)

        def place(part):
            if part_cols:
                return out_ref.at[
                    pl.ds(row0, total), pl.ds(pl.multiple_of(col0 + part * w, LN), w)
                ]
            return out_ref.at[pl.ds(pl.multiple_of(part * total, 8), total), :]

        def copy_of(i, src, dst, peer):
            copy = pltpu.make_async_remote_copy(
                src_ref=src, dst_ref=dst, send_sem=ar_s.at[g, i], recv_sem=ar_r.at[g, i],
                device_id=peer, device_id_type=MESH,
            )
            copy.start()
            sent.append(copy)
            return copy

        def rows_at(start, n):
            return pl.ds(pl.multiple_of(start, 8), n)

        def tiles(count, body):
            if count == 1:
                body(0)
            else:
                lax.fori_loop(0, count, lambda i, _: (body(i), 0)[1], 0)

        def give(i):
            sb[rows_at(i * tile, tile), :] = produce(1 - core, i * tile, tile).astype(kind)

        tiles(total // tile, give)
        copy = copy_of(0, sb, rb, core_peer)
        sent.pop()
        yield
        copy.wait()
        bit, peer = stages[0]
        n = total // 2

        def own(i, start):
            r0 = start + i * tile
            return produce(core, r0, tile) + rb[rows_at(r0, tile), :].astype(F32)

        def give_half(i):
            sb[rows_at(i * tile, tile), :] = own(i, (1 - bit) * n).astype(kind)

        def keep_half(i):
            acc[rows_at(i * tile, tile), :] = own(i, bit * n)

        tiles(n // tile, give_half)
        copy = copy_of(1, sb.at[pl.ds(0, n)], rr.at[pl.ds(0, n)], peer)
        tiles(n // tile, keep_half)
        first_copy = copy
        if extras:
            sent.pop()
        yield
        copy.wait_recv()
        off1 = bit * n
        bit, peer = stages[1]
        base, n = n, n // 2
        gone, kept = (1 - bit) * n, bit * n
        sb[base : base + n, :] = (
            acc[rows_at(gone, n), :] + rr[rows_at(gone, n), :].astype(F32)
        ).astype(kind)
        copy = copy_of(2, sb.at[pl.ds(base, n)], rr.at[pl.ds(base, n)], peer)
        acc[rows_at(kept, n), :] += rr[rows_at(kept, n), :].astype(F32)
        yield
        copy.wait_recv()
        off2 = off1 + kept
        first, base, n = base, base + n, n // 4
        copies = []
        for d in (2, 1, 3):
            at = lax.rem(in_row + d, 4) * n
            here = base + (d - 1) * n
            sb[here : here + n, :] = (
                acc[rows_at(kept + at, n), :] + rr[rows_at(first + at, n), :].astype(F32)
            ).astype(kind)
            copies.append(
                copy_of(
                    2 + d, sb.at[pl.ds(here, n)], rr.at[pl.ds(here, n)], row_peers[d - 1]
                )
            )
        yield
        at = in_row * n
        value = acc[rows_at(kept + at, n), :] + rr[rows_at(first + at, n), :].astype(F32)
        for copy in copies:
            copy.wait_recv()
        for d in range(3):
            value = value + rr[base + d * n : base + (d + 1) * n, :].astype(F32)
        if extras:
            first_copy.wait_send()
        for e, peer in enumerate(extras):
            mine = value.astype(kind)
            sb[e * n : (e + 1) * n, :] = mine
            copy = pltpu.make_async_remote_copy(
                src_ref=sb.at[pl.ds(e * n, n)], dst_ref=rx.at[e], send_sem=ex_s.at[g, e],
                recv_sem=ex_r.at[g, e], device_id=peer, device_id_type=MESH,
            )
            copy.start()
            copy.wait()
            value = mine.astype(F32) + rx[e].astype(F32)
        mine = rows_at(off2 + at, n)
        rb[mine, :] = value.astype(kind)
        copies = [
            copy_of(5 + d, rb.at[mine], rb.at[mine], row_peers[d - 1]) for d in (2, 1, 3)
        ]
        yield
        for copy in copies:
            copy.wait_recv()
        for i, off, n, peer in (
            (9, off2, total // 4, stages[1][1]),
            (10, off1, total // 2, stages[0][1]),
        ):
            here = rb.at[rows_at(off, n)]
            copy = copy_of(i, here, here, peer)
            yield
            copy.wait_recv()
        here = place(core)
        copy = copy_of(11, rb, here, core_peer)
        local = pltpu.make_async_copy(rb, here, loc_sem.at[g])
        local.start()
        yield
        copy.wait_recv()
        local.wait()

    wide_w = dm // 2
    groups = [
        (0, from_out(0), go_h, 0, 0, True),
        (1, from_out(1), go_h, dm, 0, True),
        (2, from_columns(ggz, 0, wide_w), gw_h, 0, 0, True),
        (3, from_columns(ggz, dm, wide_w), gw_h, 0, dm, True),
        (4, from_columns(gy, 0, wide_w), gm_h, 0, 0, True),
        (5, from_columns(gy, dm, wide_w), gm_h, 0, dm, True),
        (6, from_columns(drv, 0, LN), gm_h, 0, di, True),
        (7, lambda part, r0, n: sm[part, pl.ds(pl.multiple_of(r0, 8), n), :], sm_h, 0, 0, False),
    ]

    plan = list(PLAN)
    live = {}

    def service(last=False):
        todo = [g for part in plan for g in part] if last else plan.pop(0)
        for g in todo:
            if g not in live:
                live[g] = group_steps(*groups[g])
            next(live[g], None)

    for i in range(seqs * nblk // 2):
        s, i0 = (2 * i) // nblk, (2 * i) % nblk

        def backward_body(b, _, s=s):
            made = [pair_backward(2 * b + h, s) for h in range(2)]
            t1, t2, t3 = (p + q for p, q in zip(made[0][1], made[1][1]))
            gsc[s, :half, :half] += t1
            gsc[s, :half, half:] += t2
            gsc[s, half:, half:] += t3
            for cols, _, lo, hi in made:
                z[s, :half, cols] = lo
                z[s, half:, cols] = hi
            backward_slot((seqs + s) * nblk + b)
            return 0

        service()
        lax.fori_loop(i0, i0 + 2, backward_body, 0)
    slots_alone(backward_slot, 2 * seqs * nblk, b_slots)
    service()

    ginf[...] = jnp.zeros_like(ginf)
    hs_d[...] = jnp.zeros_like(hs_d)
    hs_g[...] = jnp.zeros_like(hs_g)
    bdh[...] = jnp.zeros_like(bdh)

    def head_sum(v, x):
        hi, lo = split2(v)
        return dot_nt(hi, x) + dot_nt(lo, x)

    def head_sum3(v, x):
        hi, mid, lo = split3(v)
        return dot_nt(hi, x) + dot_nt(mid, x) + dot_nt(lo, x)

    def gh_copy(b):
        cols = ds(b * BW, BW)
        return pltpu.make_async_remote_copy(
            src_ref=big.at[:, pl.ds(0, 8), cols], dst_ref=big.at[:, pl.ds(length, 8), cols],
            send_sem=gh_s.at[b], recv_sem=gh_r.at[b], device_id=prv, device_id_type=MESH,
        )

    @pl.when(jnp.logical_not(has_next))
    def _():
        big[:, length : length + 8, :] = jnp.zeros((seqs, 8, xbc), F32)

    def finish_block(b, s, ga):
        cols = ds(b * BW, BW)
        f = fil[s, :, cols]
        sg = sigmoid(f)
        gf = ga * (sg * (1.0 + f * (1.0 - sg)))
        big[s, 0:length, cols] = gf
        return jnp.sum(gf, axis=0, keepdims=True)

    def last_body(b, _):
        cols = ds(b * BW, BW)
        cb_sum = jnp.zeros((1, BW), F32)
        sk_sum = jnp.zeros((1, BW), F32)
        x = xx[:, cols]
        for s in range(seqs):
            lt = in_b[s * nblk + b]
            pr = prior_of(s, b)
            f = fil[s, :, cols]
            sg = sigmoid(f)
            sig = f * sg
            stw = dot(pst[s], x)
            gst = dot(infl[s], lt) * dot(ptl[s], x)
            gd = z[s, :, cols]
            gyf = gy[s, :, cols].astype(F32)
            sk_row = skw[0:1, cols]
            gg = gst + gd
            ga = sk_row * gyf + stw * gg
            t1 = stw * sig * gst
            dd = gyf * (y[s, :, cols] - sk_row * sig) - drv[s, :, cols].astype(F32) * gd - t1
            hs_d[s] += head_sum(dd, x)
            hs_g[s] += head_sum(sig * gg, x)
            bd = jnp.sum(t1, axis=0, keepdims=True) + dlast[s, 7:8, cols] * jnp.sum(
                lt.astype(F32) * pr, axis=0, keepdims=True
            )
            bdh[s] += head_sum3(jnp.broadcast_to(bd, (8, BW)), x)
            sk_sum = sk_sum + jnp.sum(gyf * sig, axis=0, keepdims=True)
            ginf[s] += dot_nt(scl[s, :, cols], lt)
            gf = ga * (sg * (1.0 + f * (1.0 - sg)))
            big[s, 0:length, cols] = gf
            cb_sum = cb_sum + jnp.sum(gf, axis=0, keepdims=True)
        small_put(SM_CONVB, b, cb_sum)
        sk_row_r[0:1, cols] = sk_sum

        @pl.when(has_prev)
        def _():
            gh_copy(b).start()

        return 0

    def mixed_body(b):
        cols = ds(b * BW, BW)

        @pl.when(has_next)
        def _():
            gh_copy(b).wait_recv()

        parts = []
        sums = [jnp.zeros((1, BW), F32) for _ in range(window + 1)]
        for s in range(seqs):
            gf = big[s, :, cols]
            rows = gf.shape[0]
            m = ext[s, :, cols].astype(F32)
            gm = jnp.zeros((length, BW), F32)
            for k in range(window + 1):
                shift = window - k
                moved = pltpu.roll(gf, rows - shift, 0) if shift else gf
                gm = gm + cw_r[k : k + 1, cols] * moved[:length]
                em = pltpu.roll(m, shift, 0) if shift else m
                sums[k] = sums[k] + jnp.sum(gf[:length] * em[hw:], axis=0, keepdims=True)
            parts.append(gm.astype(BF))
        for k in range(window + 1):
            small_put(SM_CONVW + k * (xbc // LN), b, sums[k])
        return parts

    def mixed_loop(b, _):
        cols = ds(b * BW, BW)
        for s, part in enumerate(mixed_body(b)):
            gy[s, :, cols] = part
        return 0

    third = nblk // 2
    lax.fori_loop(0, third, last_body, 0)
    service()
    lax.fori_loop(0, third, mixed_loop, 0)
    service()
    lax.fori_loop(third, nblk, last_body, 0)
    service()

    cb_sum = jnp.zeros((1, BW), F32)
    for s in range(seqs):
        gst_bf = gsc[s].astype(BF)
        gi = ginf[s] + dot(gst_bf, outf[s])
        go = gout[s] + dot(gst_bf.T, infl[s])
        cb_sum = cb_sum + finish_block(nblk, s, jnp.concatenate([gi, go], axis=1))
    small_put(SM_CONVB, nblk, cb_sum)

    @pl.when(has_prev)
    def _():
        gh_copy(nblk).start()

    lax.fori_loop(third, nblk, mixed_loop, 0)
    service()
    for s, part in enumerate(mixed_body(nblk)):
        drv[s, :, 0:BW] = part
    service()

    row_i = lax.broadcasted_iota(jnp.int32, (length, LN), 0)
    glr = jnp.zeros((1, LN), F32)
    gsb = jnp.zeros((1, LN), F32)
    grl = []
    for s in range(seqs):
        gc = hs_d[s] + jnp.where(row_i == length - 1, bdh[s, 0:1], 0.0)
        terms = dot3(tri[1], gc)
        gst = hs_g[s] + terms * rates3
        glr = glr + jnp.sum(terms * st[s], axis=0, keepdims=True)
        graw = gst * sigmoid(sraw[s] + bias3)
        gsb = gsb + jnp.sum(graw, axis=0, keepdims=True)
        grl.append(jnp.where(lane128 < heads, graw, 0.0).astype(BF))
    sk_h = head_sum3(jnp.broadcast_to(sk_row_r[0:1, :], (8, di)), xx[...])
    small_one(SM_HEADS, gsb)
    small_one(SM_HEADS + 1, rates3 * glr)
    small_one(SM_HEADS + 2, sk_h[0:1])
    stepg = dot(grl[0].T, ne[0, hw:, :])
    for s in range(1, seqs):
        stepg = stepg + dot(grl[s].T, ne[s, hw:, :])
    for i in range(dm // LN):
        row = SM_STEP + 24 * i
        for lo, hi in ((row, min(row + 24, 128)), (max(row, 128), row + 24)):
            if lo < hi:
                sm[lo // 128, lo % 128 : lo % 128 + hi - lo, :] = stepg[
                    lo - row : hi - row, i * LN : (i + 1) * LN
                ]

    service()
    for s in range(seqs):
        for i in range(dm // BW):
            cols = slice(i * BW, (i + 1) * BW)
            pj = dot(nrm[s], wo[:, cols])
            res_r[s, :, cols] = (tok[s, :, cols].astype(F32) + pj).astype(BF)
        service()
    res_copy = pltpu.make_async_copy(res_r, res_h, tok_sem.at[0])
    res_copy.start()
    for s in range(seqs):
        for i in range(dm // BW):
            cols = slice(i * BW, (i + 1) * BW)
            gn[s, :, cols] = (
                dot_nt(gy[s], wm[cols, :di])
                + dot_nt(drv[s, :, 0:BW], wm[cols, di:])
                + dot_nt(ggz[s], wg[cols, :])
                + dot_nt(grl[s], ws3[cols])
            )
        service()

    @pl.when(has_next)
    def _():
        halo_copy.wait_send()

    def token_body(i, sums):
        for s in range(seqs):
            rows = ds(i * 16, 16)
            v = tok[s, rows, :].astype(F32)
            inv = lax.rsqrt(jnp.mean(v * v, axis=-1, keepdims=True) + EPSILON)
            unit = v * inv
            gr = gn[s, rows, :]
            sums = sums + jnp.sum(gr * unit, axis=0, keepdims=True)
            q = gr * gain
            back = inv * (q - unit * jnp.mean(q * unit, axis=-1, keepdims=True))
            tok[s, rows, :] = (cot[s, rows, :].astype(F32) + back).astype(BF)
        return sums

    n_sum = lax.fori_loop(0, length // 16, token_body, jnp.zeros((1, dm), F32))
    for i in range(dm // LN):
        small_one(SM_NORM + i, n_sum[:, i * LN : (i + 1) * LN])
    tg_copy = pltpu.make_async_copy(tok, tg_h, tok_sem.at[1])
    tg_copy.start()
    service(last=True)
    res_copy.wait()
    tg_copy.wait()
    for copy in sent:
        copy.wait_send()

    def drain(q, _):
        @pl.when(has_prev)
        def _():
            backward_copy(q).wait_send()

        return 0

    lax.fori_loop(0, seqs * nblk, drain, 0)

    def drain_halo(b, _):
        @pl.when(has_prev)
        def _():
            gh_copy(b).wait_send()

        return 0

    lax.fori_loop(0, xbc // BW, drain_halo, 0)


def on_device(nctx, *args):
    tokens, norm_gain, wg, wm, ws, conv_w, conv_b, sb, lr, sk, gg, wo, cot = args
    seqs, length, dm = tokens.shape
    di = wg.shape[1]
    xbc = wm.shape[1]
    heads = ws.shape[1]
    nst = (xbc - di) // 2
    nchunk = di // LN
    nblk = di // BW
    hw = 16
    vm = pltpu.VMEM
    any_spec = pl.BlockSpec(memory_space=pl.ANY)
    vm_spec = pl.BlockSpec(memory_space=vm)
    dma = pltpu.SemaphoreType.DMA
    extras = max(1, (nctx // 16).bit_length())
    bufs = []
    for rows, w, kind in [(dm, dm // 2, BF)] * 6 + [(dm, LN, BF), (128, LN, F32)]:
        bufs += [vm((rows, w), kind)] * 3 + [vm((rows // 2, w), F32)]
        bufs += [vm((extras, rows // 16, w), kind) if nctx > 8 else vm((1, 16, LN), kind)]
    out = pl.pallas_call(
        functools.partial(layer_kernel, nctx),
        out_shape=(
            jax.ShapeDtypeStruct(tokens.shape, BF),
            jax.ShapeDtypeStruct(tokens.shape, BF),
            jax.ShapeDtypeStruct((di, dm), BF),
            jax.ShapeDtypeStruct((dm, di), BF),
            jax.ShapeDtypeStruct((dm, xbc), BF),
            jax.ShapeDtypeStruct((256, LN), F32),
        ),
        in_specs=[any_spec, vm_spec, any_spec, any_spec] + [vm_spec] * 7 + [any_spec] * 2,
        out_specs=(any_spec,) * 6,
        scratch_shapes=[
            vm((seqs, length, dm), BF),
            vm((seqs, length, dm), BF),
            vm((dm, di), BF),
            vm((dm, xbc), BF),
            vm((di, dm), BF),
            vm((seqs, hw, dm), BF),
            vm((seqs, hw + length, dm), BF),
            vm((dm, seqs * length), BF),
            vm((seqs, hw + length, xbc), BF),
            vm((seqs, length, xbc), F32),
            vm((seqs, length, di), BF),
            vm((seqs, length, di), BF),
            vm((seqs, length, di), F32),
            vm((seqs, length, di), F32),
            vm((seqs, length + 8, xbc), F32),
            vm((seqs, length, di), BF),
            vm((seqs, length, di), BF),
            vm((seqs, length, di), BF),
            vm((di, seqs * length), BF),
            vm((seqs, length, LN), F32),
            vm((seqs, length, LN), F32),
            vm((seqs, length, dm), F32),
            vm((seqs * nchunk, nst, LN), F32),
            vm((seqs * nchunk, nst, LN), F32),
            vm((seqs * nblk, nst, BW), BF),
            vm((seqs * nblk, nst, BW), BF),
            vm((seqs, length, LN), F32),
            vm((seqs, length, LN), F32),
            vm((seqs, length, LN), F32),
            vm((seqs, LN, length), F32),
            vm((seqs, length, LN), BF),
            vm((seqs, length, LN), BF),
            vm((seqs, length, LN), BF),
            vm((seqs, 8, di), F32),
            vm((seqs, length, nst), BF),
            vm((seqs, length, nst), BF),
            vm((seqs, nst, length), BF),
            vm((seqs, nst, length), BF),
            vm((seqs, length, length), F32),
            vm((seqs, length, length), F32),
            vm((LN, di), BF),
            vm((2, length, length), BF),
            vm((seqs, length, LN), F32),
            vm((seqs, length, LN), F32),
            vm((seqs, 8, LN), F32),
            vm((seqs, length, dm), BF),
            dma((2,)),
            vm((8, di), F32),
            vm((2, 128, LN), F32),
            vm((8, di), F32),
            bufs,
            dma((8, 12)), dma((8, 12)), dma((8,)), dma((8, extras)), dma((8, extras)),
            dma((5,)), dma, dma,
            dma((seqs * nchunk,)), dma((seqs * nchunk,)), dma((seqs * nblk,)), dma((seqs * nblk,)),
            dma((xbc // BW,)), dma((xbc // BW,)),
        ],
        compiler_params=pltpu.CompilerParams(
            collective_id=0, has_side_effects=True, vmem_limit_bytes=65200 * 1024
        ),
    )(*args[:4], ws.T, *args[5:])
    res, tg, g_out, g_gate, g_mixer, small = out
    gate0 = xbc // LN
    norm0 = gate0 + di // LN
    convw0 = norm0 + dm // LN
    taps = conv_w.shape[0]
    heads0 = convw0 + taps * (xbc // LN)
    step0 = -(-(heads0 + 3) // 8) * 8

    def finish(res_i, tg_i, go_i, gw_i, gm_i, sm_i, *outs):
        res_o, tg_o, ng_o, gw_o, gm_o, st_o, cw_o, cb_o, sb_o, lr_o, sk_o, gg_o, go_o = outs
        res_o[...] = res_i[...]
        tg_o[...] = tg_i[...]
        go_o[...] = go_i[...].astype(F32)
        gw_o[...] = gw_i[...].astype(F32)
        gm_o[...] = gm_i[...].astype(F32)

        @pl.when(pl.program_id(0) == 0)
        def _():
            for ref, first, count in (
                (cb_o, 0, xbc // LN), (gg_o, gate0, di // LN), (ng_o, norm0, dm // LN),
            ):
                for i in range(count):
                    ref[pl.ds(i * LN, LN)] = sm_i[first + i, :]
            for k in range(taps):
                for i in range(xbc // LN):
                    r = convw0 + k * (xbc // LN) + i
                    cw_o[k : k + 1, i * LN : (i + 1) * LN] = sm_i[r : r + 1, :]
            for i, ref in enumerate((sb_o, lr_o, sk_o)):
                ref[...] = sm_i[heads0 + i, 0:heads]
            for i in range(dm // LN):
                r = step0 + heads * i
                st_o[:, i * LN : (i + 1) * LN] = sm_i[r : r + heads, :]

    steps = 4

    def rows_of(a, dim=0):
        block = tuple(n // steps if i == dim else n for i, n in enumerate(a.shape))
        return pl.BlockSpec(block, lambda t: tuple(t if i == dim else 0 for i in range(a.ndim)))

    def whole(*shape):
        return pl.BlockSpec(shape, lambda t: (0,) * len(shape))

    def shape(*dims):
        return jax.ShapeDtypeStruct(dims, F32)

    small_shapes = {
        2: (dm,), 5: (heads, dm), 6: (taps, xbc), 7: (xbc,), 8: (heads,), 9: (heads,),
        10: (heads,), 11: (di,),
    }
    big_outs = {0: res, 1: tg, 3: g_gate, 4: g_mixer, 12: g_out}
    final = pl.pallas_call(
        finish,
        grid=(steps,),
        in_specs=[
            rows_of(res, 1), rows_of(tg, 1), rows_of(g_out), rows_of(g_gate), rows_of(g_mixer),
            whole(*small.shape),
        ],
        out_specs=[
            rows_of(big_outs[i], 1 if i < 2 else 0) if i in big_outs else whole(*small_shapes[i])
            for i in range(13)
        ],
        out_shape=[
            jax.ShapeDtypeStruct(big_outs[i].shape, BF if i < 2 else F32)
            if i in big_outs else shape(*small_shapes[i])
            for i in range(13)
        ],
        compiler_params=pltpu.CompilerParams(vmem_limit_bytes=62 * 1024 * 1024),
    )(res, tg, g_out, g_gate, g_mixer, small)
    final = list(final)
    final[5] = final[5].T
    return tuple(final)


def solution(mesh):
    tok = P("seq", "ctx", None)
    return jax.shard_map(
        functools.partial(on_device, mesh.shape["ctx"]),
        mesh=mesh,
        in_specs=(tok,) + (P(),) * 11 + (tok,),
        out_specs=(tok, tok) + (P(),) * 11,
        check_vma=False,
    )
```

```python
import functools

import jax
import jax.numpy as jnp
from jax import lax
from jax.experimental import pallas as pl
from jax.experimental.pallas import tpu as pltpu
from jax.sharding import PartitionSpec as P

MESH = pl.DeviceIdType.MESH
BF = jnp.bfloat16
F32 = jnp.float32
EPSILON = 1e-05
BW = 256
LN = 128
SKEW = 2
PLAN = (
    (0, 2, 3, 0, 2, 3, 1),
    (),
    (1,),
    (),
    (0,),
    (),
    (2,),
    (3,),
    (4, 0, 2, 1, 4),
    (3,),
    (0, 5, 4, 2, 1, 5),
    (6, 3),
    (6,),
    (0, 4),
    (),
    (),
    (2, 5),
    (6,),
    (1, 0),
    (),
    (),
    (7, 3, 7, 5, 4, 7, 3, 6, 1, 2, 5, 7, 4, 6, 1, 7, 5, 4, 6, 2, 2, 3, 3, 7, 5, 0, 0, 4, 1,
    7, 6, 4, 5, 5, 7, 7, 6, 1, 6),
)


def dot(a, b):
    return jnp.dot(a, b, preferred_element_type=F32)


def dot_nt(a, b):
    return lax.dot_general(a, b, (((1,), (1,)), ((), ())), preferred_element_type=F32)


def split2(v):
    hi = v.astype(BF)
    return hi, (v - hi.astype(F32)).astype(BF)


def split3(v):
    hi = v.astype(BF)
    rest = v - hi.astype(F32)
    mid = rest.astype(BF)
    return hi, mid, (rest - mid.astype(F32)).astype(BF)


def dot3(a, v):
    hi, mid, lo = split3(v)
    return dot(a, hi) + dot(a, mid) + dot(a, lo)


def pieces3(v):
    lane = lax.broadcasted_iota(jnp.int32, v.shape, 1)
    hi, mid, lo = split3(v)
    z = jnp.zeros_like(v)
    return jnp.where(
        lane < 32,
        hi.astype(F32),
        jnp.where(lane < 64, mid.astype(F32), jnp.where(lane < 96, lo.astype(F32), z)),
    ).astype(BF)


def sigmoid(v):
    return 1.0 / (1.0 + jnp.exp(-v))


def ds(start, size):
    return pl.ds(pl.multiple_of(start, size), size)


def layer_kernel(
    nctx,
    tok_h, ng_r, wg_h, wm_h, ws_r, cw_r, cb_r, sb_r, lr_r, sk_r, gg_r, wo_h, cot_h,
    res_h, tg_h, go_h, gw_h, gm_h, sm_h,
    tok, cot, wg, wm, wo, halo, ne, nt, ext, fil, drv, scl, y, z, big, gy, ggz, nrm, nrt,
    acc_a, acc_b, gn, sum_s, in_f, out_b, in_b, sraw, st, cum, cum_t, pst, ptl, pdc,
    dlast, infl, outf, inf_t, outf_t, sco, sco_t, xx, tri, hs_d, hs_g, bdh,
    res_r, tok_sem, skw, sm, sk_row_r, bufs, ar_s, ar_r, loc_sem, ex_s, ex_r,
    in_sem, halo_s, halo_r, fs_s, fs_r, bs_s, bs_r, gh_s, gh_r,
):
    seqs, length, dm = tok.shape
    di = wg.shape[1]
    xbc = wm.shape[1]
    heads = ws_r.shape[0]
    hp = di // heads
    nst = (xbc - di) // 2
    window = cw_r.shape[0] - 1
    nblk = di // BW
    gsc, gout, ginf = sco, acc_a, acc_b
    nchunk = di // LN
    hw = 16
    seq = lax.axis_index("seq")
    ctx = lax.axis_index("ctx")
    has_prev = ctx > 0
    has_next = ctx < nctx - 1
    prv = (seq, ctx - 1)
    nxt = (seq, ctx + 1)

    barrier = pltpu.get_barrier_semaphore()

    @pl.when(has_prev)
    def _():
        pl.semaphore_signal(barrier, inc=1, device_id=prv, device_id_type=MESH)

    @pl.when(has_next)
    def _():
        pl.semaphore_signal(barrier, inc=1, device_id=nxt, device_id_type=MESH)

    loads = [
        pltpu.make_async_copy(a, b, in_sem.at[i])
        for i, (a, b) in enumerate(
            ((tok_h, tok), (wm_h, wm), (cot_h, cot), (wo_h, wo), (wg_h, wg))
        )
    ]
    for copy in loads[:2]:
        copy.start()

    core = lax.rem(ctx, 2)

    def flipped(index, mask):
        bit = lax.rem(index // mask, 2)
        return bit, index + mask - 2 * mask * bit

    core_peer = (seq, flipped(ctx, 1)[1])
    stages = []
    for mask in (1 + core, 2 - core):
        bit, other = flipped(seq, mask)
        stages.append((bit, (other, ctx)))
    in_row = lax.rem(ctx // 2, 4)
    row_peers = [(seq, ctx + 2 * (lax.rem(in_row + d, 4) - in_row)) for d in (1, 2, 3)]
    extras = []
    mask = 8
    while mask < nctx:
        extras.append((seq, flipped(ctx, mask)[1]))
        mask *= 2
    peers = [peer for _, peer in stages] + row_peers + extras
    for peer in peers:
        pl.semaphore_signal(barrier, inc=1, device_id=peer, device_id_type=MESH)
    lane128 = lax.broadcasted_iota(jnp.int32, (1, LN), 1)
    r_i = lax.broadcasted_iota(jnp.int32, (LN, di), 0)
    c_i = lax.broadcasted_iota(jnp.int32, (LN, di), 1)
    first = jnp.bitwise_and(r_i, 31) * hp
    xx[...] = jnp.where((c_i >= first) & (c_i < first + hp) & (r_i < 96), 1.0, 0.0).astype(BF)
    t_r = lax.broadcasted_iota(jnp.int32, (length, length), 0)
    t_c = lax.broadcasted_iota(jnp.int32, (length, length), 1)
    tri[0] = jnp.where(t_r >= t_c, 1.0, 0.0).astype(BF)
    tri[1] = jnp.where(t_r <= t_c, 1.0, 0.0).astype(BF)
    k_i = lax.broadcasted_iota(jnp.int32, (heads, LN), 0)
    l_i = lax.broadcasted_iota(jnp.int32, (heads, LN), 1)
    rep = jnp.where((l_i % 32 == k_i) & (l_i < 96), 1.0, 0.0)

    def replicated(row_ref):
        row = jnp.broadcast_to(row_ref[...].reshape(1, heads), (8, heads))
        hi, mid, lo = split3(row)
        r = rep.astype(BF)
        return (dot(hi, r) + dot(mid, r) + dot(lo, r))[0:1]

    ws3 = dot(ws_r[...].T, rep.astype(BF)).astype(BF)
    bias3 = replicated(sb_r)
    rates3 = -jnp.exp(replicated(lr_r))
    sk8 = jnp.broadcast_to(replicated(sk_r), (8, LN))
    skw[...] = dot(pieces3(sk8), xx[...])

    pl.semaphore_wait(
        barrier, has_prev.astype(jnp.int32) + has_next.astype(jnp.int32) + len(peers)
    )
    loads[0].wait()
    for copy in loads[2:]:
        copy.start()

    halo_copy = pltpu.make_async_remote_copy(
        src_ref=tok.at[:, pl.ds(length - hw, hw), :], dst_ref=halo, send_sem=halo_s,
        recv_sem=halo_r, device_id=nxt, device_id_type=MESH,
    )

    @pl.when(has_next)
    def _():
        halo_copy.start()

    @pl.when(jnp.logical_not(has_prev))
    def _():
        halo[...] = jnp.zeros_like(halo)
        in_f[...] = jnp.zeros_like(in_f)

    @pl.when(jnp.logical_not(has_next))
    def _():
        in_b[...] = jnp.zeros_like(in_b)

    gain = ng_r[...].reshape(1, dm)

    def norm_rows(rows):
        v = rows.astype(F32)
        inv = lax.rsqrt(jnp.mean(v * v, axis=-1, keepdims=True) + EPSILON)
        return ((v * inv) * gain).astype(BF)

    for s in range(seqs):

        def norm_body(i, _, s=s):
            ne[s, ds(hw + i * 16, 16), :] = norm_rows(tok[s, ds(i * 16, 16), :])
            return 0

        lax.fori_loop(0, length // 16, norm_body, 0, unroll=2)

    for s in range(seqs):
        raw = dot(ne[s, pl.ds(hw, length), :], ws3)
        sraw[s] = raw
        step = jax.nn.softplus(raw + bias3)
        st[s] = step
        cu = dot3(tri[0], step * rates3)
        cum[s] = cu
        cum_t[s] = cu.T
        last = cu[length - 1 : length]
        pst[s] = pieces3(step)
        ptl[s] = pieces3(jnp.exp(last - cu))
        dec = jnp.exp(cu)
        pdc[s] = pieces3(dec)
        dlast[s] = dot(pieces3(dec[length - 8 :]), xx[...])

    for s in range(seqs):
        for b in range(dm // BW):
            nt[b * BW : (b + 1) * BW, s * length : (s + 1) * length] = ne[
                s, hw : hw + length, b * BW : (b + 1) * BW
            ].T

    @pl.when(has_prev)
    def _():
        halo_copy.wait_recv()

    for s in range(seqs):
        ne[s, 0:hw, :] = norm_rows(halo[s])

    loads[1].wait()

    def filter_block(b, s):
        cols = ds(b * BW, BW)
        m_bf = dot(ne[s], wm[:, cols]).astype(BF)
        m = m_bf.astype(F32)
        f = cb_r[cols].reshape(1, BW)
        for k in range(window + 1):
            shift = window - k
            moved = pltpu.roll(m, shift, 0) if shift else m
            f = f + cw_r[k : k + 1, cols] * moved[hw:]
        return cols, m_bf, f

    for s in range(seqs):
        cols, m_bf, f = filter_block(nblk, s)
        ext[s, :, cols] = m_bf
        fil[s, :, cols] = f
        act = f * sigmoid(f)
        i_bf = act[:, :nst].astype(BF)
        o_bf = act[:, nst:].astype(BF)
        infl[s] = i_bf
        outf[s] = o_bf
        inf_t[s] = i_bf.T
        outf_t[s] = o_bf.T
        sco[s] = dot_nt(o_bf, i_bf)
        sco_t[s] = dot_nt(i_bf, o_bf)

    def forward_copy(q):
        return pltpu.make_async_remote_copy(
            src_ref=sum_s.at[q], dst_ref=in_f.at[q], send_sem=fs_s.at[q],
            recv_sem=fs_r.at[q], device_id=nxt, device_id_type=MESH,
        )

    def backward_copy(q):
        return pltpu.make_async_remote_copy(
            src_ref=out_b.at[q], dst_ref=in_b.at[q], send_sem=bs_s.at[q],
            recv_sem=bs_r.at[q], device_id=prv, device_id_type=MESH,
        )

    f_skew = SKEW * ctx
    b_skew = SKEW * (nctx - 1 - ctx)
    f_slots = seqs * nchunk + SKEW * (nctx - 1)
    b_slots = seqs * nblk + SKEW * (nctx - 1)

    def forward_slot(slot):
        q = slot - f_skew

        @pl.when((q >= 0) & (q < seqs * nchunk))
        def _():
            @pl.when(has_prev)
            def _():
                forward_copy(q).wait_recv()

            @pl.when(has_next)
            def _():
                row = dlast[q // nchunk, 7:8, ds(lax.rem(q, nchunk) * LN, LN)]
                sum_s[q] = row * in_f[q] + sum_s[q]
                forward_copy(q).start()

    def backward_slot(slot):
        q = slot - b_skew

        @pl.when((q >= 0) & (q < seqs * nblk))
        def _():
            @pl.when(has_next)
            def _():
                backward_copy(q).wait_recv()

            @pl.when(has_prev)
            def _():
                row = dlast[q // nblk, 7:8, ds(lax.rem(q, nblk) * BW, BW)]
                add = jnp.concatenate([sum_s[2 * q], sum_s[2 * q + 1]], axis=1)
                out_b[q] = (row * in_b[q].astype(F32) + add).astype(BF)
                backward_copy(q).start()

    def slots_alone(one, first, last):
        lax.fori_loop(first, last, lambda t, _: (one(t), 0)[1], 0)

    for s in range(seqs):

        def signal_body(i, _, s=s):
            made = []
            for b in (2 * i, 2 * i + 1):
                cols, m_bf, f = filter_block(b, s)
                sig = f * sigmoid(f)
                x = xx[:, cols]
                dr = sig * dot(pst[s], x)
                sc = (dr * dot(ptl[s], x)).astype(BF)
                made.append(
                    (b, cols, m_bf, f, skw[0:1, cols] * sig, dr.astype(BF), sc, dot(inf_t[s], sc))
                )
            for b, cols, m_bf, f, sk_sig, dr, sc, summ in made:
                ext[s, :, cols] = m_bf
                fil[s, :, cols] = f
                y[s, :, cols] = sk_sig
                drv[s, :, cols] = dr
                scl[s, :, cols] = sc
                sum_s[s * nchunk + 2 * b] = summ[:, :LN]
                sum_s[s * nchunk + 2 * b + 1] = summ[:, LN:]
            for slot in (2 * i, 2 * i + 1):
                forward_slot(s * nblk + slot)
            return 0

        lax.fori_loop(0, nblk // 2, signal_body, 0)

    SM_CONVB = 0
    SM_GATE = SM_CONVB + xbc // LN
    SM_NORM = SM_GATE + di // LN
    SM_CONVW = SM_NORM + dm // LN
    SM_HEADS = SM_CONVW + (window + 1) * (xbc // LN)
    SM_STEP = -(-(SM_HEADS + 3) // 8) * 8
    sm[...] = jnp.zeros_like(sm)

    def small_one(row, value):
        sm[row // 128, pl.ds(row % 128, 1), :] = value

    def small_put(base, b, value):
        small_one(base + 2 * b, value[:, :LN])
        small_one(base + 2 * b + 1, value[:, LN:])

    half = length // 2
    d_r = lax.broadcasted_iota(jnp.int32, (half, half), 0)
    d_c = lax.broadcasted_iota(jnp.int32, (half, half), 1)
    NEG = -1e30

    def columns_of(s, j):
        moved = pltpu.roll(cum[s], lax.rem(LN - 2 * j, LN), 1)
        return moved[:, 0:1], moved[:, 1:2]

    def pair_forward(j, s):
        cols = ds(j * LN, LN)
        d = drv[s, :, cols]
        lane_low = lane128 < hp
        top, bottom = [], []
        for hh, col in enumerate(columns_of(s, j)):
            row = cum_t[s, pl.ds(2 * j + hh, 1), :]
            fa = jnp.exp(jnp.where(d_r >= d_c, col[:half] - row[:, :half], NEG))
            fb = jnp.exp(col[half:] - row[:, :half])
            fc = jnp.exp(jnp.where(d_r >= d_c, col[half:] - row[:, half:], NEG))
            top.append((sco[s, :half, :half] * fa).astype(BF))
            bottom.append(
                jnp.concatenate(
                    [
                        (sco[s, half:, :half] * fb).astype(BF),
                        (sco[s, half:, half:] * fc).astype(BF),
                    ],
                    axis=1,
                )
            )
        lo = dot(jnp.concatenate(top, axis=0), d[:half])
        hi = dot(jnp.concatenate(bottom, axis=0), d)
        return (
            y[s, :half, cols] + jnp.where(lane_low, lo[:half], lo[half:]),
            y[s, half:, cols] + jnp.where(lane_low, hi[:half], hi[half:]),
        )

    loads[2].wait()
    loads[3].wait()
    loads[4].wait()

    for s in range(seqs):

        def forward_body(i, _, s=s):
            made = []
            for b in (2 * i, 2 * i + 1):
                cols = ds(b * BW, BW)
                made.append(
                    (
                        b, cols, dot_nt(cot[s], wo[cols, :]),
                        dot(ne[s, hw : hw + length, :], wg[:, cols]),
                        [pair_forward(2 * b + h, s) for h in range(2)],
                    )
                )
            for b, cols, g, zz, pairs in made:
                big[s, 0:length, cols] = g
                z[s, :, cols] = zz
                for h, (lo, hi) in enumerate(pairs):
                    lanes = ds((2 * b + h) * LN, LN)
                    y[s, :half, lanes] = lo
                    y[s, half:, lanes] = hi
            for slot in (2 * i, 2 * i + 1):
                forward_slot((seqs + s) * nblk + slot)
            return 0

        lax.fori_loop(0, nblk // 2, forward_body, 0)

    acc_a[...] = jnp.zeros_like(acc_a)
    acc_b[...] = jnp.zeros_like(acc_b)

    def prior_of(s, b):
        return jnp.concatenate(
            [in_f[s * nchunk + 2 * b], in_f[s * nchunk + 2 * b + 1]], axis=1
        )

    def gate_blocks(blocks, s):
        made = []
        a_sum = c_sum = None
        for b in blocks:
            cols = ds(b * BW, BW)
            phi, plo = split2(prior_of(s, b))
            out = (dot(outf[s], phi) + dot(outf[s], plo)) * dot(pdc[s], xx[:, cols])
            yy = y[s, :, cols] + out
            zz = z[s, :, cols]
            gated = yy * (zz * sigmoid(zz))
            q = big[s, 0:length, cols] * gg_r[cols].reshape(1, BW)
            a = gated * gated
            c = q * gated
            a, c = a[:, :LN] + a[:, LN:], c[:, :LN] + c[:, LN:]
            a_sum, c_sum = (a, c) if a_sum is None else (a_sum + a, c_sum + c)
            made.append((cols, yy))
        for cols, yy in made:
            y[s, :, cols] = yy
        acc_a[s] += a_sum
        acc_b[s] += c_sum

    def grad_blocks(blocks, s, iv, mean):
        made = []
        g_out = None
        for b in blocks:
            cols = ds(b * BW, BW)
            yy = y[s, :, cols]
            zz = z[s, :, cols]
            sg = sigmoid(zz)
            act = zz * sg
            unit = (yy * act) * iv
            gain_row = gg_r[cols].reshape(1, BW)
            g = big[s, 0:length, cols]
            no = (unit * gain_row).astype(BF)
            gain_sum = jnp.sum(g * unit, axis=0, keepdims=True)
            gr = iv * (g * gain_row - unit * mean)
            gyb = (gr * act).astype(BF)
            gzb = (gr * yy * (sg * (1.0 + zz * (1.0 - sg)))).astype(BF)
            w = gyb.astype(F32) * dot(pdc[s], xx[:, cols])
            whi, wlo = split2(w)
            gp = dot(outf_t[s], whi) + dot(outf_t[s], wlo)
            phi, plo = split2(prior_of(s, b))
            go = dot_nt(whi, phi) + (dot_nt(wlo, phi) + dot_nt(whi, plo))
            g_out = go if g_out is None else g_out + go
            made.append((b, cols, no, no.T, gain_sum, gyb, gzb, gp))
        for b, cols, no, no_t, gain_sum, gyb, gzb, gp in made:
            nrm[s, :, cols] = no
            nrt[cols, s * length : (s + 1) * length] = no_t
            sk_row_r[1 + s : 2 + s, cols] = gain_sum
            gy[s, :, cols] = gyb
            ggz[s, :, cols] = gzb
            sum_s[s * nchunk + 2 * b] = gp[:, :LN]
            sum_s[s * nchunk + 2 * b + 1] = gp[:, LN:]
        gout[s] += g_out

    first_done = f_slots - nchunk * (seqs - 1)
    slots_alone(forward_slot, seqs * nchunk, first_done)
    for s in range(seqs):
        slot0 = first_done + s * nchunk

        def passing(i, s=s, slot0=slot0):
            if s < seqs - 1:
                forward_slot(slot0 + i)
            else:
                backward_slot(i)

        def gate_body(i, _, s=s, passing=passing):
            gate_blocks((2 * i, 2 * i + 1), s)
            passing(2 * i)
            passing(2 * i + 1)
            return 0

        lax.fori_loop(0, nblk // 2, gate_body, 0)
        iv = lax.rsqrt(jnp.sum(acc_a[s], axis=-1, keepdims=True) / di + EPSILON)
        mean = iv * jnp.sum(acc_b[s], axis=-1, keepdims=True) / di
        gout[s] = jnp.zeros_like(gout[s])

        def sent_forward(c, _, s=s):
            @pl.when(has_next)
            def _():
                forward_copy(s * nchunk + c).wait_send()

            return 0

        lax.fori_loop(0, nchunk, sent_forward, 0)

        def grad_body(i, _, s=s, iv=iv, mean=mean, passing=passing):
            grad_blocks((2 * i, 2 * i + 1), s, iv, mean)
            passing(nblk + 2 * i)
            passing(nblk + 2 * i + 1)
            return 0

        lax.fori_loop(0, nblk // 2, grad_body, 0)

    def gate_gain_body(b, _):
        cols = ds(b * BW, BW)
        total = sk_row_r[1:2, cols]
        for s in range(1, seqs):
            total = total + sk_row_r[1 + s : 2 + s, cols]
        small_put(SM_GATE, b, total)
        return 0

    lax.fori_loop(0, nblk, gate_gain_body, 0)

    gsc[...] = jnp.zeros_like(gsc)

    def pair_backward(j, s):
        cols = ds(j * LN, LN)
        d = drv[s, :, cols]
        g = gy[s, :, cols]
        lane_low = lane128 < hp
        zero = jnp.zeros_like(d)
        top, bottom = [], []
        t1 = t2 = t3 = None
        for hh, col in enumerate(columns_of(s, j)):
            row = cum_t[s, pl.ds(2 * j + hh, 1), :]
            dh = jnp.where(lane_low if hh == 0 else jnp.logical_not(lane_low), d, zero)
            m1 = dot_nt(dh[:half], g)
            m2 = dot_nt(dh[half:], g[half:])
            fa = jnp.exp(jnp.where(d_r <= d_c, row[:, :half] - col[:half], NEG))
            fb = jnp.exp(row[:, half:] - col[:half])
            fc = jnp.exp(jnp.where(d_r <= d_c, row[:, half:] - col[half:], NEG))
            top.append(
                jnp.concatenate(
                    [
                        (sco_t[s, :half, :half] * fa).astype(BF),
                        (sco_t[s, :half, half:] * fb).astype(BF),
                    ],
                    axis=1,
                )
            )
            bottom.append((sco_t[s, half:, half:] * fc).astype(BF))
            p1, p2, p3 = m1[:, :half] * fa, m1[:, half:] * fb, m2 * fc
            t1, t2, t3 = (p1, p2, p3) if hh == 0 else (t1 + p1, t2 + p2, t3 + p3)
        lo = dot(jnp.concatenate(top, axis=0), g)
        hi = dot(jnp.concatenate(bottom, axis=0), g[half:])
        return (
            cols, (t1, t2, t3), jnp.where(lane_low, lo[:half], lo[half:]),
            jnp.where(lane_low, hi[:half], hi[half:]),
        )

    sent = []

    def wide(a_ref, b_ref, rows, cols):
        t = dot(a_ref[rows, 0:length], b_ref[0, :, cols])
        for s in range(1, seqs):
            t = t + dot(a_ref[rows, s * length : (s + 1) * length], b_ref[s, :, cols])
        return t

    def from_out(i):
        return lambda part, r0, n: wide(
            nrt, cot, pl.ds(pl.multiple_of(i * dm + r0, 16), n),
            pl.ds(pl.multiple_of(part * (dm // 2), LN), dm // 2),
        )

    def from_columns(ref, base, w):
        return lambda part, r0, n: wide(
            nt, ref, pl.ds(pl.multiple_of(r0, 16), n),
            pl.ds(pl.multiple_of(base + part * w, LN), w),
        )

    def group_steps(g, produce, out_ref, row0, col0, part_cols):
        sb, rb, rr, acc, rx = bufs[5 * g : 5 * g + 5]
        total, w = sb.shape
        kind = sb.dtype
        tile = min(384, total // 2)

        def place(part):
            if part_cols:
                return out_ref.at[
                    pl.ds(row0, total), pl.ds(pl.multiple_of(col0 + part * w, LN), w)
                ]
            return out_ref.at[pl.ds(pl.multiple_of(part * total, 8), total), :]

        def copy_of(i, src, dst, peer):
            copy = pltpu.make_async_remote_copy(
                src_ref=src, dst_ref=dst, send_sem=ar_s.at[g, i], recv_sem=ar_r.at[g, i],
                device_id=peer, device_id_type=MESH,
            )
            copy.start()
            sent.append(copy)
            return copy

        def rows_at(start, n):
            return pl.ds(pl.multiple_of(start, 8), n)

        def tiles(count, body):
            if count == 1:
                body(0)
            else:
                lax.fori_loop(0, count, lambda i, _: (body(i), 0)[1], 0)

        def give(i):
            sb[rows_at(i * tile, tile), :] = produce(1 - core, i * tile, tile).astype(kind)

        tiles(total // tile, give)
        copy = copy_of(0, sb, rb, core_peer)
        sent.pop()
        yield
        copy.wait()
        bit, peer = stages[0]
        n = total // 2

        def own(i, start):
            r0 = start + i * tile
            return produce(core, r0, tile) + rb[rows_at(r0, tile), :].astype(F32)

        def give_half(i):
            sb[rows_at(i * tile, tile), :] = own(i, (1 - bit) * n).astype(kind)

        def keep_half(i):
            acc[rows_at(i * tile, tile), :] = own(i, bit * n)

        tiles(n // tile, give_half)
        copy = copy_of(1, sb.at[pl.ds(0, n)], rr.at[pl.ds(0, n)], peer)
        tiles(n // tile, keep_half)
        first_copy = copy
        if extras:
            sent.pop()
        yield
        copy.wait_recv()
        off1 = bit * n
        bit, peer = stages[1]
        base, n = n, n // 2
        gone, kept = (1 - bit) * n, bit * n
        sb[base : base + n, :] = (
            acc[rows_at(gone, n), :] + rr[rows_at(gone, n), :].astype(F32)
        ).astype(kind)
        copy = copy_of(2, sb.at[pl.ds(base, n)], rr.at[pl.ds(base, n)], peer)
        acc[rows_at(kept, n), :] += rr[rows_at(kept, n), :].astype(F32)
        yield
        copy.wait_recv()
        off2 = off1 + kept
        first, base, n = base, base + n, n // 4
        copies = []
        for d in (2, 1, 3):
            at = lax.rem(in_row + d, 4) * n
            here = base + (d - 1) * n
            sb[here : here + n, :] = (
                acc[rows_at(kept + at, n), :] + rr[rows_at(first + at, n), :].astype(F32)
            ).astype(kind)
            copies.append(
                copy_of(
                    2 + d, sb.at[pl.ds(here, n)], rr.at[pl.ds(here, n)], row_peers[d - 1]
                )
            )
        yield
        at = in_row * n
        value = acc[rows_at(kept + at, n), :] + rr[rows_at(first + at, n), :].astype(F32)
        for copy in copies:
            copy.wait_recv()
        for d in range(3):
            value = value + rr[base + d * n : base + (d + 1) * n, :].astype(F32)
        if extras:
            first_copy.wait_send()
        for e, peer in enumerate(extras):
            mine = value.astype(kind)
            sb[e * n : (e + 1) * n, :] = mine
            copy = pltpu.make_async_remote_copy(
                src_ref=sb.at[pl.ds(e * n, n)], dst_ref=rx.at[e], send_sem=ex_s.at[g, e],
                recv_sem=ex_r.at[g, e], device_id=peer, device_id_type=MESH,
            )
            copy.start()
            copy.wait()
            value = mine.astype(F32) + rx[e].astype(F32)
        mine = rows_at(off2 + at, n)
        rb[mine, :] = value.astype(kind)
        copies = [
            copy_of(5 + d, rb.at[mine], rb.at[mine], row_peers[d - 1]) for d in (2, 1, 3)
        ]
        yield
        for copy in copies:
            copy.wait_recv()
        for i, off, n, peer in (
            (9, off2, total // 4, stages[1][1]),
            (10, off1, total // 2, stages[0][1]),
        ):
            here = rb.at[rows_at(off, n)]
            copy = copy_of(i, here, here, peer)
            yield
            copy.wait_recv()
        here = place(core)
        copy = copy_of(11, rb, here, core_peer)
        local = pltpu.make_async_copy(rb, here, loc_sem.at[g])
        local.start()
        yield
        copy.wait_recv()
        local.wait()

    wide_w = dm // 2
    groups = [
        (0, from_out(0), go_h, 0, 0, True),
        (1, from_out(1), go_h, dm, 0, True),
        (2, from_columns(ggz, 0, wide_w), gw_h, 0, 0, True),
        (3, from_columns(ggz, dm, wide_w), gw_h, 0, dm, True),
        (4, from_columns(gy, 0, wide_w), gm_h, 0, 0, True),
        (5, from_columns(gy, dm, wide_w), gm_h, 0, dm, True),
        (6, from_columns(drv, 0, LN), gm_h, 0, di, True),
        (7, lambda part, r0, n: sm[part, pl.ds(pl.multiple_of(r0, 8), n), :], sm_h, 0, 0, False),
    ]

    plan = list(PLAN)
    live = {}
    slot_now = [seqs * nblk]

    def service(last=False):
        todo = [g for part in plan for g in part] if last else plan.pop(0)
        for g in todo:
            if g not in live:
                live[g] = group_steps(*groups[g])
            next(live[g], None)
            if slot_now[0] < b_slots:
                backward_slot(slot_now[0])
                slot_now[0] += 1

    for i in range(seqs * nblk // 2):
        s, i0 = (2 * i) // nblk, (2 * i) % nblk

        service()
        slot0 = slot_now[0] - i0

        def backward_body(b, _, s=s, slot0=slot0):
            made = [pair_backward(2 * b + h, s) for h in range(2)]
            t1, t2, t3 = (p + q for p, q in zip(made[0][1], made[1][1]))
            gsc[s, :half, :half] += t1
            gsc[s, :half, half:] += t2
            gsc[s, half:, half:] += t3
            for cols, _, lo, hi in made:
                z[s, :half, cols] = lo
                z[s, half:, cols] = hi
            backward_slot(slot0 + b)
            return 0

        lax.fori_loop(i0, i0 + 2, backward_body, 0)
        slot_now[0] += 2
    slots_alone(backward_slot, slot_now[0], b_slots)
    slot_now[0] = b_slots
    service()

    ginf[...] = jnp.zeros_like(ginf)
    hs_d[...] = jnp.zeros_like(hs_d)
    hs_g[...] = jnp.zeros_like(hs_g)
    bdh[...] = jnp.zeros_like(bdh)

    def head_sum(v, x):
        hi, lo = split2(v)
        return dot_nt(hi, x) + dot_nt(lo, x)

    def head_sum3(v, x):
        hi, mid, lo = split3(v)
        return dot_nt(hi, x) + dot_nt(mid, x) + dot_nt(lo, x)

    def gh_copy(b):
        cols = ds(b * BW, BW)
        return pltpu.make_async_remote_copy(
            src_ref=big.at[:, pl.ds(0, 8), cols], dst_ref=big.at[:, pl.ds(length, 8), cols],
            send_sem=gh_s.at[b], recv_sem=gh_r.at[b], device_id=prv, device_id_type=MESH,
        )

    @pl.when(jnp.logical_not(has_next))
    def _():
        big[:, length : length + 8, :] = jnp.zeros((seqs, 8, xbc), F32)

    def finish_block(b, s, ga):
        cols = ds(b * BW, BW)
        f = fil[s, :, cols]
        sg = sigmoid(f)
        gf = ga * (sg * (1.0 + f * (1.0 - sg)))
        big[s, 0:length, cols] = gf
        return jnp.sum(gf, axis=0, keepdims=True)

    def last_body(b, _):
        cols = ds(b * BW, BW)
        cb_sum = jnp.zeros((1, BW), F32)
        sk_sum = jnp.zeros((1, BW), F32)
        x = xx[:, cols]
        for s in range(seqs):
            lt = in_b[s * nblk + b]
            pr = prior_of(s, b)
            f = fil[s, :, cols]
            sg = sigmoid(f)
            sig = f * sg
            stw = dot(pst[s], x)
            gst = dot(infl[s], lt) * dot(ptl[s], x)
            gd = z[s, :, cols]
            gyf = gy[s, :, cols].astype(F32)
            sk_row = skw[0:1, cols]
            gg = gst + gd
            ga = sk_row * gyf + stw * gg
            t1 = stw * sig * gst
            dd = gyf * (y[s, :, cols] - sk_row * sig) - drv[s, :, cols].astype(F32) * gd - t1
            hs_d[s] += head_sum(dd, x)
            hs_g[s] += head_sum(sig * gg, x)
            bd = jnp.sum(t1, axis=0, keepdims=True) + dlast[s, 7:8, cols] * jnp.sum(
                lt.astype(F32) * pr, axis=0, keepdims=True
            )
            bdh[s] += head_sum3(jnp.broadcast_to(bd, (8, BW)), x)
            sk_sum = sk_sum + jnp.sum(gyf * sig, axis=0, keepdims=True)
            ginf[s] += dot_nt(scl[s, :, cols], lt)
            gf = ga * (sg * (1.0 + f * (1.0 - sg)))
            big[s, 0:length, cols] = gf
            cb_sum = cb_sum + jnp.sum(gf, axis=0, keepdims=True)
        small_put(SM_CONVB, b, cb_sum)
        sk_row_r[0:1, cols] = sk_sum

        @pl.when(has_prev)
        def _():
            gh_copy(b).start()

        return 0

    def mixed_body(b):
        cols = ds(b * BW, BW)

        @pl.when(has_next)
        def _():
            gh_copy(b).wait_recv()

        parts = []
        sums = [jnp.zeros((1, BW), F32) for _ in range(window + 1)]
        for s in range(seqs):
            gf = big[s, :, cols]
            rows = gf.shape[0]
            m = ext[s, :, cols].astype(F32)
            gm = jnp.zeros((length, BW), F32)
            for k in range(window + 1):
                shift = window - k
                moved = pltpu.roll(gf, rows - shift, 0) if shift else gf
                gm = gm + cw_r[k : k + 1, cols] * moved[:length]
                em = pltpu.roll(m, shift, 0) if shift else m
                sums[k] = sums[k] + jnp.sum(gf[:length] * em[hw:], axis=0, keepdims=True)
            parts.append(gm.astype(BF))
        for k in range(window + 1):
            small_put(SM_CONVW + k * (xbc // LN), b, sums[k])
        return parts

    def mixed_loop(b, _):
        cols = ds(b * BW, BW)
        for s, part in enumerate(mixed_body(b)):
            gy[s, :, cols] = part
        return 0

    third = nblk // 2
    lax.fori_loop(0, third, last_body, 0)
    service()
    lax.fori_loop(0, third, mixed_loop, 0)
    service()
    lax.fori_loop(third, nblk, last_body, 0)
    service()

    cb_sum = jnp.zeros((1, BW), F32)
    for s in range(seqs):
        gst_bf = gsc[s].astype(BF)
        gi = ginf[s] + dot(gst_bf, outf[s])
        go = gout[s] + dot(gst_bf.T, infl[s])
        cb_sum = cb_sum + finish_block(nblk, s, jnp.concatenate([gi, go], axis=1))
    small_put(SM_CONVB, nblk, cb_sum)

    @pl.when(has_prev)
    def _():
        gh_copy(nblk).start()

    lax.fori_loop(third, nblk, mixed_loop, 0)
    service()
    for s, part in enumerate(mixed_body(nblk)):
        drv[s, :, 0:BW] = part
    service()

    row_i = lax.broadcasted_iota(jnp.int32, (length, LN), 0)
    glr = jnp.zeros((1, LN), F32)
    gsb = jnp.zeros((1, LN), F32)
    grl = []
    for s in range(seqs):
        gc = hs_d[s] + jnp.where(row_i == length - 1, bdh[s, 0:1], 0.0)
        terms = dot3(tri[1], gc)
        gst = hs_g[s] + terms * rates3
        glr = glr + jnp.sum(terms * st[s], axis=0, keepdims=True)
        graw = gst * sigmoid(sraw[s] + bias3)
        gsb = gsb + jnp.sum(graw, axis=0, keepdims=True)
        grl.append(jnp.where(lane128 < heads, graw, 0.0).astype(BF))
    sk_h = head_sum3(jnp.broadcast_to(sk_row_r[0:1, :], (8, di)), xx[...])
    small_one(SM_HEADS, gsb)
    small_one(SM_HEADS + 1, rates3 * glr)
    small_one(SM_HEADS + 2, sk_h[0:1])
    stepg = dot(grl[0].T, ne[0, hw:, :])
    for s in range(1, seqs):
        stepg = stepg + dot(grl[s].T, ne[s, hw:, :])
    for i in range(dm // LN):
        row = SM_STEP + 24 * i
        for lo, hi in ((row, min(row + 24, 128)), (max(row, 128), row + 24)):
            if lo < hi:
                sm[lo // 128, lo % 128 : lo % 128 + hi - lo, :] = stepg[
                    lo - row : hi - row, i * LN : (i + 1) * LN
                ]

    service()
    for s in range(seqs):
        for i in range(dm // BW):
            cols = slice(i * BW, (i + 1) * BW)
            pj = dot(nrm[s], wo[:, cols])
            res_r[s, :, cols] = (tok[s, :, cols].astype(F32) + pj).astype(BF)
        service()
    res_copy = pltpu.make_async_copy(res_r, res_h, tok_sem.at[0])
    res_copy.start()
    for s in range(seqs):
        for i in range(dm // BW):
            cols = slice(i * BW, (i + 1) * BW)
            gn[s, :, cols] = (
                dot_nt(gy[s], wm[cols, :di])
                + dot_nt(drv[s, :, 0:BW], wm[cols, di:])
                + dot_nt(ggz[s], wg[cols, :])
                + dot_nt(grl[s], ws3[cols])
            )
        service()

    @pl.when(has_next)
    def _():
        halo_copy.wait_send()

    def token_body(i, sums):
        for s in range(seqs):
            rows = ds(i * 16, 16)
            v = tok[s, rows, :].astype(F32)
            inv = lax.rsqrt(jnp.mean(v * v, axis=-1, keepdims=True) + EPSILON)
            unit = v * inv
            gr = gn[s, rows, :]
            sums = sums + jnp.sum(gr * unit, axis=0, keepdims=True)
            q = gr * gain
            back = inv * (q - unit * jnp.mean(q * unit, axis=-1, keepdims=True))
            tok[s, rows, :] = (cot[s, rows, :].astype(F32) + back).astype(BF)
        return sums

    n_sum = jnp.zeros((1, dm), F32)
    for i in range(4):
        n_sum = lax.fori_loop(
            i * (length // 64), (i + 1) * (length // 64), token_body, n_sum, unroll=2
        )
        service()
    for i in range(dm // LN):
        small_one(SM_NORM + i, n_sum[:, i * LN : (i + 1) * LN])
    tg_copy = pltpu.make_async_copy(tok, tg_h, tok_sem.at[1])
    tg_copy.start()
    service(last=True)
    res_copy.wait()
    tg_copy.wait()
    for copy in sent:
        copy.wait_send()

    def drain(q, _):
        @pl.when(has_prev)
        def _():
            backward_copy(q).wait_send()

        return 0

    lax.fori_loop(0, seqs * nblk, drain, 0)

    def drain_halo(b, _):
        @pl.when(has_prev)
        def _():
            gh_copy(b).wait_send()

        return 0

    lax.fori_loop(0, xbc // BW, drain_halo, 0)


def on_device(nctx, *args):
    tokens, norm_gain, wg, wm, ws, conv_w, conv_b, sb, lr, sk, gg, wo, cot = args
    seqs, length, dm = tokens.shape
    di = wg.shape[1]
    xbc = wm.shape[1]
    heads = ws.shape[1]
    nst = (xbc - di) // 2
    nchunk = di // LN
    nblk = di // BW
    hw = 16
    vm = pltpu.VMEM
    any_spec = pl.BlockSpec(memory_space=pl.ANY)
    vm_spec = pl.BlockSpec(memory_space=vm)
    dma = pltpu.SemaphoreType.DMA
    extras = max(1, (nctx // 16).bit_length())
    bufs = []
    for rows, w, kind in [(dm, dm // 2, BF)] * 6 + [(dm, LN, BF), (128, LN, F32)]:
        bufs += [vm((rows, w), kind)] * 3 + [vm((rows // 2, w), F32)]
        bufs += [vm((extras, rows // 16, w), kind) if nctx > 8 else vm((1, 16, LN), kind)]
    out = pl.pallas_call(
        functools.partial(layer_kernel, nctx),
        out_shape=(
            jax.ShapeDtypeStruct(tokens.shape, BF),
            jax.ShapeDtypeStruct(tokens.shape, BF),
            jax.ShapeDtypeStruct((di, dm), BF),
            jax.ShapeDtypeStruct((dm, di), BF),
            jax.ShapeDtypeStruct((dm, xbc), BF),
            jax.ShapeDtypeStruct((256, LN), F32),
        ),
        in_specs=[any_spec, vm_spec, any_spec, any_spec] + [vm_spec] * 7 + [any_spec] * 2,
        out_specs=(any_spec,) * 6,
        scratch_shapes=[
            vm((seqs, length, dm), BF),
            vm((seqs, length, dm), BF),
            vm((dm, di), BF),
            vm((dm, xbc), BF),
            vm((di, dm), BF),
            vm((seqs, hw, dm), BF),
            vm((seqs, hw + length, dm), BF),
            vm((dm, seqs * length), BF),
            vm((seqs, hw + length, xbc), BF),
            vm((seqs, length, xbc), F32),
            vm((seqs, length, di), BF),
            vm((seqs, length, di), BF),
            vm((seqs, length, di), F32),
            vm((seqs, length, di), F32),
            vm((seqs, length + 8, xbc), F32),
            vm((seqs, length, di), BF),
            vm((seqs, length, di), BF),
            vm((seqs, length, di), BF),
            vm((di, seqs * length), BF),
            vm((seqs, length, LN), F32),
            vm((seqs, length, LN), F32),
            vm((seqs, length, dm), F32),
            vm((seqs * nchunk, nst, LN), F32),
            vm((seqs * nchunk, nst, LN), F32),
            vm((seqs * nblk, nst, BW), BF),
            vm((seqs * nblk, nst, BW), BF),
            vm((seqs, length, LN), F32),
            vm((seqs, length, LN), F32),
            vm((seqs, length, LN), F32),
            vm((seqs, LN, length), F32),
            vm((seqs, length, LN), BF),
            vm((seqs, length, LN), BF),
            vm((seqs, length, LN), BF),
            vm((seqs, 8, di), F32),
            vm((seqs, length, nst), BF),
            vm((seqs, length, nst), BF),
            vm((seqs, nst, length), BF),
            vm((seqs, nst, length), BF),
            vm((seqs, length, length), F32),
            vm((seqs, length, length), F32),
            vm((LN, di), BF),
            vm((2, length, length), BF),
            vm((seqs, length, LN), F32),
            vm((seqs, length, LN), F32),
            vm((seqs, 8, LN), F32),
            vm((seqs, length, dm), BF),
            dma((2,)),
            vm((8, di), F32),
            vm((2, 128, LN), F32),
            vm((8, di), F32),
            bufs,
            dma((8, 12)), dma((8, 12)), dma((8,)), dma((8, extras)), dma((8, extras)),
            dma((5,)), dma, dma,
            dma((seqs * nchunk,)), dma((seqs * nchunk,)), dma((seqs * nblk,)), dma((seqs * nblk,)),
            dma((xbc // BW,)), dma((xbc // BW,)),
        ],
        compiler_params=pltpu.CompilerParams(
            collective_id=0, has_side_effects=True, vmem_limit_bytes=65200 * 1024
        ),
    )(*args[:4], ws.T, *args[5:])
    res, tg, g_out, g_gate, g_mixer, small = out
    gate0 = xbc // LN
    norm0 = gate0 + di // LN
    convw0 = norm0 + dm // LN
    taps = conv_w.shape[0]
    heads0 = convw0 + taps * (xbc // LN)
    step0 = -(-(heads0 + 3) // 8) * 8

    def finish(res_i, tg_i, go_i, gw_i, gm_i, sm_i, *outs):
        res_o, tg_o, ng_o, gw_o, gm_o, st_o, cw_o, cb_o, sb_o, lr_o, sk_o, gg_o, go_o = outs
        res_o[...] = res_i[...]
        tg_o[...] = tg_i[...]
        go_o[...] = go_i[...].astype(F32)
        gw_o[...] = gw_i[...].astype(F32)
        gm_o[...] = gm_i[...].astype(F32)

        @pl.when(pl.program_id(0) == 0)
        def _():
            for ref, first, count in (
                (cb_o, 0, xbc // LN), (gg_o, gate0, di // LN), (ng_o, norm0, dm // LN),
            ):
                for i in range(count):
                    ref[pl.ds(i * LN, LN)] = sm_i[first + i, :]
            for k in range(taps):
                for i in range(xbc // LN):
                    r = convw0 + k * (xbc // LN) + i
                    cw_o[k : k + 1, i * LN : (i + 1) * LN] = sm_i[r : r + 1, :]
            for i, ref in enumerate((sb_o, lr_o, sk_o)):
                ref[...] = sm_i[heads0 + i, 0:heads]
            for i in range(dm // LN):
                r = step0 + heads * i
                st_o[:, i * LN : (i + 1) * LN] = sm_i[r : r + heads, :]

    steps = 4

    def rows_of(a, dim=0):
        block = tuple(n // steps if i == dim else n for i, n in enumerate(a.shape))
        return pl.BlockSpec(block, lambda t: tuple(t if i == dim else 0 for i in range(a.ndim)))

    def whole(*shape):
        return pl.BlockSpec(shape, lambda t: (0,) * len(shape))

    def shape(*dims):
        return jax.ShapeDtypeStruct(dims, F32)

    small_shapes = {
        2: (dm,), 5: (heads, dm), 6: (taps, xbc), 7: (xbc,), 8: (heads,), 9: (heads,),
        10: (heads,), 11: (di,),
    }
    big_outs = {0: res, 1: tg, 3: g_gate, 4: g_mixer, 12: g_out}
    final = pl.pallas_call(
        finish,
        grid=(steps,),
        in_specs=[
            rows_of(res, 1), rows_of(tg, 1), rows_of(g_out), rows_of(g_gate), rows_of(g_mixer),
            whole(*small.shape),
        ],
        out_specs=[
            rows_of(big_outs[i], 1 if i < 2 else 0) if i in big_outs else whole(*small_shapes[i])
            for i in range(13)
        ],
        out_shape=[
            jax.ShapeDtypeStruct(big_outs[i].shape, BF if i < 2 else F32)
            if i in big_outs else shape(*small_shapes[i])
            for i in range(13)
        ],
        compiler_params=pltpu.CompilerParams(vmem_limit_bytes=62 * 1024 * 1024),
    )(res, tg, g_out, g_gate, g_mixer, small)
    final = list(final)
    final[5] = final[5].T
    return tuple(final)


def solution(mesh):
    tok = P("seq", "ctx", None)
    return jax.shard_map(
        functools.partial(on_device, mesh.shape["ctx"]),
        mesh=mesh,
        in_specs=(tok,) + (P(),) * 11 + (tok,),
        out_specs=(tok, tok) + (P(),) * 11,
        check_vma=False,
    )
```

```python
import functools

import jax
import jax.numpy as jnp
from jax import lax
from jax.experimental import pallas as pl
from jax.experimental.pallas import tpu as pltpu
from jax.sharding import PartitionSpec as P

MESH = pl.DeviceIdType.MESH
BF = jnp.bfloat16
F32 = jnp.float32
EPSILON = 1e-05
BW = 256
LN = 128
SKEW = 2
PLAN = (
    (0, 2, 3, 0, 2, 3, 1),
    (),
    (1,),
    (),
    (0,),
    (),
    (2,),
    (3,),
    (4, 0, 2, 1, 4),
    (3,),
    (0, 5, 4, 2, 1, 5),
    (6, 3),
    (6,),
    (0, 4),
    (),
    (),
    (2, 5),
    (6,),
    (1, 0),
    (),
    (),
    (7, 3, 7, 5, 4, 7, 3, 6, 1, 2, 5, 7, 4, 6, 1, 7, 5, 4, 6, 2, 2, 3, 3, 7, 5, 0, 0, 4, 1,
    7, 6, 4, 5, 5, 6, 7, 7, 6, 1),
)


def dot(a, b):
    return jnp.dot(a, b, preferred_element_type=F32)


def dot_nt(a, b):
    return lax.dot_general(a, b, (((1,), (1,)), ((), ())), preferred_element_type=F32)


def split2(v):
    hi = v.astype(BF)
    return hi, (v - hi.astype(F32)).astype(BF)


def split3(v):
    hi = v.astype(BF)
    rest = v - hi.astype(F32)
    mid = rest.astype(BF)
    return hi, mid, (rest - mid.astype(F32)).astype(BF)


def dot3(a, v):
    hi, mid, lo = split3(v)
    return dot(a, hi) + dot(a, mid) + dot(a, lo)


def pieces3(v):
    lane = lax.broadcasted_iota(jnp.int32, v.shape, 1)
    hi, mid, lo = split3(v)
    z = jnp.zeros_like(v)
    return jnp.where(
        lane < 32,
        hi.astype(F32),
        jnp.where(lane < 64, mid.astype(F32), jnp.where(lane < 96, lo.astype(F32), z)),
    ).astype(BF)


def sigmoid(v):
    return 1.0 / (1.0 + jnp.exp(-v))


def ds(start, size):
    return pl.ds(pl.multiple_of(start, size), size)


def layer_kernel(
    nctx,
    tok_h, ng_r, wg_h, wm_h, ws_r, cw_r, cb_r, sb_r, lr_r, sk_r, gg_r, wo_h, cot_h,
    res_h, tg_h, go_h, gw_h, gm_h, sm_h,
    tok, cot, wg, wm, wo, halo, ne, nt, ext, fil, drv, scl, y, z, big, gy, ggz, nrm, nrt,
    acc_a, acc_b, gn, sum_s, in_f, out_b, in_b, sraw, st, cum, cum_t, pst, ptl, pdc,
    dlast, infl, outf, inf_t, outf_t, sco, sco_t, xx, tri, hs_d, hs_g, bdh,
    res_r, tok_sem, sm, sk_row_r, bufs, ar_s, ar_r, loc_sem, ex_s, ex_r,
    in_sem, halo_s, halo_r, fs_s, fs_r, bs_s, bs_r, gh_s, gh_r,
):
    seqs, length, dm = tok.shape
    di = wg.shape[1]
    xbc = wm.shape[1]
    heads = ws_r.shape[0]
    hp = di // heads
    nst = (xbc - di) // 2
    window = cw_r.shape[0] - 1
    nblk = di // BW
    gsc, gout, ginf = sco, acc_a, acc_b
    nchunk = di // LN
    hw = 16
    seq = lax.axis_index("seq")
    ctx = lax.axis_index("ctx")
    has_prev = ctx > 0
    has_next = ctx < nctx - 1
    prv = (seq, ctx - 1)
    nxt = (seq, ctx + 1)

    barrier = pltpu.get_barrier_semaphore()

    @pl.when(has_prev)
    def _():
        pl.semaphore_signal(barrier, inc=1, device_id=prv, device_id_type=MESH)

    @pl.when(has_next)
    def _():
        pl.semaphore_signal(barrier, inc=1, device_id=nxt, device_id_type=MESH)

    loads = [
        pltpu.make_async_copy(a, b, in_sem.at[i])
        for i, (a, b) in enumerate(
            ((tok_h, tok), (wm_h, wm), (cot_h, cot), (wo_h, wo), (wg_h, wg))
        )
    ]
    for copy in loads[:2]:
        copy.start()

    core = lax.rem(ctx, 2)

    def flipped(index, mask):
        bit = lax.rem(index // mask, 2)
        return bit, index + mask - 2 * mask * bit

    core_peer = (seq, flipped(ctx, 1)[1])
    stages = []
    for mask in (1 + core, 2 - core):
        bit, other = flipped(seq, mask)
        stages.append((bit, (other, ctx)))
    in_row = lax.rem(ctx // 2, 4)
    row_peers = [(seq, ctx + 2 * (lax.rem(in_row + d, 4) - in_row)) for d in (1, 2, 3)]
    extras = []
    mask = 8
    while mask < nctx:
        extras.append((seq, flipped(ctx, mask)[1]))
        mask *= 2
    peers = [peer for _, peer in stages] + row_peers + extras
    for peer in peers:
        pl.semaphore_signal(barrier, inc=1, device_id=peer, device_id_type=MESH)
    lane128 = lax.broadcasted_iota(jnp.int32, (1, LN), 1)
    r_i = lax.broadcasted_iota(jnp.int32, (LN, di), 0)
    c_i = lax.broadcasted_iota(jnp.int32, (LN, di), 1)
    first = jnp.bitwise_and(r_i, 31) * hp
    xx[...] = jnp.where((c_i >= first) & (c_i < first + hp) & (r_i < 96), 1.0, 0.0).astype(BF)
    t_r = lax.broadcasted_iota(jnp.int32, (length, length), 0)
    t_c = lax.broadcasted_iota(jnp.int32, (length, length), 1)
    tri[...] = jnp.where(t_r >= t_c, 1.0, 0.0).astype(BF)
    k_i = lax.broadcasted_iota(jnp.int32, (heads, LN), 0)
    l_i = lax.broadcasted_iota(jnp.int32, (heads, LN), 1)
    rep = jnp.where((l_i % 32 == k_i) & (l_i < 96), 1.0, 0.0)

    def replicated(row_ref):
        row = jnp.broadcast_to(row_ref[...].reshape(1, heads), (8, heads))
        hi, mid, lo = split3(row)
        r = rep.astype(BF)
        return (dot(hi, r) + dot(mid, r) + dot(lo, r))[0:1]

    ws3 = dot(ws_r[...].T, rep.astype(BF)).astype(BF)
    bias3 = replicated(sb_r)
    rates3 = -jnp.exp(replicated(lr_r))
    sk8 = jnp.broadcast_to(replicated(sk_r), (8, LN))
    sk_row_r[...] = dot(pieces3(sk8), xx[...])

    pl.semaphore_wait(
        barrier, has_prev.astype(jnp.int32) + has_next.astype(jnp.int32) + len(peers)
    )
    loads[0].wait()
    for copy in loads[2:]:
        copy.start()

    halo_copy = pltpu.make_async_remote_copy(
        src_ref=tok.at[:, pl.ds(length - hw, hw), :], dst_ref=halo, send_sem=halo_s,
        recv_sem=halo_r, device_id=nxt, device_id_type=MESH,
    )

    @pl.when(has_next)
    def _():
        halo_copy.start()

    @pl.when(jnp.logical_not(has_prev))
    def _():
        halo[...] = jnp.zeros_like(halo)
        in_f[...] = jnp.zeros_like(in_f)

    @pl.when(jnp.logical_not(has_next))
    def _():
        in_b[...] = jnp.zeros_like(in_b)

    gain = ng_r[...].reshape(1, dm)

    def norm_rows(rows):
        v = rows.astype(F32)
        inv = lax.rsqrt(jnp.mean(v * v, axis=-1, keepdims=True) + EPSILON)
        return ((v * inv) * gain).astype(BF)

    for s in range(seqs):

        def norm_body(i, _, s=s):
            ne[s, ds(hw + i * 16, 16), :] = norm_rows(tok[s, ds(i * 16, 16), :])
            return 0

        lax.fori_loop(0, length // 16, norm_body, 0, unroll=2)

    for s in range(seqs):
        raw = dot(ne[s, pl.ds(hw, length), :], ws3)
        sraw[s] = raw
        step = jax.nn.softplus(raw + bias3)
        st[s] = step
        cu = dot3(tri[...], step * rates3)
        cum[s] = cu
        cum_t[s] = cu.T
        last = cu[length - 1 : length]
        pst[s] = pieces3(step)
        ptl[s] = pieces3(jnp.exp(last - cu))
        dec = jnp.exp(cu)
        pdc[s] = pieces3(dec)
        dlast[s] = dot(pieces3(dec[length - 8 :]), xx[...])

    @pl.when(has_prev)
    def _():
        halo_copy.wait_recv()

    for s in range(seqs):
        ne[s, 0:hw, :] = norm_rows(halo[s])

    loads[1].wait()

    def filter_block(b, s):
        cols = ds(b * BW, BW)
        m_bf = dot(ne[s], wm[:, cols]).astype(BF)
        m = m_bf.astype(F32)
        f = cb_r[cols].reshape(1, BW)
        for k in range(window + 1):
            shift = window - k
            moved = pltpu.roll(m, shift, 0) if shift else m
            f = f + cw_r[k : k + 1, cols] * moved[hw:]
        return cols, m_bf, f

    for s in range(seqs):
        cols, m_bf, f = filter_block(nblk, s)
        ext[s, :, cols] = m_bf
        fil[s, :, cols] = f
        act = f * sigmoid(f)
        i_bf = act[:, :nst].astype(BF)
        o_bf = act[:, nst:].astype(BF)
        infl[s] = i_bf
        outf[s] = o_bf
        inf_t[s] = i_bf.T
        outf_t[s] = o_bf.T

    def forward_copy(q):
        return pltpu.make_async_remote_copy(
            src_ref=sum_s.at[q], dst_ref=in_f.at[q], send_sem=fs_s.at[q],
            recv_sem=fs_r.at[q], device_id=nxt, device_id_type=MESH,
        )

    def backward_copy(q):
        return pltpu.make_async_remote_copy(
            src_ref=out_b.at[q], dst_ref=in_b.at[q], send_sem=bs_s.at[q],
            recv_sem=bs_r.at[q], device_id=prv, device_id_type=MESH,
        )

    f_skew = SKEW * ctx
    b_skew = SKEW * (nctx - 1 - ctx)
    f_slots = seqs * nchunk + SKEW * (nctx - 1)
    b_slots = seqs * nblk + SKEW * (nctx - 1)

    def forward_slot(slot):
        q = slot - f_skew

        @pl.when((q >= 0) & (q < seqs * nchunk))
        def _():
            @pl.when(has_prev)
            def _():
                forward_copy(q).wait_recv()

            @pl.when(has_next)
            def _():
                row = dlast[q // nchunk, 7:8, ds(lax.rem(q, nchunk) * LN, LN)]
                sum_s[q] = row * in_f[q] + sum_s[q]
                forward_copy(q).start()

    def backward_slot(slot):
        q = slot - b_skew

        @pl.when((q >= 0) & (q < seqs * nblk))
        def _():
            @pl.when(has_next)
            def _():
                backward_copy(q).wait_recv()

            @pl.when(has_prev)
            def _():
                row = dlast[q // nblk, 7:8, ds(lax.rem(q, nblk) * BW, BW)]
                add = jnp.concatenate([sum_s[2 * q], sum_s[2 * q + 1]], axis=1)
                out_b[q] = (row * in_b[q].astype(F32) + add).astype(BF)
                backward_copy(q).start()

    def slots_alone(one, first, last):
        lax.fori_loop(first, last, lambda t, _: (one(t), 0)[1], 0)

    for s in range(seqs):

        def signal_body(i, _, s=s):
            made = []
            for b in (2 * i, 2 * i + 1):
                cols, m_bf, f = filter_block(b, s)
                sig = f * sigmoid(f)
                x = xx[:, cols]
                dr = sig * dot(pst[s], x)
                sc = (dr * dot(ptl[s], x)).astype(BF)
                made.append(
                    (b, cols, m_bf, f, sk_row_r[7:8, cols] * sig, dr.astype(BF), sc, dot(inf_t[s], sc))
                )
            for b, cols, m_bf, f, sk_sig, dr, sc, summ in made:
                ext[s, :, cols] = m_bf
                fil[s, :, cols] = f
                y[s, :, cols] = sk_sig
                drv[s, :, cols] = dr
                scl[s, :, cols] = sc
                sum_s[s * nchunk + 2 * b] = summ[:, :LN]
                sum_s[s * nchunk + 2 * b + 1] = summ[:, LN:]
            for slot in (2 * i, 2 * i + 1):
                forward_slot(s * nblk + slot)
            return 0

        lax.fori_loop(0, nblk // 2, signal_body, 0)

    SM_CONVB = 0
    SM_GATE = SM_CONVB + xbc // LN
    SM_NORM = SM_GATE + di // LN
    SM_CONVW = SM_NORM + dm // LN
    SM_HEADS = SM_CONVW + (window + 1) * (xbc // LN)
    SM_STEP = -(-(SM_HEADS + 3) // 8) * 8
    sm[...] = jnp.zeros_like(sm)

    def small_one(row, value):
        sm[row // 128, pl.ds(row % 128, 1), :] = value

    def small_put(base, b, value):
        small_one(base + 2 * b, value[:, :LN])
        small_one(base + 2 * b + 1, value[:, LN:])

    half = length // 2
    d_r = lax.broadcasted_iota(jnp.int32, (half, half), 0)
    d_c = lax.broadcasted_iota(jnp.int32, (half, half), 1)
    NEG = -1e30

    def columns_of(s, j):
        moved = pltpu.roll(cum[s], lax.rem(LN - 2 * j, LN), 1)
        return moved[:, 0:1], moved[:, 1:2]

    def pair_forward(j, s):
        cols = ds(j * LN, LN)
        d = drv[s, :, cols]
        lane_low = lane128 < hp
        top, bottom = [], []
        for hh, col in enumerate(columns_of(s, j)):
            row = cum_t[s, pl.ds(2 * j + hh, 1), :]
            fa = jnp.exp(jnp.where(d_r >= d_c, col[:half] - row[:, :half], NEG))
            fb = jnp.exp(col[half:] - row[:, :half])
            fc = jnp.exp(jnp.where(d_r >= d_c, col[half:] - row[:, half:], NEG))
            top.append((sco[s, :half, :half] * fa).astype(BF))
            bottom.append(
                jnp.concatenate(
                    [
                        (sco[s, half:, :half] * fb).astype(BF),
                        (sco[s, half:, half:] * fc).astype(BF),
                    ],
                    axis=1,
                )
            )
        lo = dot(jnp.concatenate(top, axis=0), d[:half])
        hi = dot(jnp.concatenate(bottom, axis=0), d)
        return (
            y[s, :half, cols] + jnp.where(lane_low, lo[:half], lo[half:]),
            y[s, half:, cols] + jnp.where(lane_low, hi[:half], hi[half:]),
        )

    loads[2].wait()
    loads[3].wait()
    loads[4].wait()

    for s in range(seqs):
        for b in range(dm // BW):
            nt[b * BW : (b + 1) * BW, s * length : (s + 1) * length] = ne[
                s, hw : hw + length, b * BW : (b + 1) * BW
            ].T

    for s in range(seqs):
        sco[s] = dot_nt(outf[s], infl[s])
        sco_t[s] = dot_nt(infl[s], outf[s])

    for s in range(seqs):

        def forward_body(i, _, s=s):
            made = []
            for b in (2 * i, 2 * i + 1):
                cols = ds(b * BW, BW)
                made.append(
                    (
                        b, cols, dot_nt(cot[s], wo[cols, :]),
                        dot(ne[s, hw : hw + length, :], wg[:, cols]),
                        [pair_forward(2 * b + h, s) for h in range(2)],
                    )
                )
            for b, cols, g, zz, pairs in made:
                big[s, 0:length, cols] = g
                z[s, :, cols] = zz
                for h, (lo, hi) in enumerate(pairs):
                    lanes = ds((2 * b + h) * LN, LN)
                    y[s, :half, lanes] = lo
                    y[s, half:, lanes] = hi
            for slot in (2 * i, 2 * i + 1):
                forward_slot((seqs + s) * nblk + slot)
            return 0

        lax.fori_loop(0, nblk // 2, forward_body, 0)

    acc_a[...] = jnp.zeros_like(acc_a)
    acc_b[...] = jnp.zeros_like(acc_b)

    def prior_of(s, b):
        return jnp.concatenate(
            [in_f[s * nchunk + 2 * b], in_f[s * nchunk + 2 * b + 1]], axis=1
        )

    def gate_blocks(blocks, s):
        made = []
        a_sum = c_sum = None
        for b in blocks:
            cols = ds(b * BW, BW)
            phi, plo = split2(prior_of(s, b))
            out = (dot(outf[s], phi) + dot(outf[s], plo)) * dot(pdc[s], xx[:, cols])
            yy = y[s, :, cols] + out
            zz = z[s, :, cols]
            gated = yy * (zz * sigmoid(zz))
            q = big[s, 0:length, cols] * gg_r[cols].reshape(1, BW)
            a = gated * gated
            c = q * gated
            a, c = a[:, :LN] + a[:, LN:], c[:, :LN] + c[:, LN:]
            a_sum, c_sum = (a, c) if a_sum is None else (a_sum + a, c_sum + c)
            made.append((cols, yy))
        for cols, yy in made:
            y[s, :, cols] = yy
        acc_a[s] += a_sum
        acc_b[s] += c_sum

    def grad_blocks(blocks, s, iv, mean):
        made = []
        g_out = None
        for b in blocks:
            cols = ds(b * BW, BW)
            yy = y[s, :, cols]
            zz = z[s, :, cols]
            sg = sigmoid(zz)
            act = zz * sg
            unit = (yy * act) * iv
            gain_row = gg_r[cols].reshape(1, BW)
            g = big[s, 0:length, cols]
            no = (unit * gain_row).astype(BF)
            gain_sum = jnp.sum(g * unit, axis=0, keepdims=True)
            gr = iv * (g * gain_row - unit * mean)
            gyb = (gr * act).astype(BF)
            gzb = (gr * yy * (sg * (1.0 + zz * (1.0 - sg)))).astype(BF)
            w = gyb.astype(F32) * dot(pdc[s], xx[:, cols])
            whi, wlo = split2(w)
            gp = dot(outf_t[s], whi) + dot(outf_t[s], wlo)
            phi, plo = split2(prior_of(s, b))
            go = dot_nt(whi, phi) + (dot_nt(wlo, phi) + dot_nt(whi, plo))
            g_out = go if g_out is None else g_out + go
            made.append((b, cols, no, no.T, gain_sum, gyb, gzb, gp))
        for b, cols, no, no_t, gain_sum, gyb, gzb, gp in made:
            nrm[s, :, cols] = no
            nrt[cols, s * length : (s + 1) * length] = no_t
            sk_row_r[1 + s : 2 + s, cols] = gain_sum
            gy[s, :, cols] = gyb
            ggz[s, :, cols] = gzb
            sum_s[s * nchunk + 2 * b] = gp[:, :LN]
            sum_s[s * nchunk + 2 * b + 1] = gp[:, LN:]
        gout[s] += g_out

    first_done = f_slots - nchunk * (seqs - 1)
    slots_alone(forward_slot, seqs * nchunk, first_done)
    for s in range(seqs):
        slot0 = first_done + s * nchunk

        def passing(i, s=s, slot0=slot0):
            if s < seqs - 1:
                forward_slot(slot0 + i)
            else:
                backward_slot(i)

        def gate_body(i, _, s=s, passing=passing):
            gate_blocks((2 * i, 2 * i + 1), s)
            passing(2 * i)
            passing(2 * i + 1)
            return 0

        lax.fori_loop(0, nblk // 2, gate_body, 0)
        iv = lax.rsqrt(jnp.sum(acc_a[s], axis=-1, keepdims=True) / di + EPSILON)
        mean = iv * jnp.sum(acc_b[s], axis=-1, keepdims=True) / di
        gout[s] = jnp.zeros_like(gout[s])

        def sent_forward(c, _, s=s):
            @pl.when(has_next)
            def _():
                forward_copy(s * nchunk + c).wait_send()

            return 0

        lax.fori_loop(0, nchunk, sent_forward, 0)

        def grad_body(i, _, s=s, iv=iv, mean=mean, passing=passing):
            grad_blocks((2 * i, 2 * i + 1), s, iv, mean)
            passing(nblk + 2 * i)
            passing(nblk + 2 * i + 1)
            return 0

        lax.fori_loop(0, nblk // 2, grad_body, 0)

    def gate_gain_body(b, _):
        cols = ds(b * BW, BW)
        total = sk_row_r[1:2, cols]
        for s in range(1, seqs):
            total = total + sk_row_r[1 + s : 2 + s, cols]
        small_put(SM_GATE, b, total)
        return 0

    lax.fori_loop(0, nblk, gate_gain_body, 0)

    gsc[...] = jnp.zeros_like(gsc)

    def pair_backward(j, s):
        cols = ds(j * LN, LN)
        d = drv[s, :, cols]
        g = gy[s, :, cols]
        lane_low = lane128 < hp
        zero = jnp.zeros_like(d)
        top, bottom = [], []
        t1 = t2 = t3 = None
        for hh, col in enumerate(columns_of(s, j)):
            row = cum_t[s, pl.ds(2 * j + hh, 1), :]
            dh = jnp.where(lane_low if hh == 0 else jnp.logical_not(lane_low), d, zero)
            m1 = dot_nt(dh[:half], g)
            m2 = dot_nt(dh[half:], g[half:])
            fa = jnp.exp(jnp.where(d_r <= d_c, row[:, :half] - col[:half], NEG))
            fb = jnp.exp(row[:, half:] - col[:half])
            fc = jnp.exp(jnp.where(d_r <= d_c, row[:, half:] - col[half:], NEG))
            top.append(
                jnp.concatenate(
                    [
                        (sco_t[s, :half, :half] * fa).astype(BF),
                        (sco_t[s, :half, half:] * fb).astype(BF),
                    ],
                    axis=1,
                )
            )
            bottom.append((sco_t[s, half:, half:] * fc).astype(BF))
            p1, p2, p3 = m1[:, :half] * fa, m1[:, half:] * fb, m2 * fc
            t1, t2, t3 = (p1, p2, p3) if hh == 0 else (t1 + p1, t2 + p2, t3 + p3)
        lo = dot(jnp.concatenate(top, axis=0), g)
        hi = dot(jnp.concatenate(bottom, axis=0), g[half:])
        return (
            cols, (t1, t2, t3), jnp.where(lane_low, lo[:half], lo[half:]),
            jnp.where(lane_low, hi[:half], hi[half:]),
        )

    sent = []

    def wide(a_ref, b_ref, rows, cols):
        t = dot(a_ref[rows, 0:length], b_ref[0, :, cols])
        for s in range(1, seqs):
            t = t + dot(a_ref[rows, s * length : (s + 1) * length], b_ref[s, :, cols])
        return t

    def from_out(i):
        return lambda part, r0, n: wide(
            nrt, cot, pl.ds(pl.multiple_of(i * dm + r0, 16), n),
            pl.ds(pl.multiple_of(part * (dm // 2), LN), dm // 2),
        )

    def from_columns(ref, base, w):
        return lambda part, r0, n: wide(
            nt, ref, pl.ds(pl.multiple_of(r0, 16), n),
            pl.ds(pl.multiple_of(base + part * w, LN), w),
        )

    def group_steps(g, produce, out_ref, row0, col0, part_cols):
        sb, rb, rr, acc, rx = bufs[5 * g : 5 * g + 5]
        total, w = sb.shape
        kind = sb.dtype
        tile = min(384, total // 2)

        def place(part):
            if part_cols:
                return out_ref.at[
                    pl.ds(row0, total), pl.ds(pl.multiple_of(col0 + part * w, LN), w)
                ]
            return out_ref.at[pl.ds(pl.multiple_of(part * total, 8), total), :]

        def copy_of(i, src, dst, peer):
            copy = pltpu.make_async_remote_copy(
                src_ref=src, dst_ref=dst, send_sem=ar_s.at[g, i], recv_sem=ar_r.at[g, i],
                device_id=peer, device_id_type=MESH,
            )
            copy.start()
            sent.append(copy)
            return copy

        def rows_at(start, n):
            return pl.ds(pl.multiple_of(start, 8), n)

        def tiles(count, body):
            if count == 1:
                body(0)
            else:
                lax.fori_loop(0, count, lambda i, _: (body(i), 0)[1], 0)

        def give(i):
            sb[rows_at(i * tile, tile), :] = produce(1 - core, i * tile, tile).astype(kind)

        tiles(total // tile, give)
        copy = copy_of(0, sb, rb, core_peer)
        sent.pop()
        yield
        copy.wait()
        bit, peer = stages[0]
        n = total // 2

        def own(i, start):
            r0 = start + i * tile
            return produce(core, r0, tile) + rb[rows_at(r0, tile), :].astype(F32)

        def give_half(i):
            sb[rows_at(i * tile, tile), :] = own(i, (1 - bit) * n).astype(kind)

        def keep_half(i):
            acc[rows_at(i * tile, tile), :] = own(i, bit * n)

        tiles(n // tile, give_half)
        copy = copy_of(1, sb.at[pl.ds(0, n)], rr.at[pl.ds(0, n)], peer)
        tiles(n // tile, keep_half)
        first_copy = copy
        if extras:
            sent.pop()
        yield
        copy.wait_recv()
        off1 = bit * n
        bit, peer = stages[1]
        base, n = n, n // 2
        gone, kept = (1 - bit) * n, bit * n
        sb[base : base + n, :] = (
            acc[rows_at(gone, n), :] + rr[rows_at(gone, n), :].astype(F32)
        ).astype(kind)
        copy = copy_of(2, sb.at[pl.ds(base, n)], rr.at[pl.ds(base, n)], peer)
        acc[rows_at(kept, n), :] += rr[rows_at(kept, n), :].astype(F32)
        yield
        copy.wait_recv()
        off2 = off1 + kept
        first, base, n = base, base + n, n // 4
        copies = []
        for d in (2, 1, 3):
            at = lax.rem(in_row + d, 4) * n
            here = base + (d - 1) * n
            sb[here : here + n, :] = (
                acc[rows_at(kept + at, n), :] + rr[rows_at(first + at, n), :].astype(F32)
            ).astype(kind)
            copies.append(
                copy_of(
                    2 + d, sb.at[pl.ds(here, n)], rr.at[pl.ds(here, n)], row_peers[d - 1]
                )
            )
        yield
        at = in_row * n
        value = acc[rows_at(kept + at, n), :] + rr[rows_at(first + at, n), :].astype(F32)
        for copy in copies:
            copy.wait_recv()
        for d in range(3):
            value = value + rr[base + d * n : base + (d + 1) * n, :].astype(F32)
        if extras:
            first_copy.wait_send()
        for e, peer in enumerate(extras):
            mine = value.astype(kind)
            sb[e * n : (e + 1) * n, :] = mine
            copy = pltpu.make_async_remote_copy(
                src_ref=sb.at[pl.ds(e * n, n)], dst_ref=rx.at[e], send_sem=ex_s.at[g, e],
                recv_sem=ex_r.at[g, e], device_id=peer, device_id_type=MESH,
            )
            copy.start()
            copy.wait()
            value = mine.astype(F32) + rx[e].astype(F32)
        mine = rows_at(off2 + at, n)
        rb[mine, :] = value.astype(kind)
        copies = [
            copy_of(5 + d, rb.at[mine], rb.at[mine], row_peers[d - 1]) for d in (2, 1, 3)
        ]
        yield
        for copy in copies:
            copy.wait_recv()
        for i, off, n, peer in (
            (9, off2, total // 4, stages[1][1]),
            (10, off1, total // 2, stages[0][1]),
        ):
            here = rb.at[rows_at(off, n)]
            copy = copy_of(i, here, here, peer)
            yield
            copy.wait_recv()
        here = place(core)
        copy = copy_of(11, rb, here, core_peer)
        local = pltpu.make_async_copy(rb, here, loc_sem.at[g])
        local.start()
        yield
        copy.wait_recv()
        local.wait()

    wide_w = dm // 2
    groups = [
        (0, from_out(0), go_h, 0, 0, True),
        (1, from_out(1), go_h, dm, 0, True),
        (2, from_columns(ggz, 0, wide_w), gw_h, 0, 0, True),
        (3, from_columns(ggz, dm, wide_w), gw_h, 0, dm, True),
        (4, from_columns(gy, 0, wide_w), gm_h, 0, 0, True),
        (5, from_columns(gy, dm, wide_w), gm_h, 0, dm, True),
        (6, from_columns(drv, 0, LN), gm_h, 0, di, True),
        (7, lambda part, r0, n: sm[part, pl.ds(pl.multiple_of(r0, 8), n), :], sm_h, 0, 0, False),
    ]

    plan = list(PLAN)
    live = {}
    slot_now = [seqs * nblk]

    def service(last=False):
        todo = [g for part in plan for g in part] if last else plan.pop(0)
        for g in todo:
            if g not in live:
                live[g] = group_steps(*groups[g])
            next(live[g], None)
            if slot_now[0] < b_slots:
                backward_slot(slot_now[0])
                slot_now[0] += 1

    for i in range(seqs * nblk // 2):
        s, i0 = (2 * i) // nblk, (2 * i) % nblk

        service()
        slot0 = slot_now[0] - i0

        def backward_body(b, _, s=s, slot0=slot0):
            made = [pair_backward(2 * b + h, s) for h in range(2)]
            t1, t2, t3 = (p + q for p, q in zip(made[0][1], made[1][1]))
            gsc[s, :half, :half] += t1
            gsc[s, :half, half:] += t2
            gsc[s, half:, half:] += t3
            for cols, _, lo, hi in made:
                z[s, :half, cols] = lo
                z[s, half:, cols] = hi
            backward_slot(slot0 + b)
            return 0

        lax.fori_loop(i0, i0 + 2, backward_body, 0)
        slot_now[0] += 2
    slots_alone(backward_slot, slot_now[0], b_slots)
    slot_now[0] = b_slots
    service()

    ginf[...] = jnp.zeros_like(ginf)
    hs_d[...] = jnp.zeros_like(hs_d)
    hs_g[...] = jnp.zeros_like(hs_g)
    bdh[...] = jnp.zeros_like(bdh)

    def head_sum(v, x):
        hi, lo = split2(v)
        return dot_nt(hi, x) + dot_nt(lo, x)

    def head_sum3(v, x):
        hi, mid, lo = split3(v)
        return dot_nt(hi, x) + dot_nt(mid, x) + dot_nt(lo, x)

    def gh_copy(b):
        cols = ds(b * BW, BW)
        return pltpu.make_async_remote_copy(
            src_ref=big.at[:, pl.ds(0, 8), cols], dst_ref=big.at[:, pl.ds(length, 8), cols],
            send_sem=gh_s.at[b], recv_sem=gh_r.at[b], device_id=prv, device_id_type=MESH,
        )

    @pl.when(jnp.logical_not(has_next))
    def _():
        big[:, length : length + 8, :] = jnp.zeros((seqs, 8, xbc), F32)

    def finish_block(b, s, ga):
        cols = ds(b * BW, BW)
        f = fil[s, :, cols]
        sg = sigmoid(f)
        gf = ga * (sg * (1.0 + f * (1.0 - sg)))
        big[s, 0:length, cols] = gf
        return jnp.sum(gf, axis=0, keepdims=True)

    def last_body(b, _):
        cols = ds(b * BW, BW)
        cb_sum = jnp.zeros((1, BW), F32)
        sk_sum = jnp.zeros((1, BW), F32)
        x = xx[:, cols]
        for s in range(seqs):
            lt = in_b[s * nblk + b]
            pr = prior_of(s, b)
            f = fil[s, :, cols]
            sg = sigmoid(f)
            sig = f * sg
            stw = dot(pst[s], x)
            gst = dot(infl[s], lt) * dot(ptl[s], x)
            gd = z[s, :, cols]
            gyf = gy[s, :, cols].astype(F32)
            sk_row = sk_row_r[7:8, cols]
            gg = gst + gd
            ga = sk_row * gyf + stw * gg
            t1 = stw * sig * gst
            dd = gyf * (y[s, :, cols] - sk_row * sig) - drv[s, :, cols].astype(F32) * gd - t1
            hs_d[s] += head_sum(dd, x)
            hs_g[s] += head_sum(sig * gg, x)
            bd = jnp.sum(t1, axis=0, keepdims=True) + dlast[s, 7:8, cols] * jnp.sum(
                lt.astype(F32) * pr, axis=0, keepdims=True
            )
            bdh[s] += head_sum3(jnp.broadcast_to(bd, (8, BW)), x)
            sk_sum = sk_sum + jnp.sum(gyf * sig, axis=0, keepdims=True)
            ginf[s] += dot_nt(scl[s, :, cols], lt)
            gf = ga * (sg * (1.0 + f * (1.0 - sg)))
            big[s, 0:length, cols] = gf
            cb_sum = cb_sum + jnp.sum(gf, axis=0, keepdims=True)
        small_put(SM_CONVB, b, cb_sum)
        sk_row_r[0:1, cols] = sk_sum

        @pl.when(has_prev)
        def _():
            gh_copy(b).start()

        return 0

    def mixed_body(b):
        cols = ds(b * BW, BW)

        @pl.when(has_next)
        def _():
            gh_copy(b).wait_recv()

        parts = []
        sums = [jnp.zeros((1, BW), F32) for _ in range(window + 1)]
        for s in range(seqs):
            gf = big[s, :, cols]
            rows = gf.shape[0]
            m = ext[s, :, cols].astype(F32)
            gm = jnp.zeros((length, BW), F32)
            for k in range(window + 1):
                shift = window - k
                moved = pltpu.roll(gf, rows - shift, 0) if shift else gf
                gm = gm + cw_r[k : k + 1, cols] * moved[:length]
                em = pltpu.roll(m, shift, 0) if shift else m
                sums[k] = sums[k] + jnp.sum(gf[:length] * em[hw:], axis=0, keepdims=True)
            parts.append(gm.astype(BF))
        for k in range(window + 1):
            small_put(SM_CONVW + k * (xbc // LN), b, sums[k])
        return parts

    def mixed_loop(b, _):
        cols = ds(b * BW, BW)
        for s, part in enumerate(mixed_body(b)):
            gy[s, :, cols] = part
        return 0

    third = nblk // 2
    lax.fori_loop(0, third, last_body, 0)
    service()
    lax.fori_loop(0, third, mixed_loop, 0)
    service()
    lax.fori_loop(third, nblk, last_body, 0)
    service()

    cb_sum = jnp.zeros((1, BW), F32)
    for s in range(seqs):
        gst_bf = gsc[s].astype(BF)
        gi = ginf[s] + dot(gst_bf, outf[s])
        go = gout[s] + dot(gst_bf.T, infl[s])
        cb_sum = cb_sum + finish_block(nblk, s, jnp.concatenate([gi, go], axis=1))
    small_put(SM_CONVB, nblk, cb_sum)

    @pl.when(has_prev)
    def _():
        gh_copy(nblk).start()

    lax.fori_loop(third, nblk, mixed_loop, 0)
    service()
    for s, part in enumerate(mixed_body(nblk)):
        drv[s, :, 0:BW] = part
    service()

    row_i = lax.broadcasted_iota(jnp.int32, (length, LN), 0)
    glr = jnp.zeros((1, LN), F32)
    gsb = jnp.zeros((1, LN), F32)
    grl = []
    for s in range(seqs):
        gc = hs_d[s] + jnp.where(row_i == length - 1, bdh[s, 0:1], 0.0)
        terms = dot3(jnp.where(t_r <= t_c, 1.0, 0.0).astype(BF), gc)
        gst = hs_g[s] + terms * rates3
        glr = glr + jnp.sum(terms * st[s], axis=0, keepdims=True)
        graw = gst * sigmoid(sraw[s] + bias3)
        gsb = gsb + jnp.sum(graw, axis=0, keepdims=True)
        grl.append(jnp.where(lane128 < heads, graw, 0.0).astype(BF))
    sk_h = head_sum3(jnp.broadcast_to(sk_row_r[0:1, :], (8, di)), xx[...])
    small_one(SM_HEADS, gsb)
    small_one(SM_HEADS + 1, rates3 * glr)
    small_one(SM_HEADS + 2, sk_h[0:1])
    stepg = dot(grl[0].T, ne[0, hw:, :])
    for s in range(1, seqs):
        stepg = stepg + dot(grl[s].T, ne[s, hw:, :])
    for i in range(dm // LN):
        row = SM_STEP + 24 * i
        for lo, hi in ((row, min(row + 24, 128)), (max(row, 128), row + 24)):
            if lo < hi:
                sm[lo // 128, lo % 128 : lo % 128 + hi - lo, :] = stepg[
                    lo - row : hi - row, i * LN : (i + 1) * LN
                ]

    service()
    for s in range(seqs):
        for i in range(dm // BW):
            cols = slice(i * BW, (i + 1) * BW)
            pj = dot(nrm[s], wo[:, cols])
            res_r[s, :, cols] = (tok[s, :, cols].astype(F32) + pj).astype(BF)
        service()
    res_copy = pltpu.make_async_copy(res_r, res_h, tok_sem.at[0])
    res_copy.start()
    for s in range(seqs):
        for i in range(dm // BW):
            cols = slice(i * BW, (i + 1) * BW)
            gn[s, :, cols] = (
                dot_nt(gy[s], wm[cols, :di])
                + dot_nt(drv[s, :, 0:BW], wm[cols, di:])
                + dot_nt(ggz[s], wg[cols, :])
                + dot_nt(grl[s], ws3[cols])
            )
        service()

    @pl.when(has_next)
    def _():
        halo_copy.wait_send()

    def token_body(i, sums):
        for s in range(seqs):
            rows = ds(i * 16, 16)
            v = tok[s, rows, :].astype(F32)
            inv = lax.rsqrt(jnp.mean(v * v, axis=-1, keepdims=True) + EPSILON)
            unit = v * inv
            gr = gn[s, rows, :]
            sums = sums + jnp.sum(gr * unit, axis=0, keepdims=True)
            q = gr * gain
            back = inv * (q - unit * jnp.mean(q * unit, axis=-1, keepdims=True))
            tok[s, rows, :] = (cot[s, rows, :].astype(F32) + back).astype(BF)
        return sums

    n_sum = jnp.zeros((1, dm), F32)
    for i in range(4):
        n_sum = lax.fori_loop(
            i * (length // 64), (i + 1) * (length // 64), token_body, n_sum, unroll=2
        )
        service()
    for i in range(dm // LN):
        small_one(SM_NORM + i, n_sum[:, i * LN : (i + 1) * LN])
    tg_copy = pltpu.make_async_copy(tok, tg_h, tok_sem.at[1])
    tg_copy.start()
    service(last=True)
    res_copy.wait()
    tg_copy.wait()
    for copy in sent:
        copy.wait_send()

    def drain(q, _):
        @pl.when(has_prev)
        def _():
            backward_copy(q).wait_send()

        return 0

    lax.fori_loop(0, seqs * nblk, drain, 0)

    def drain_halo(b, _):
        @pl.when(has_prev)
        def _():
            gh_copy(b).wait_send()

        return 0

    lax.fori_loop(0, xbc // BW, drain_halo, 0)


def on_device(nctx, *args):
    tokens, norm_gain, wg, wm, ws, conv_w, conv_b, sb, lr, sk, gg, wo, cot = args
    seqs, length, dm = tokens.shape
    di = wg.shape[1]
    xbc = wm.shape[1]
    heads = ws.shape[1]
    nst = (xbc - di) // 2
    nchunk = di // LN
    nblk = di // BW
    hw = 16
    vm = pltpu.VMEM
    any_spec = pl.BlockSpec(memory_space=pl.ANY)
    vm_spec = pl.BlockSpec(memory_space=vm)
    dma = pltpu.SemaphoreType.DMA
    extras = max(1, (nctx // 16).bit_length())
    bufs = []
    for rows, w, kind in [(dm, dm // 2, BF)] * 6 + [(dm, LN, BF), (128, LN, F32)]:
        bufs += [vm((rows, w), kind)] * 3 + [vm((rows // 2, w), F32)]
        bufs += [vm((extras, rows // 16, w), kind) if nctx > 8 else vm((1, 16, LN), kind)]
    out = pl.pallas_call(
        functools.partial(layer_kernel, nctx),
        out_shape=(
            jax.ShapeDtypeStruct(tokens.shape, BF),
            jax.ShapeDtypeStruct(tokens.shape, BF),
            jax.ShapeDtypeStruct((di, dm), BF),
            jax.ShapeDtypeStruct((dm, di), BF),
            jax.ShapeDtypeStruct((dm, xbc), BF),
            jax.ShapeDtypeStruct((256, LN), F32),
        ),
        in_specs=[any_spec, vm_spec, any_spec, any_spec] + [vm_spec] * 7 + [any_spec] * 2,
        out_specs=(any_spec,) * 6,
        scratch_shapes=[
            vm((seqs, length, dm), BF),
            vm((seqs, length, dm), BF),
            vm((dm, di), BF),
            vm((dm, xbc), BF),
            vm((di, dm), BF),
            vm((seqs, hw, dm), BF),
            vm((seqs, hw + length, dm), BF),
            vm((dm, seqs * length), BF),
            vm((seqs, hw + length, xbc), BF),
            vm((seqs, length, xbc), F32),
            vm((seqs, length, di), BF),
            vm((seqs, length, di), BF),
            vm((seqs, length, di), F32),
            vm((seqs, length, di), F32),
            vm((seqs, length + 8, xbc), F32),
            vm((seqs, length, di), BF),
            vm((seqs, length, di), BF),
            vm((seqs, length, di), BF),
            vm((di, seqs * length), BF),
            vm((seqs, length, LN), F32),
            vm((seqs, length, LN), F32),
            vm((seqs, length, dm), F32),
            vm((seqs * nchunk, nst, LN), F32),
            vm((seqs * nchunk, nst, LN), F32),
            vm((seqs * nblk, nst, BW), BF),
            vm((seqs * nblk, nst, BW), BF),
            vm((seqs, length, LN), F32),
            vm((seqs, length, LN), F32),
            vm((seqs, length, LN), F32),
            vm((seqs, LN, length), F32),
            vm((seqs, length, LN), BF),
            vm((seqs, length, LN), BF),
            vm((seqs, length, LN), BF),
            vm((seqs, 8, di), F32),
            vm((seqs, length, nst), BF),
            vm((seqs, length, nst), BF),
            vm((seqs, nst, length), BF),
            vm((seqs, nst, length), BF),
            vm((seqs, length, length), F32),
            vm((seqs, length, length), F32),
            vm((LN, di), BF),
            vm((length, length), BF),
            vm((seqs, length, LN), F32),
            vm((seqs, length, LN), F32),
            vm((seqs, 8, LN), F32),
            vm((seqs, length, dm), BF),
            dma((2,)),
            vm((2, 128, LN), F32),
            vm((8, di), F32),
            bufs,
            dma((8, 12)), dma((8, 12)), dma((8,)), dma((8, extras)), dma((8, extras)),
            dma((5,)), dma, dma,
            dma((seqs * nchunk,)), dma((seqs * nchunk,)), dma((seqs * nblk,)), dma((seqs * nblk,)),
            dma((xbc // BW,)), dma((xbc // BW,)),
        ],
        compiler_params=pltpu.CompilerParams(
            collective_id=0, has_side_effects=True, vmem_limit_bytes=65400 * 1024
        ),
    )(*args[:4], ws.T, *args[5:])
    res, tg, g_out, g_gate, g_mixer, small = out
    gate0 = xbc // LN
    norm0 = gate0 + di // LN
    convw0 = norm0 + dm // LN
    taps = conv_w.shape[0]
    heads0 = convw0 + taps * (xbc // LN)
    step0 = -(-(heads0 + 3) // 8) * 8

    def finish(res_i, tg_i, go_i, gw_i, gm_i, sm_i, *outs):
        res_o, tg_o, ng_o, gw_o, gm_o, st_o, cw_o, cb_o, sb_o, lr_o, sk_o, gg_o, go_o = outs
        res_o[...] = res_i[...]
        tg_o[...] = tg_i[...]
        go_o[...] = go_i[...].astype(F32)
        gw_o[...] = gw_i[...].astype(F32)
        gm_o[...] = gm_i[...].astype(F32)

        @pl.when(pl.program_id(0) == 0)
        def _():
            for ref, first, count in (
                (cb_o, 0, xbc // LN), (gg_o, gate0, di // LN), (ng_o, norm0, dm // LN),
            ):
                for i in range(count):
                    ref[pl.ds(i * LN, LN)] = sm_i[first + i, :]
            for k in range(taps):
                for i in range(xbc // LN):
                    r = convw0 + k * (xbc // LN) + i
                    cw_o[k : k + 1, i * LN : (i + 1) * LN] = sm_i[r : r + 1, :]
            for i, ref in enumerate((sb_o, lr_o, sk_o)):
                ref[...] = sm_i[heads0 + i, 0:heads]
            for i in range(dm // LN):
                r = step0 + heads * i
                st_o[:, i * LN : (i + 1) * LN] = sm_i[r : r + heads, :]

    steps = 4

    def rows_of(a, dim=0):
        block = tuple(n // steps if i == dim else n for i, n in enumerate(a.shape))
        return pl.BlockSpec(block, lambda t: tuple(t if i == dim else 0 for i in range(a.ndim)))

    def whole(*shape):
        return pl.BlockSpec(shape, lambda t: (0,) * len(shape))

    def shape(*dims):
        return jax.ShapeDtypeStruct(dims, F32)

    small_shapes = {
        2: (dm,), 5: (heads, dm), 6: (taps, xbc), 7: (xbc,), 8: (heads,), 9: (heads,),
        10: (heads,), 11: (di,),
    }
    big_outs = {0: res, 1: tg, 3: g_gate, 4: g_mixer, 12: g_out}
    final = pl.pallas_call(
        finish,
        grid=(steps,),
        in_specs=[
            rows_of(res, 1), rows_of(tg, 1), rows_of(g_out), rows_of(g_gate), rows_of(g_mixer),
            whole(*small.shape),
        ],
        out_specs=[
            rows_of(big_outs[i], 1 if i < 2 else 0) if i in big_outs else whole(*small_shapes[i])
            for i in range(13)
        ],
        out_shape=[
            jax.ShapeDtypeStruct(big_outs[i].shape, BF if i < 2 else F32)
            if i in big_outs else shape(*small_shapes[i])
            for i in range(13)
        ],
        compiler_params=pltpu.CompilerParams(vmem_limit_bytes=62 * 1024 * 1024),
    )(res, tg, g_out, g_gate, g_mixer, small)
    final = list(final)
    final[5] = final[5].T
    return tuple(final)


def solution(mesh):
    tok = P("seq", "ctx", None)
    return jax.shard_map(
        functools.partial(on_device, mesh.shape["ctx"]),
        mesh=mesh,
        in_specs=(tok,) + (P(),) * 11 + (tok,),
        out_specs=(tok, tok) + (P(),) * 11,
        check_vma=False,
    )
```
